256 devices in a mesh: leaf: 128 (over z, y, x), sub: 2 (over core).
Axes of the slice: x: 4, y: 4, z: 8, core: 2. Of those that a mesh axis runs over, the one named last changes fastest.
Arguments:
- points: bfloat16 [8, 65536], P(None, ('leaf', 'sub')), may hold values from 0 to 1
- omega: bfloat16 [128, 65536], P(None, ('leaf', 'sub')), may hold values from -6 to 6
- tree_order: int32 [65536], P(('leaf', 'sub')), may hold values from 0 to 65535, as said below
- sibling_blocks: int32 [128, 16], P('leaf'), may hold values from 0 to 127, as said below
- cousin_blocks: int32 [128, 32], P('leaf'), may hold values from 0 to 127, as said below
- skeleton: int32 [4, 256], replicated, may hold values from 0 to 65535, as said below
Outputs:
- node_basis: float32 [65536, 256], P(('leaf', 'sub'))
- coupling: float32 [2, 256, 256], replicated
The draws below stay inside these ranges and needn't reach their ends.
Inputs may be any that keep to these rules, and one draw needn't show every extreme that they name: tree_order maps each aligned group of 256 rows onto itself, a permutation inside each group. `sibling_blocks`: row b holds 16 different blocks of the sibling of b's node of 32 blocks, whose index is (b // 32) xor 1. `cousin_blocks`: row b holds 32 different blocks of the half of the blocks that does not hold b. `skeleton`: row c holds 256 different tree rows of node c.
All inputs are finite; a program needn't handle non-finite values.
Results may differ from the reference program's by a relative error of at most 0.0043.
Values may be sent and summed in bfloat16 or wider, within the bound.
A program may use at most 128 MiB of HBM per device.

```python
import math
import jax
import jax.numpy as jnp
from jax import lax

FEATS = 8
SAMPLES = 128
RANK = 256
LEAF = 512
ROWS = 256
BLOCKS = 128
N = 65536
NODE = 16384
SIBS = 16
COUSINS = 32


def pick_blocks(key, group_size, picked):
    keys = jax.random.split(key, BLOCKS)
    offsets = jax.vmap(lambda one_key: jax.random.permutation(one_key, group_size)[:picked])(keys).astype(jnp.int32)
    owners = jnp.arange(BLOCKS, dtype=jnp.int32)
    base_block = jnp.bitwise_xor(owners // group_size, 1) * group_size
    return base_block[:, None] + offsets


def draw_tree_order(key, part):
    key = jax.random.fold_in(key, 11)
    keys = jax.random.split(key, N // ROWS)
    inside = jax.vmap(lambda one_key: jax.random.permutation(one_key, ROWS))(keys).astype(jnp.int32)
    base_row = jnp.arange(N // ROWS, dtype=jnp.int32)[:, None] * ROWS
    return (inside + base_row).reshape(N)


def draw_sibling_blocks(key, part):
    key = jax.random.fold_in(key, 12)
    return pick_blocks(key, BLOCKS // 4, SIBS)


def draw_cousin_blocks(key, part):
    key = jax.random.fold_in(key, 13)
    return pick_blocks(key, BLOCKS // 2, COUSINS)


def draw_skeleton(key, part):
    key = jax.random.fold_in(key, 14)
    pick_key, target_key = jax.random.split(key)
    keys = jax.random.split(pick_key, 4)
    chosen = jax.vmap(lambda one_key: jax.random.permutation(one_key, NODE)[:RANK])(keys).astype(jnp.int32)
    middle_targets = jax.random.randint(target_key, (2,), 0, NODE).astype(jnp.int32)
    targets = jnp.concatenate([jnp.zeros((1,), jnp.int32), middle_targets, jnp.full((1,), NODE - 1, jnp.int32)])
    turned = (chosen - chosen[:, :1] + targets[:, None]) % NODE
    return turned + jnp.arange(4, dtype=jnp.int32)[:, None] * NODE


def levels(key, dims, cuts, smallest, high):
    level = 1.0
    for position, parts in cuts:
        heights = jax.random.uniform(jax.random.fold_in(jax.random.fold_in(key, 6), position), (parts,), jnp.float32, smallest / len(cuts), high / len(cuts))
        level = level * jnp.repeat(jnp.exp(heights), dims[position] // parts).reshape((-1,) + (1,) * (len(dims) - 1 - position))
    return level


def gaussian(own_key, dims, spread, limit, cuts=(), kind=jnp.bfloat16):
    drawn = spread * jax.random.normal(own_key, dims, jnp.float32)
    if cuts:
        drawn = drawn * levels(own_key, dims, cuts, -0.22, 0.18)
    return jnp.clip(drawn, -limit, limit).astype(kind)


def setup_inputs(seed: int = 0) -> dict:
    splits = jax.random.split(jax.random.key(seed), 7)
    return {
        "points": jnp.clip(1.0 * jax.random.uniform(splits[0], (FEATS, N), jnp.float32) ** levels(splits[0], (FEATS, N), ((1, 256),), -0.2, 0.2), 0.0, 1.0).astype(jnp.bfloat16),
        "omega": gaussian(splits[1], (SAMPLES, N), 1.0, 6.0, ((1, 256),)),
        "tree_order": draw_tree_order(jax.random.fold_in(splits[6], 71), 0),
        "sibling_blocks": draw_sibling_blocks(jax.random.fold_in(splits[6], 71), 0),
        "cousin_blocks": draw_cousin_blocks(jax.random.fold_in(splits[6], 71), 0),
        "skeleton": draw_skeleton(jax.random.fold_in(splits[6], 71), 0),
    }


SPREAD = 2.0
SHIFT = 0.01
HIGHEST = lax.Precision.HIGHEST

def kernel_values(row_points, col_points):
    inner_products = lax.dot_general(row_points, col_points, (((0,), (0,)), ((), ())), precision=HIGHEST)
    distance = lax.optimization_barrier(jnp.sum(row_points * row_points, axis=0))[:, None] + lax.optimization_barrier(jnp.sum(col_points * col_points, axis=0))[None, :] - 2.0 * inner_products
    return jnp.exp(-SPREAD * distance)

def cholesky_factor(gram_matrix):
    shifted = gram_matrix + SHIFT * jnp.trace(gram_matrix) * jnp.eye(gram_matrix.shape[0], dtype=jnp.float32)
    return jnp.linalg.cholesky(shifted)

def right_solve(lower_part, values, factor):
    return factor * jax.scipy.linalg.solve_triangular(lower_part, values.T, lower=True).T

def reference(points, omega, tree_order, sibling_blocks, cousin_blocks, skeleton):
    tree_points = points[:, tree_order].astype(jnp.float32)
    tree_omega = omega[:, tree_order]
    blocked_points = tree_points.reshape(FEATS, BLOCKS, LEAF).transpose(1, 0, 2)
    blocked_omega = tree_omega.reshape(SAMPLES, BLOCKS, LEAF).transpose(1, 0, 2)

    def block_samples(block):
        row_points = blocked_points[block]
        pieces = []
        for partners in (sibling_blocks[block], cousin_blocks[block]):
            col_points = blocked_points[partners].transpose(1, 0, 2).reshape(FEATS, -1)
            col_weights = blocked_omega[partners].transpose(1, 0, 2).reshape(SAMPLES, -1).astype(jnp.float32)
            kernel_block = lax.optimization_barrier(kernel_values(row_points, col_points).astype(jnp.bfloat16))
            kernel_block = kernel_block.astype(jnp.float32)
            pieces.append(lax.dot_general(kernel_block, col_weights, (((1,), (1,)), ((), ())), precision=HIGHEST))
        return jnp.concatenate(pieces, axis=1)
    samples = lax.map(block_samples, jnp.arange(BLOCKS, dtype=jnp.int32)).reshape(N, RANK)
    node_rows = samples.reshape(4, NODE, RANK)
    factor = math.sqrt(NODE)
    lowers = [cholesky_factor(jnp.dot(node_rows[member].T, node_rows[member], precision=HIGHEST)) for member in range(4)]
    node_basis = jnp.concatenate([right_solve(lowers[member], node_rows[member], factor) for member in range(4)], axis=0)
    flat_skeleton = skeleton.reshape(-1)
    skel_samples = samples[flat_skeleton].reshape(4, RANK, RANK)
    skel_points = tree_points[:, flat_skeleton].reshape(FEATS, 4, RANK)
    reduced = [right_solve(lowers[member], skel_samples[member], factor) for member in range(4)]
    couplings = []
    for couple in range(2):
        kernel_skel = kernel_values(skel_points[:, 2 * couple], skel_points[:, 2 * couple + 1])
        middle = jnp.dot(kernel_skel, reduced[2 * couple + 1], precision=HIGHEST)
        couplings.append(jnp.dot(reduced[2 * couple].T, middle, precision=HIGHEST) / math.sqrt(RANK))
    return (node_basis, jnp.stack(couplings))
```

```python
import functools
import math

import jax
import jax.numpy as jnp
from jax import lax
from jax.experimental import pallas as pl
from jax.experimental.pallas import tpu as pltpu
from jax.sharding import PartitionSpec as P

MESH = pl.DeviceIdType.MESH
HIGH = lax.Precision.HIGH
HIGHEST = lax.Precision.HIGHEST
F32 = jnp.float32
BF16 = jnp.bfloat16
VMEM = pl.BlockSpec(memory_space=pltpu.VMEM)
SMEM = pl.BlockSpec(memory_space=pltpu.SMEM)

ROWS = 256
FEATS = 8
SAMPLES = 128
RANK = 256
SPAN = 288
LINK = F32


def place():
    leaf = lax.axis_index("leaf")
    core = lax.axis_index("sub")
    return leaf % 4, (leaf // 4) % 4, leaf // 16, core


def device(x, y, z, core):
    return (z * 16 + y * 4 + x, core)


def greet(partners):
    barrier = pltpu.get_barrier_semaphore()
    for partner in partners:
        pl.semaphore_signal(barrier, inc=1, device_id=partner, device_id_type=MESH)
    pl.semaphore_wait(barrier, len(partners))


def send(src, dst, send_sem, recv_sem, target):
    copy = pltpu.make_async_remote_copy(
        src_ref=src,
        dst_ref=dst,
        send_sem=send_sem,
        recv_sem=recv_sem,
        device_id=target,
        device_id_type=MESH,
    )
    copy.start()
    return copy


def features(coordinates, scale, ones_first):
    norm = -2.0 * jnp.sum(coordinates * coordinates, axis=0, keepdims=True)
    first = norm.astype(BF16).astype(F32)
    second = (norm - first).astype(BF16).astype(F32)
    third = norm - first - second
    row = lax.broadcasted_iota(jnp.int32, coordinates.shape, 0)
    start = 3 if ones_first else 0
    other = 0 if ones_first else 3
    tail = jnp.where((row >= other) & (row < other + 3), 1.0, 0.0)
    tail = jnp.where(row == start, first, tail)
    tail = jnp.where(row == start + 1, second, tail)
    tail = jnp.where(row == start + 2, third, tail)
    return jnp.concatenate([scale * coordinates, tail], axis=0)


def gather_kernel(
    points, omega, order, siblings, cousins,
    blocks, row_points, lists, tree_points,
    own, own_rows, own_lists,
    z_send, z_recv, up_send, up_recv, down_send, down_recv, far_send, far_recv,
    rows_send, rows_recv, list_send, list_recv,
):
    x, y, z, core = place()
    mate = 7 - 6 * (z % 2)
    offsets = [mate, 2, 6, 3, 5, 4]
    z_partners = [device(x, y, (z + offset) % 8, core) for offset in offsets]
    up = device(x, (y + 1) % 4, z, core)
    down = device(x, (y + 3) % 4, z, core)
    near = [
        (dx, dc, device((x + dx) % 4, y, z, (core + dc) % 2))
        for dx in range(4)
        for dc in range(2)
        if dx or dc
    ]
    greet(z_partners + [up, down] + [who for _, _, who in near])

    own[0:ROWS, :] = omega[...].astype(F32).T.astype(BF16)
    columns = features(points[...].astype(F32), 1.0, False).astype(BF16)
    own[256:272, :] = columns[:, :128]
    own[272:288, :] = columns[:, 128:]
    pending = []
    z_copies = []
    for k, offset in enumerate(offsets):
        back = (8 - offset) % 8
        z_copies.append(
            send(own, blocks.at[back], z_send.at[k], z_recv.at[back], z_partners[k])
        )

    local = order[...] % ROWS
    lane = lax.broadcasted_iota(jnp.int32, (ROWS, ROWS), 0)
    pick = jnp.where(lane == local, 1.0, 0.0).astype(BF16)
    mine = jnp.dot(points[...], pick, preferred_element_type=F32)
    tree_points[...] = mine
    own_rows[...] = features(mine, 4.0, True).astype(BF16)
    own_lists[...] = jnp.zeros_like(own_lists)
    own_lists[0:1, 0:16] = siblings[...]
    own_lists[1:2, 0:32] = cousins[...]
    row_points[x * 2 + core] = own_rows[...]
    lists[x] = own_lists[...]
    small = []
    for k, (dx, dc, who) in enumerate(near):
        small.append(
            send(own_rows, row_points.at[x * 2 + core], rows_send.at[k], rows_recv.at[k], who)
        )
        if not dc:
            small.append(
                send(own_lists, lists.at[x], list_send.at[dx], list_recv.at[dx], who)
            )

    far = []

    def relay(k):
        offset = offsets[k]
        if k % 2:
            down_copies[k].wait_recv()
            far.append(
                send(blocks.at[24 + offset], blocks.at[16 + offset], far_send.at[k], far_recv.at[k], up)
            )
        else:
            up_copies[k].wait_recv()
            far.append(
                send(blocks.at[8 + offset], blocks.at[16 + offset], far_send.at[k], far_recv.at[k], down)
            )

    up_copies, down_copies = [], []
    for k, offset in enumerate(offsets):
        pltpu.make_async_remote_copy(
            src_ref=own, dst_ref=blocks.at[offset], send_sem=z_send.at[k],
            recv_sem=z_recv.at[offset], device_id=up, device_id_type=MESH,
        ).wait_recv()
        down_copies.append(
            send(blocks.at[offset], blocks.at[24 + offset], up_send.at[k], down_recv.at[k], up)
        )
        up_copies.append(
            send(blocks.at[offset], blocks.at[8 + offset], down_send.at[k], up_recv.at[k], down)
        )
        if k:
            relay(k - 1)
    relay(5)
    for k in range(6):
        if k % 2:
            up_copies[k].wait_recv()
        else:
            down_copies[k].wait_recv()
    for copy in far:
        copy.wait()
    for copy in small:
        copy.wait()
    for copy in z_copies + up_copies + down_copies:
        copy.wait_send()


def gather(points, omega, order, siblings, cousins):
    dma = pltpu.SemaphoreType.DMA
    return pl.pallas_call(
        gather_kernel,
        out_shape=(
            jax.ShapeDtypeStruct((32, SPAN, 128), BF16),
            jax.ShapeDtypeStruct((8, 16, ROWS), BF16),
            jax.ShapeDtypeStruct((4, 8, 128), jnp.int32),
            jax.ShapeDtypeStruct((FEATS, ROWS), F32),
        ),
        in_specs=[VMEM] * 5,
        out_specs=(VMEM,) * 4,
        scratch_shapes=[
            pltpu.VMEM((SPAN, 128), BF16),
            pltpu.VMEM((16, ROWS), BF16),
            pltpu.VMEM((8, 128), jnp.int32),
            dma((6,)), dma((8,)), dma((6,)), dma((6,)), dma((6,)), dma((6,)), dma((6,)), dma((6,)),
            dma((7,)), dma((7,)), dma((4,)), dma((4,)),
        ],
        compiler_params=pltpu.CompilerParams(
            collective_id=0, has_side_effects=True, vmem_limit_bytes=32 << 20
        ),
        name="gather",
    )(points, omega, order, siblings, cousins)


def sample_kernel(blocks, row_points, lists, out, total, rows):
    x, y, z, _ = place()
    for row_block in range(4):
        for half in range(2):
            rows[half * ROWS : (half + 1) * ROWS, :] = (
                row_points[2 * row_block + half].astype(F32).T.astype(BF16)
            )
        total[...] = jnp.zeros_like(total)
        for side, count in ((0, 16), (1, 32)):

            def add_block(entry, carry, side=side, row_block=row_block):
                block = lists[row_block, side, entry]

                @pl.when(block % 4 == x)
                def _():
                    slot = ((block // 4 + 4 - y) % 4) * 8 + (block // 16 + 8 - z) % 8
                    weights = blocks[slot, 0:ROWS, :]
                    columns = jnp.concatenate(
                        [blocks[slot, 256:272, :], blocks[slot, 272:288, :]], axis=1
                    )
                    for part in range(2):
                        span = pl.ds(part * ROWS, ROWS)
                        exponent = jnp.dot(rows[span, :], columns, preferred_element_type=F32)
                        tile = jnp.exp(exponent).astype(BF16)
                        total[side, span, :] += jnp.dot(tile, weights, preferred_element_type=F32)

                return carry

            lax.fori_loop(0, count, add_block, 0)
        for half in range(2):
            for side in range(2):
                out[half, row_block, :, side * SAMPLES : (side + 1) * SAMPLES] = total[
                    side, half * ROWS : (half + 1) * ROWS, :
                ]


def sample(blocks, row_points, lists):
    return pl.pallas_call(
        sample_kernel,
        out_shape=jax.ShapeDtypeStruct((2, 4, ROWS, RANK), F32),
        in_specs=[VMEM, VMEM, SMEM],
        out_specs=VMEM,
        scratch_shapes=[pltpu.VMEM((2, 2 * ROWS, SAMPLES), F32), pltpu.VMEM((2 * ROWS, 16), BF16)],
        compiler_params=pltpu.CompilerParams(vmem_limit_bytes=32 << 20),
        name="sample",
    )(blocks, row_points, lists)


def collect_kernel(
    parts, skeleton, tree_points,
    samples, full,
    other_core, relay_out, relay_in, near_out, near_in, table, other_table, piece, pieces,
    core_sems, relay_sems, near_sems, table_sems, piece_send, piece_recv,
    z_send, z_recv, y_sems, x_sems, swap_send, swap_recv,
):
    x, y, z, core = place()
    leaf = z * 16 + y * 4 + x
    node = z // 2
    other = device(x, y, z, 1 - core)
    mates = []
    for dz in range(2):
        for dy in range(4):
            for dx in range(4):
                if dz or dy or dx:
                    where = ((x + dx) % 4, (y + dy) % 4, node * 2 + (z + dz) % 2)
                    mates.append((dz * 16 + dy * 4 + dx, where, device(*where, core)))
    column = [device(x, y, (z + dz) % 8, core) for dz in range(1, 8)]
    strangers = [device(x, y, ((node + dn) % 4) * 2 + dz, core) for dn in range(1, 4) for dz in range(2)]
    greet([other] + [who for _, _, who in mates] + strangers)
    right, left = device((x + 1) % 4, y, z, core), device((x + 3) % 4, y, z, core)
    above, below = device(x, (y + 1) % 4, z, core), device(x, (y + 3) % 4, z, core)

    swap = send(parts.at[1 - core], other_core, core_sems.at[0], core_sems.at[1], other)
    swap.wait()

    def partial(place_x):
        return parts[core, place_x] + other_core[place_x]

    ahead, behind, across = (x + 1) % 4, (x + 3) % 4, (x + 2) % 4
    farthest = partial(across)
    relay_out[...] = farthest.astype(LINK)
    relays = [
        send(relay_out.at[0:128], relay_in.at[0], relay_sems.at[0], relay_sems.at[1], right),
        send(relay_out.at[128:256], relay_in.at[1], relay_sems.at[2], relay_sems.at[3], left),
    ]
    to_right, to_left = partial(ahead), partial(behind)
    near_out[0, 128:256, :] = to_right[128:256].astype(LINK)
    near_out[1, 0:128, :] = to_left[0:128].astype(LINK)
    nears = [
        send(near_out.at[0, 128:256], near_in.at[0, 128:256], near_sems.at[0], near_sems.at[1], right),
        send(near_out.at[1, 0:128], near_in.at[1, 0:128], near_sems.at[2], near_sems.at[3], left),
    ]
    relays[0].wait_recv()
    near_out[0, 0:128, :] = (to_right[0:128] + relay_in[0].astype(F32)).astype(LINK)
    nears.append(
        send(near_out.at[0, 0:128], near_in.at[0, 0:128], near_sems.at[4], near_sems.at[5], right)
    )
    relays[1].wait_recv()
    near_out[1, 128:256, :] = (to_left[128:256] + relay_in[1].astype(F32)).astype(LINK)
    nears.append(
        send(near_out.at[1, 128:256], near_in.at[1, 128:256], near_sems.at[6], near_sems.at[7], left)
    )
    mine = partial(x)
    first_row = (leaf * 2 + core) * ROWS
    row = lax.broadcasted_iota(jnp.int32, (ROWS, RANK), 0) + first_row
    chosen = jnp.where(row == skeleton[pl.ds(node, 1), :], 1.0, 0.0)
    skeleton_points = jnp.dot(
        tree_points[...].astype(BF16), chosen.astype(BF16), preferred_element_type=F32
    )
    for copy in nears:
        copy.wait_recv()
    rows = mine + (near_in[0].astype(F32) + near_in[1].astype(F32))
    samples[...] = rows

    table[0:256, :] = lax.dot_general(
        rows, rows, (((0,), (0,)), ((), ())), precision=HIGHEST, preferred_element_type=F32
    )
    table[128:256, 0:128] = jnp.zeros((128, 128), F32)
    table[128:136, 0:128] = skeleton_points[:, 0:128]
    table[136:144, 0:128] = skeleton_points[:, 128:256]
    table[256:512, :] = lax.dot_general(
        chosen, rows, (((0,), (0,)), ((), ())), precision=HIGHEST, preferred_element_type=F32
    )
    start = pl.multiple_of((1 - core) * 256, 256)
    swap_table = send(
        table.at[pl.ds(start, 256)], other_table, table_sems.at[0], table_sems.at[1], other
    )
    swap_table.wait()
    keep = pl.multiple_of(core * 256, 256)
    other_table[...] += table[pl.ds(keep, 256), :]

    def chunk(where):
        first = (where[0] * 8 + where[1] * 2 + where[2] % 2) * 8
        return other_table.at[pl.ds(pl.multiple_of(first, 8), 8)]

    spreads = []
    for slot, where, who in mates:
        spreads.append(
            send(chunk(where), pieces.at[slot], piece_send.at[slot], piece_recv.at[slot], who)
        )
    sums = chunk((x, y, z))[...]
    for copy in spreads:
        copy.wait_recv()
    for slot, _, _ in mates:
        sums = sums + pieces[slot]
    piece[...] = sums
    full[core, x, y, z] = sums
    for copy in spreads:
        copy.wait_send()

    stages = [
        send(piece, full.at[core, x, y, z], z_send.at[k], z_recv.at[k], who)
        for k, who in enumerate(column)
    ]
    for copy in stages:
        copy.wait()

    def ring(mine_at, sems, plus, minus, before, after, cut):
        mine_ref = full.at[mine_at]
        out = [
            send(mine_ref, mine_ref, sems.at[0], sems.at[1], plus),
            send(mine_ref, mine_ref, sems.at[2], sems.at[3], minus),
        ]
        out[0].wait_recv()
        first_half = full.at[before + (pl.ds(0, cut),)]
        out.append(send(first_half, first_half, sems.at[4], sems.at[5], plus))
        out[1].wait_recv()
        second_half = full.at[after + (pl.ds(cut, cut),)]
        out.append(send(second_half, second_half, sems.at[6], sems.at[7], minus))
        return out

    hops = ring((core, x, y), y_sems, above, below, (core, x, (y + 3) % 4), (core, x, (y + 1) % 4), 4)
    for copy in hops[2:]:
        copy.wait_recv()
    for copy in hops:
        copy.wait_send()

    hops = ring((core, x), x_sems, right, left, (core, behind), (core, ahead), 2)
    swaps = []

    def hand(place_x):
        ref = full.at[core, place_x]
        swaps.append(send(ref, ref, swap_send.at[len(swaps)], swap_recv.at[len(swaps)], other))

    hand(x)
    hand(behind)
    hand(ahead)
    for copy in hops[2:]:
        copy.wait_recv()
    hand(across)
    for copy in hops:
        copy.wait_send()
    for copy in swaps:
        copy.wait()
    for copy in relays + nears:
        copy.wait_send()


def collect(parts, skeleton, tree_points):
    dma = pltpu.SemaphoreType.DMA
    return pl.pallas_call(
        collect_kernel,
        out_shape=(
            jax.ShapeDtypeStruct((ROWS, RANK), F32),
            jax.ShapeDtypeStruct((2, 4, 4, 8, 8, RANK), F32),
        ),
        in_specs=[VMEM] * 3,
        out_specs=(VMEM,) * 2,
        scratch_shapes=[
            pltpu.VMEM((4, ROWS, RANK), F32),
            pltpu.VMEM((ROWS, RANK), LINK),
            pltpu.VMEM((2, 128, RANK), LINK),
            pltpu.VMEM((2, ROWS, RANK), LINK),
            pltpu.VMEM((2, ROWS, RANK), LINK),
            pltpu.VMEM((512, RANK), F32),
            pltpu.VMEM((256, RANK), F32),
            pltpu.VMEM((8, RANK), F32),
            pltpu.VMEM((32, 8, RANK), F32),
            dma((2,)), dma((4,)), dma((8,)), dma((2,)), dma((32,)), dma((32,)),
            dma((7,)), dma((7,)), dma((8,)), dma((8,)), dma((4,)), dma((4,)),
        ],
        compiler_params=pltpu.CompilerParams(
            collective_id=1, has_side_effects=True, vmem_limit_bytes=32 << 20
        ),
        name="collect",
    )(parts, skeleton, tree_points)


def finish_kernel(full, samples, basis, coupling, work, chosen):
    node = lax.axis_index("leaf") // 32
    row = lax.broadcasted_iota(jnp.int32, (RANK, RANK), 0)
    col = lax.broadcasted_iota(jnp.int32, (RANK, RANK), 1)
    skeleton_points = []
    for n in range(4):
        for at_x in range(4):
            for at_y in range(4):
                span = pl.ds(at_x * 64 + at_y * 16, 16)
                work[n, span, :] = full[0, at_x, at_y, 2 * n : 2 * n + 2].reshape(16, RANK)
                chosen[n, span, :] = full[1, at_x, at_y, 2 * n : 2 * n + 2].reshape(16, RANK)
        skeleton_points.append(
            jnp.concatenate([work[n, 128:136, 0:128], work[n, 136:144, 0:128]], axis=1)
        )
        gram = work[n]
        on_diagonal = jnp.where(row == col, gram, 0.0)
        trace = jnp.sum(jnp.sum(on_diagonal, axis=0, keepdims=True), axis=1, keepdims=True)
        work[n] = gram + jnp.where(row == col, 0.01 * trace, 0.0)

    middles = []
    for k in range(2):
        row_side = features(skeleton_points[2 * k], 4.0, True).T.astype(BF16)
        col_side = features(skeleton_points[2 * k + 1], 1.0, False).astype(BF16)
        kernel_skel = jnp.exp(jnp.dot(row_side, col_side, preferred_element_type=F32))
        right = jnp.dot(kernel_skel, chosen[2 * k + 1], precision=HIGH, preferred_element_type=F32)
        middles.append(
            lax.dot_general(
                chosen[2 * k], right, (((0,), (0,)), ((), ())),
                precision=HIGH, preferred_element_type=F32,
            )
        )

    lane8 = lax.broadcasted_iota(jnp.int32, (8, 128), 1)
    row8 = lax.broadcasted_iota(jnp.int32, (8, 128), 0)
    group8 = (lane8 // 32) * 32
    lane = lax.broadcasted_iota(jnp.int32, (32, 128), 1)
    for p in range(8):
        top = 32 * p
        aligned = (top // 128) * 128
        packed = jnp.zeros((32, 128), F32)
        for n in range(4):
            block = work[n, top : top + 32, aligned : aligned + 128]
            turn = (32 * n - (top - aligned)) % 128
            if turn:
                block = pltpu.roll(block, turn, 1)
            packed = jnp.where(lane // 32 == n, block, packed)
        left = [packed[8 * g : 8 * g + 8] for g in range(4)]
        inverse = [jnp.where(lane8 - group8 == row8 + 8 * g, 1.0, 0.0) for g in range(4)]
        for j in range(32):
            own, inner = j // 8, j % 8
            index = group8 + j
            spread = {
                g: jnp.take_along_axis(left[g], index, axis=1, mode="promise_in_bounds")
                for g in range(own, 4)
            }
            scale = lax.rsqrt(spread[own][inner : inner + 1, :])
            left_row = left[own][inner : inner + 1, :] * scale
            inverse_row = inverse[own][inner : inner + 1, :] * scale
            for g in range(own, 4):
                factor = spread[g] * scale
                if g == own:
                    factor = jnp.where(row8 > inner, factor, 0.0)
                left[g] = left[g] - factor * left_row
                inverse[g] = inverse[g] - factor * inverse_row
                if g == own:
                    inverse[g] = jnp.where(row8 == inner, inverse_row, inverse[g])
        packed = jnp.concatenate(inverse, axis=0)
        diagonal = jnp.concatenate([jnp.where(lane // 32 == n, packed, 0.0) for n in range(4)], axis=0)
        stacked = jnp.concatenate([work[n, top : top + 32, :] for n in range(4)], axis=0)
        srow = lax.broadcasted_iota(jnp.int32, (128, RANK), 0)
        scol = lax.broadcasted_iota(jnp.int32, (128, RANK), 1)
        identity = jnp.where(srow % 32 == scol % 32, 1.0, 0.0)
        stacked = jnp.where(scol // 32 == p, identity, stacked)
        solved = jnp.dot(diagonal, stacked, precision=HIGHEST, preferred_element_type=F32)
        done = jnp.where(scol < top + 32, solved, 0.0)
        for n in range(4):
            work[n, top : top + 32, :] = done[32 * n : 32 * n + 32]
        rest = RANK - top - 32
        if rest:
            turned = solved.T[top + 32 :, :]
            tlane = lax.broadcasted_iota(jnp.int32, (rest, 128), 1)
            tcol = lax.broadcasted_iota(jnp.int32, (rest, RANK), 1)
            for n in range(4):
                update = jnp.dot(
                    jnp.where(tlane // 32 == n, turned, 0.0), solved,
                    precision=HIGHEST, preferred_element_type=F32,
                )
                work[n, top + 32 :, :] = jnp.where(tcol // 32 == p, 0.0, work[n, top + 32 :, :]) - update

    last = (((1,), (1,)), ((), ()))
    basis[...] = 128.0 * lax.dot_general(
        samples[...], work[node], last, precision=HIGH, preferred_element_type=F32
    )
    for k in range(2):
        half = jnp.dot(work[2 * k], middles[k], precision=HIGH, preferred_element_type=F32)
        coupling[k] = (16384.0 / math.sqrt(RANK)) * lax.dot_general(
            half, work[2 * k + 1], last, precision=HIGH, preferred_element_type=F32
        )


def finish(full, samples):
    return pl.pallas_call(
        finish_kernel,
        out_shape=(
            jax.ShapeDtypeStruct((ROWS, RANK), F32),
            jax.ShapeDtypeStruct((2, RANK, RANK), F32),
        ),
        in_specs=[VMEM] * 2,
        out_specs=(VMEM,) * 2,
        scratch_shapes=[pltpu.VMEM((4, RANK, RANK), F32), pltpu.VMEM((4, RANK, RANK), F32)],
        compiler_params=pltpu.CompilerParams(vmem_limit_bytes=32 << 20),
        name="finish",
    )(full, samples)


def body(points, omega, tree_order, sibling_blocks, cousin_blocks, skeleton):
    blocks, row_points, lists, tree_points = gather(
        points, omega, tree_order.reshape(1, ROWS), sibling_blocks, cousin_blocks
    )
    parts = sample(blocks, row_points, lists)
    samples, full = collect(parts, skeleton, tree_points)
    return finish(full, samples)


def solution(mesh):
    return jax.shard_map(
        body,
        mesh=mesh,
        in_specs=(
            P(None, ("leaf", "sub")),
            P(None, ("leaf", "sub")),
            P(("leaf", "sub")),
            P("leaf", None),
            P("leaf", None),
            P(),
        ),
        out_specs=(P(("leaf", "sub"), None), P()),
        check_vma=False,
    )
```

```python
import functools
import math

import jax
import jax.numpy as jnp
from jax import lax
from jax.experimental import pallas as pl
from jax.experimental.pallas import tpu as pltpu
from jax.sharding import PartitionSpec as P

MESH = pl.DeviceIdType.MESH
HIGH = lax.Precision.HIGH
HIGHEST = lax.Precision.HIGHEST
F32 = jnp.float32
BF16 = jnp.bfloat16
VMEM = pl.BlockSpec(memory_space=pltpu.VMEM)
SMEM = pl.BlockSpec(memory_space=pltpu.SMEM)
HBM = pl.BlockSpec(memory_space=pltpu.HBM)

ROWS = 256
FEATS = 8
SAMPLES = 128
RANK = 256
SPAN = 288
LINK = F32


def place():
    leaf = lax.axis_index("leaf")
    core = lax.axis_index("sub")
    return leaf % 4, (leaf // 4) % 4, leaf // 16, core


def device(x, y, z, core):
    return (z * 16 + y * 4 + x, core)


def greet(partners):
    barrier = pltpu.get_barrier_semaphore()
    for partner in partners:
        pl.semaphore_signal(barrier, inc=1, device_id=partner, device_id_type=MESH)
    pl.semaphore_wait(barrier, len(partners))


def send(src, dst, send_sem, recv_sem, target):
    copy = pltpu.make_async_remote_copy(
        src_ref=src,
        dst_ref=dst,
        send_sem=send_sem,
        recv_sem=recv_sem,
        device_id=target,
        device_id_type=MESH,
    )
    copy.start()
    return copy


def features(coordinates, scale, ones_first):
    norm = -2.0 * jnp.sum(coordinates * coordinates, axis=0, keepdims=True)
    first = norm.astype(BF16).astype(F32)
    second = (norm - first).astype(BF16).astype(F32)
    third = norm - first - second
    row = lax.broadcasted_iota(jnp.int32, coordinates.shape, 0)
    start = 3 if ones_first else 0
    other = 0 if ones_first else 3
    tail = jnp.where((row >= other) & (row < other + 3), 1.0, 0.0)
    tail = jnp.where(row == start, first, tail)
    tail = jnp.where(row == start + 1, second, tail)
    tail = jnp.where(row == start + 2, third, tail)
    return jnp.concatenate([scale * coordinates, tail], axis=0)


def gather_kernel(
    points_in, omega_in, order_in, siblings_in, cousins_in,
    blocks, row_points, lists, tree_points,
    points, omega, order, siblings, cousins, load_sems, own, own_rows, own_lists,
    z_send, z_recv, up_send, up_recv, down_send, down_recv, far_send, far_recv,
    rows_send, rows_recv, list_send, list_recv,
):
    loads = [
        pltpu.make_async_copy(source, target, load_sems.at[k])
        for k, (source, target) in enumerate(
            [
                (omega_in, omega),
                (points_in, points),
                (order_in, order),
                (siblings_in, siblings),
                (cousins_in, cousins),
            ]
        )
    ]
    for copy in loads:
        copy.start()
    x, y, z, core = place()
    mate = 7 - 6 * (z % 2)
    offsets = [mate, 2, 6, 3, 5, 4]
    z_partners = [device(x, y, (z + offset) % 8, core) for offset in offsets]
    up = device(x, (y + 1) % 4, z, core)
    down = device(x, (y + 3) % 4, z, core)
    near = [
        (dx, dc, device((x + dx) % 4, y, z, (core + dc) % 2))
        for dx in range(4)
        for dc in range(2)
        if dx or dc
    ]
    loads[0].wait()
    own[0:ROWS, :] = omega[...].astype(F32).T.astype(BF16)
    loads[1].wait()
    columns = features(points[...].astype(F32), 1.0, False).astype(BF16)
    own[256:272, :] = columns[:, :128]
    own[272:288, :] = columns[:, 128:]
    greet(z_partners + [up, down] + [who for _, _, who in near])
    z_copies = []
    for k, offset in enumerate(offsets):
        back = (8 - offset) % 8
        z_copies.append(
            send(own, blocks.at[back], z_send.at[k], z_recv.at[back], z_partners[k])
        )

    for copy in loads[2:]:
        copy.wait()
    local = order[...] % ROWS
    lane = lax.broadcasted_iota(jnp.int32, (ROWS, ROWS), 0)
    pick = jnp.where(lane == local, 1.0, 0.0).astype(BF16)
    mine = jnp.dot(points[...], pick, preferred_element_type=F32)
    tree_points[...] = mine
    own_rows[...] = features(mine, 4.0, True).astype(BF16)
    own_lists[...] = jnp.zeros_like(own_lists)
    own_lists[0:1, 0:16] = siblings[...]
    own_lists[1:2, 0:32] = cousins[...]
    row_points[x * 2 + core] = own_rows[...]
    lists[x] = own_lists[...]
    small = []
    for k, (dx, dc, who) in enumerate(near):
        small.append(
            send(own_rows, row_points.at[x * 2 + core], rows_send.at[k], rows_recv.at[k], who)
        )
        if not dc:
            small.append(
                send(own_lists, lists.at[x], list_send.at[dx], list_recv.at[dx], who)
            )

    far = []

    def relay(k):
        offset = offsets[k]
        if k % 2:
            down_copies[k].wait_recv()
            far.append(
                send(blocks.at[24 + offset], blocks.at[16 + offset], far_send.at[k], far_recv.at[k], up)
            )
        else:
            up_copies[k].wait_recv()
            far.append(
                send(blocks.at[8 + offset], blocks.at[16 + offset], far_send.at[k], far_recv.at[k], down)
            )

    up_copies, down_copies = [], []
    for k, offset in enumerate(offsets):
        pltpu.make_async_remote_copy(
            src_ref=own, dst_ref=blocks.at[offset], send_sem=z_send.at[k],
            recv_sem=z_recv.at[offset], device_id=up, device_id_type=MESH,
        ).wait_recv()
        down_copies.append(
            send(blocks.at[offset], blocks.at[24 + offset], up_send.at[k], down_recv.at[k], up)
        )
        up_copies.append(
            send(blocks.at[offset], blocks.at[8 + offset], down_send.at[k], up_recv.at[k], down)
        )
        if k:
            relay(k - 1)
    relay(5)
    for k in range(6):
        if k % 2:
            up_copies[k].wait_recv()
        else:
            down_copies[k].wait_recv()
    for copy in far:
        copy.wait()
    for copy in small:
        copy.wait()
    for copy in z_copies + up_copies + down_copies:
        copy.wait_send()


def gather(points, omega, order, siblings, cousins):
    dma = pltpu.SemaphoreType.DMA
    return pl.pallas_call(
        gather_kernel,
        out_shape=(
            jax.ShapeDtypeStruct((32, SPAN, 128), BF16),
            jax.ShapeDtypeStruct((8, 16, ROWS), BF16),
            jax.ShapeDtypeStruct((4, 8, 128), jnp.int32),
            jax.ShapeDtypeStruct((FEATS, ROWS), F32),
        ),
        in_specs=[HBM] * 5,
        out_specs=(VMEM,) * 4,
        scratch_shapes=[
            pltpu.VMEM((FEATS, ROWS), BF16),
            pltpu.VMEM((SAMPLES, ROWS), BF16),
            pltpu.VMEM((1, ROWS), jnp.int32),
            pltpu.VMEM((1, 16), jnp.int32),
            pltpu.VMEM((1, 32), jnp.int32),
            dma((5,)),
            pltpu.VMEM((SPAN, 128), BF16),
            pltpu.VMEM((16, ROWS), BF16),
            pltpu.VMEM((8, 128), jnp.int32),
            dma((6,)), dma((8,)), dma((6,)), dma((6,)), dma((6,)), dma((6,)), dma((6,)), dma((6,)),
            dma((7,)), dma((7,)), dma((4,)), dma((4,)),
        ],
        compiler_params=pltpu.CompilerParams(
            collective_id=0, has_side_effects=True, vmem_limit_bytes=32 << 20
        ),
        name="gather",
    )(points, omega, order, siblings, cousins)


def sample_kernel(blocks, row_points, lists, out, total, rows, slots):
    x, y, z, _ = place()
    sides = ((0, 16), (1, 32))

    counts = {}
    for row_block in range(4):
        for side, length in sides:

            def pick(entry, count, row_block=row_block, side=side):
                block = lists[row_block, side, entry]
                slots[row_block, side, count] = ((block // 4 + 4 - y) % 4) * 8 + (block // 16 + 8 - z) % 8
                return count + jnp.where(block % 4 == x, 1, 0)

            counts[row_block, side] = lax.fori_loop(0, length, pick, 0, unroll=True)

    total[...] = jnp.zeros_like(total)
    for row_block in range(4):
        for half in range(2):
            rows[row_block, half * ROWS : (half + 1) * ROWS, :] = (
                row_points[2 * row_block + half].astype(F32).T.astype(BF16)
            )
        for side, _ in sides:
            count = counts[row_block, side]

            def add_pair(step, carry, row_block=row_block, side=side, count=count):
                first = 2 * step
                paired = first + 1 < count
                one = slots[row_block, side, first]
                two = jnp.where(paired, slots[row_block, side, first + 1], one)
                weight = jnp.where(paired, 1.0, 0.0).astype(BF16)
                columns = jnp.concatenate(
                    [
                        blocks[one, 256:272, :],
                        blocks[one, 272:288, :],
                        blocks[two, 256:272, :],
                        blocks[two, 272:288, :],
                    ],
                    axis=1,
                )
                weights = jnp.concatenate(
                    [blocks[one, 0:ROWS, :], blocks[two, 0:ROWS, :] * weight], axis=0
                )
                exponent = jnp.dot(rows[row_block], columns, preferred_element_type=F32)
                tile = jnp.exp(exponent).astype(BF16)
                total[row_block, side] += jnp.dot(tile, weights, preferred_element_type=F32)
                return carry

            lax.fori_loop(0, (count + 1) // 2, add_pair, 0)
        for half in range(2):
            for side in range(2):
                out[half, row_block, :, side * SAMPLES : (side + 1) * SAMPLES] = total[
                    row_block, side, half * ROWS : (half + 1) * ROWS, :
                ]


def sample(blocks, row_points, lists):
    return pl.pallas_call(
        sample_kernel,
        out_shape=jax.ShapeDtypeStruct((2, 4, ROWS, RANK), F32),
        in_specs=[VMEM, VMEM, SMEM],
        out_specs=VMEM,
        scratch_shapes=[
            pltpu.VMEM((4, 2, 2 * ROWS, SAMPLES), F32),
            pltpu.VMEM((4, 2 * ROWS, 16), BF16),
            pltpu.SMEM((4, 2, 40), jnp.int32),
        ],
        compiler_params=pltpu.CompilerParams(vmem_limit_bytes=32 << 20),
        name="sample",
    )(blocks, row_points, lists)


def collect_kernel(
    parts, skeleton, tree_points,
    samples, full,
    other_core, relay_out, relay_in, near_out, near_in, table, other_table, piece, pieces,
    core_sems, relay_sems, near_sems, table_sems, piece_send, piece_recv,
    z_send, z_recv, y_sems, x_sems, swap_sems,
):
    x, y, z, core = place()
    leaf = z * 16 + y * 4 + x
    node = z // 2
    other = device(x, y, z, 1 - core)
    mates = []
    for dz in range(2):
        for dy in range(4):
            for dx in range(4):
                if dz or dy or dx:
                    where = ((x + dx) % 4, (y + dy) % 4, node * 2 + (z + dz) % 2)
                    mates.append((dz * 16 + dy * 4 + dx, where, device(*where, core)))
    column = [device(x, y, (z + dz) % 8, core) for dz in range(1, 8)]
    strangers = [device(x, y, ((node + dn) % 4) * 2 + dz, core) for dn in range(1, 4) for dz in range(2)]
    greet([other] + [who for _, _, who in mates] + strangers)
    right, left = device((x + 1) % 4, y, z, core), device((x + 3) % 4, y, z, core)
    above, below = device(x, (y + 1) % 4, z, core), device(x, (y + 3) % 4, z, core)

    swap = send(parts.at[1 - core], other_core, core_sems.at[0], core_sems.at[1], other)
    swap.wait()

    def partial(place_x):
        return parts[core, place_x] + other_core[place_x]

    ahead, behind, across = (x + 1) % 4, (x + 3) % 4, (x + 2) % 4
    farthest = partial(across)
    relay_out[...] = farthest.astype(LINK)
    relays = [
        send(relay_out.at[0:128], relay_in.at[0], relay_sems.at[0], relay_sems.at[1], right),
        send(relay_out.at[128:256], relay_in.at[1], relay_sems.at[2], relay_sems.at[3], left),
    ]
    to_right, to_left = partial(ahead), partial(behind)
    near_out[0, 128:256, :] = to_right[128:256].astype(LINK)
    near_out[1, 0:128, :] = to_left[0:128].astype(LINK)
    nears = [
        send(near_out.at[0, 128:256], near_in.at[0, 128:256], near_sems.at[0], near_sems.at[1], right),
        send(near_out.at[1, 0:128], near_in.at[1, 0:128], near_sems.at[2], near_sems.at[3], left),
    ]
    relays[0].wait_recv()
    near_out[0, 0:128, :] = (to_right[0:128] + relay_in[0].astype(F32)).astype(LINK)
    nears.append(
        send(near_out.at[0, 0:128], near_in.at[0, 0:128], near_sems.at[4], near_sems.at[5], right)
    )
    relays[1].wait_recv()
    near_out[1, 128:256, :] = (to_left[128:256] + relay_in[1].astype(F32)).astype(LINK)
    nears.append(
        send(near_out.at[1, 128:256], near_in.at[1, 128:256], near_sems.at[6], near_sems.at[7], left)
    )
    mine = partial(x)
    first_row = (leaf * 2 + core) * ROWS
    row = lax.broadcasted_iota(jnp.int32, (ROWS, RANK), 0) + first_row
    chosen = jnp.where(row == skeleton[pl.ds(node, 1), :], 1.0, 0.0)
    skeleton_points = jnp.dot(
        tree_points[...].astype(BF16), chosen.astype(BF16), preferred_element_type=F32
    )
    for copy in nears:
        copy.wait_recv()
    rows = mine + (near_in[0].astype(F32) + near_in[1].astype(F32))
    samples[...] = rows

    table[0:256, :] = lax.dot_general(
        rows, rows, (((0,), (0,)), ((), ())), precision=HIGHEST, preferred_element_type=F32
    )
    table[128:256, 0:128] = jnp.zeros((128, 128), F32)
    table[128:136, 0:128] = skeleton_points[:, 0:128]
    table[136:144, 0:128] = skeleton_points[:, 128:256]
    table[256:512, :] = lax.dot_general(
        chosen, rows, (((0,), (0,)), ((), ())), precision=HIGHEST, preferred_element_type=F32
    )
    start = pl.multiple_of((1 - core) * 256, 256)
    swap_table = send(
        table.at[pl.ds(start, 256)], other_table, table_sems.at[0], table_sems.at[1], other
    )
    swap_table.wait()
    keep = pl.multiple_of(core * 256, 256)
    other_table[...] += table[pl.ds(keep, 256), :]

    def chunk(where):
        first = (where[0] * 8 + where[1] * 2 + where[2] % 2) * 8
        return other_table.at[pl.ds(pl.multiple_of(first, 8), 8)]

    spreads = []
    for slot, where, who in mates:
        spreads.append(
            send(chunk(where), pieces.at[slot], piece_send.at[slot], piece_recv.at[slot], who)
        )
    sums = chunk((x, y, z))[...]
    for copy in spreads:
        copy.wait_recv()
    for slot, _, _ in mates:
        sums = sums + pieces[slot]
    piece[...] = sums
    full[core, x, y, z] = sums
    for copy in spreads:
        copy.wait_send()

    stages = [
        send(piece, full.at[core, x, y, z], z_send.at[k], z_recv.at[k], who)
        for k, who in enumerate(column)
    ]
    for copy in stages:
        copy.wait()

    first_lanes, second_lanes = pl.ds(0, 128), pl.ds(128, 128)
    every8, every4 = pl.ds(0, 8), pl.ds(0, 4)
    cuts8, cuts4 = (pl.ds(0, 4), pl.ds(4, 4)), (pl.ds(0, 2), pl.ds(2, 2))
    next_y, last_y = (y + 1) % 4, (y + 3) % 4

    def push(ref, sems, k, who):
        return send(ref, ref, sems.at[2 * k], sems.at[2 * k + 1], who)

    def region(at_x, at_y, at_z, lanes):
        return full.at[core, at_x, at_y, at_z, every8, lanes]

    first = [push(region(x, y, every8, first_lanes), y_sems, 0, above)]
    first.append(push(region(x, y, every8, first_lanes), y_sems, 1, below))
    second = [push(region(x, y, every8, second_lanes), x_sems, 0, right)]
    second.append(push(region(x, y, every8, second_lanes), x_sems, 1, left))
    first[0].wait_recv()
    first.append(push(region(x, last_y, cuts8[0], first_lanes), y_sems, 2, above))
    second[0].wait_recv()
    second.append(push(region(behind, y, cuts8[0], second_lanes), x_sems, 2, right))
    first[1].wait_recv()
    first.append(push(region(x, next_y, cuts8[1], first_lanes), y_sems, 3, below))
    second[1].wait_recv()
    second.append(push(region(ahead, y, cuts8[1], second_lanes), x_sems, 3, left))
    for copy in first[2:]:
        copy.wait_recv()
    first.append(push(region(x, every4, every8, first_lanes), x_sems, 4, right))
    first.append(push(region(x, every4, every8, first_lanes), x_sems, 5, left))
    for copy in second[2:]:
        copy.wait_recv()
    second.append(push(region(every4, y, every8, second_lanes), y_sems, 4, above))
    second.append(push(region(every4, y, every8, second_lanes), y_sems, 5, below))
    swaps = []

    def hand(at_x, at_y, lanes):
        swaps.append(push(region(at_x, at_y, every8, lanes), swap_sems, len(swaps), other))

    hand(x, every4, first_lanes)
    hand(every4, y, second_lanes)
    first[4].wait_recv()
    first.append(push(region(behind, cuts4[0], every8, first_lanes), x_sems, 6, right))
    second[4].wait_recv()
    second.append(push(region(cuts4[0], last_y, every8, second_lanes), y_sems, 6, above))
    first[5].wait_recv()
    first.append(push(region(ahead, cuts4[1], every8, first_lanes), x_sems, 7, left))
    second[5].wait_recv()
    second.append(push(region(cuts4[1], next_y, every8, second_lanes), y_sems, 7, below))
    hand(behind, every4, first_lanes)
    hand(every4, last_y, second_lanes)
    hand(ahead, every4, first_lanes)
    hand(every4, next_y, second_lanes)
    for copy in first[6:]:
        copy.wait_recv()
    hand(across, every4, first_lanes)
    for copy in second[6:]:
        copy.wait_recv()
    hand(every4, (y + 2) % 4, second_lanes)
    for copy in first + second:
        copy.wait_send()
    for copy in swaps:
        copy.wait()
    for copy in relays + nears:
        copy.wait_send()


def collect(parts, skeleton, tree_points):
    dma = pltpu.SemaphoreType.DMA
    return pl.pallas_call(
        collect_kernel,
        out_shape=(
            jax.ShapeDtypeStruct((ROWS, RANK), F32),
            jax.ShapeDtypeStruct((2, 4, 4, 8, 8, RANK), F32),
        ),
        in_specs=[VMEM] * 3,
        out_specs=(VMEM,) * 2,
        scratch_shapes=[
            pltpu.VMEM((4, ROWS, RANK), F32),
            pltpu.VMEM((ROWS, RANK), LINK),
            pltpu.VMEM((2, 128, RANK), LINK),
            pltpu.VMEM((2, ROWS, RANK), LINK),
            pltpu.VMEM((2, ROWS, RANK), LINK),
            pltpu.VMEM((512, RANK), F32),
            pltpu.VMEM((256, RANK), F32),
            pltpu.VMEM((8, RANK), F32),
            pltpu.VMEM((32, 8, RANK), F32),
            dma((2,)), dma((4,)), dma((8,)), dma((2,)), dma((32,)), dma((32,)),
            dma((7,)), dma((7,)), dma((16,)), dma((16,)), dma((16,)),
        ],
        compiler_params=pltpu.CompilerParams(
            collective_id=1, has_side_effects=True, vmem_limit_bytes=32 << 20
        ),
        name="collect",
    )(parts, skeleton, tree_points)


def fold(factors, lines):
    a, b, c, d = (factor * values for factor, values in zip(factors, lines, strict=True))
    return (a + b) + (c + d)


def pivots(entry):
    def pair(a, b, c):
        scale = lax.rsqrt(a)
        return scale, b * scale, a * lax.rsqrt(a * (a * c - b * b))

    r0, l10, r1 = pair(entry(0, 0), entry(1, 0), entry(1, 1))
    l20, l30 = entry(2, 0) * r0, entry(3, 0) * r0
    l21, l31 = (entry(2, 1) - l20 * l10) * r1, (entry(3, 1) - l30 * l10) * r1
    r2, l32, r3 = pair(
        entry(2, 2) - (l20 * l20 + l21 * l21),
        entry(3, 2) - (l30 * l20 + l31 * l21),
        entry(3, 3) - (l30 * l30 + l31 * l31),
    )

    def solve(values):
        v0 = values[0] * r0
        v1 = (values[1] - v0 * l10) * r1
        v2 = (values[2] - (v0 * l20 + v1 * l21)) * r2
        v3 = ((values[3] - (v0 * l30 + v1 * l31)) - v2 * l32) * r3
        return [v0, v1, v2, v3]

    return solve


def finish_kernel(full, samples, basis, coupling, work, chosen):
    node = lax.axis_index("leaf") // 32
    row = lax.broadcasted_iota(jnp.int32, (RANK, RANK), 0)
    col = lax.broadcasted_iota(jnp.int32, (RANK, RANK), 1)
    skeleton_points, sizes = [], []
    for n in range(4):
        for at_x in range(4):
            for at_y in range(4):
                span = pl.ds(at_x * 64 + at_y * 16, 16)
                work[n, span, :] = full[0, at_x, at_y, 2 * n : 2 * n + 2].reshape(16, RANK)
                chosen[n, span, :] = full[1, at_x, at_y, 2 * n : 2 * n + 2].reshape(16, RANK)
        skeleton_points.append(
            jnp.concatenate([work[n, 128:136, 0:128], work[n, 136:144, 0:128]], axis=1)
        )
        gram = work[n]
        on_diagonal = jnp.where(row == col, gram, 0.0)
        trace = jnp.sum(jnp.sum(on_diagonal, axis=0, keepdims=True), axis=1, keepdims=True)
        work[n] = gram * (1.0 / trace) + jnp.where(row == col, 0.01, 0.0)
        sizes.append(lax.rsqrt(trace))

    middles = []
    for k in range(2):
        row_side = features(skeleton_points[2 * k], 4.0, True).T.astype(BF16)
        col_side = features(skeleton_points[2 * k + 1], 1.0, False).astype(BF16)
        kernel_skel = jnp.exp(jnp.dot(row_side, col_side, preferred_element_type=F32))
        right = jnp.dot(kernel_skel, chosen[2 * k + 1], precision=HIGH, preferred_element_type=F32)
        middles.append(
            lax.dot_general(
                chosen[2 * k], right, (((0,), (0,)), ((), ())),
                precision=HIGH, preferred_element_type=F32,
            )
        )

    lane8 = lax.broadcasted_iota(jnp.int32, (8, 128), 1)
    row8 = lax.broadcasted_iota(jnp.int32, (8, 128), 0)
    group8 = (lane8 // 32) * 32
    lane = lax.broadcasted_iota(jnp.int32, (32, 128), 1)
    for p in range(8):
        top = 32 * p
        aligned = (top // 128) * 128
        packed = jnp.zeros((32, 128), F32)
        for n in range(4):
            block = work[n, top : top + 32, aligned : aligned + 128]
            turn = (32 * n - (top - aligned)) % 128
            if turn:
                block = pltpu.roll(block, turn, 1)
            packed = jnp.where(lane // 32 == n, block, packed)
        left = [packed[8 * g : 8 * g + 8] for g in range(4)]
        inverse = [jnp.where(lane8 - group8 == row8 + 8 * g, 1.0, 0.0) for g in range(4)]
        for j in range(0, 32, 4):
            own, inner = j // 8, j % 8
            spread = {
                g: [
                    jnp.take_along_axis(left[g], group8 + (j + t), axis=1, mode="promise_in_bounds")
                    for t in range(4)
                ]
                for g in range(own, 4)
            }

            def line(tile, t, inner=inner):
                return jnp.broadcast_to(tile[inner + t : inner + t + 1, :], (8, 128))

            solve = pivots(lambda t, u: line(spread[own][u], t))
            left_rows = solve([line(left[own], t) for t in range(4)])
            inverse_rows = solve([line(inverse[own], t) for t in range(4)])
            for g in range(own, 4):
                if g == own and inner == 4:
                    continue
                factors = solve(spread[g])
                if g == own:
                    factors = [jnp.where(row8 > 3, factor, 0.0) for factor in factors]
                left[g] = left[g] - fold(factors, left_rows)
                inverse[g] = inverse[g] - fold(factors, inverse_rows)
            for t in range(4):
                inverse[own] = jnp.where(row8 == inner + t, inverse_rows[t], inverse[own])
        packed = jnp.concatenate(inverse, axis=0)
        diagonal = jnp.concatenate([jnp.where(lane // 32 == n, packed, 0.0) for n in range(4)], axis=0)
        stacked = jnp.concatenate([work[n, top : top + 32, :] for n in range(4)], axis=0)
        srow = lax.broadcasted_iota(jnp.int32, (128, RANK), 0)
        scol = lax.broadcasted_iota(jnp.int32, (128, RANK), 1)
        identity = jnp.where(srow % 32 == scol % 32, 1.0, 0.0)
        stacked = jnp.where(scol // 32 == p, identity, stacked)
        solved = jnp.dot(diagonal, stacked, precision=HIGHEST, preferred_element_type=F32)
        done = jnp.where(scol < top + 32, solved, 0.0)
        for n in range(4):
            work[n, top : top + 32, :] = done[32 * n : 32 * n + 32]
        rest = RANK - top - 32
        if rest:
            turned = solved.T[top + 32 :, :]
            tlane = lax.broadcasted_iota(jnp.int32, (rest, 128), 1)
            tcol = lax.broadcasted_iota(jnp.int32, (rest, RANK), 1)
            for n in range(4):
                update = jnp.dot(
                    jnp.where(tlane // 32 == n, turned, 0.0), solved,
                    precision=HIGHEST, preferred_element_type=F32,
                )
                work[n, top + 32 :, :] = jnp.where(tcol // 32 == p, 0.0, work[n, top + 32 :, :]) - update

    last = (((1,), (1,)), ((), ()))
    size = sum(jnp.where(node == n, sizes[n], 0.0) for n in range(4))
    basis[...] = (128.0 * size) * lax.dot_general(
        samples[...], work[node], last, precision=HIGH, preferred_element_type=F32
    )
    for k in range(2):
        half = jnp.dot(work[2 * k], middles[k], precision=HIGH, preferred_element_type=F32)
        coupling[k] = ((16384.0 / math.sqrt(RANK)) * sizes[2 * k] * sizes[2 * k + 1]) * lax.dot_general(
            half, work[2 * k + 1], last, precision=HIGH, preferred_element_type=F32
        )


def finish(full, samples):
    return pl.pallas_call(
        finish_kernel,
        out_shape=(
            jax.ShapeDtypeStruct((ROWS, RANK), F32),
            jax.ShapeDtypeStruct((2, RANK, RANK), F32),
        ),
        in_specs=[VMEM] * 2,
        out_specs=(VMEM,) * 2,
        scratch_shapes=[pltpu.VMEM((4, RANK, RANK), F32), pltpu.VMEM((4, RANK, RANK), F32)],
        compiler_params=pltpu.CompilerParams(vmem_limit_bytes=32 << 20),
        name="finish",
    )(full, samples)


def body(points, omega, tree_order, sibling_blocks, cousin_blocks, skeleton):
    blocks, row_points, lists, tree_points = gather(
        points, omega, tree_order.reshape(1, ROWS), sibling_blocks, cousin_blocks
    )
    parts = sample(blocks, row_points, lists)
    samples, full = collect(parts, skeleton, tree_points)
    return finish(full, samples)


def solution(mesh):
    return jax.shard_map(
        body,
        mesh=mesh,
        in_specs=(
            P(None, ("leaf", "sub")),
            P(None, ("leaf", "sub")),
            P(("leaf", "sub")),
            P("leaf", None),
            P("leaf", None),
            P(),
        ),
        out_specs=(P(("leaf", "sub"), None), P()),
        check_vma=False,
    )
```

```python
import functools
import math

import jax
import jax.numpy as jnp
from jax import lax
from jax.experimental import pallas as pl
from jax.experimental.pallas import tpu as pltpu
from jax.sharding import PartitionSpec as P

MESH = pl.DeviceIdType.MESH
HIGH = lax.Precision.HIGH
HIGHEST = lax.Precision.HIGHEST
F32 = jnp.float32
BF16 = jnp.bfloat16
VMEM = pl.BlockSpec(memory_space=pltpu.VMEM)
SMEM = pl.BlockSpec(memory_space=pltpu.SMEM)
HBM = pl.BlockSpec(memory_space=pltpu.HBM)

ROWS = 256
FEATS = 8
SAMPLES = 128
RANK = 256
SPAN = 288
LINK = BF16


def place():
    leaf = lax.axis_index("leaf")
    core = lax.axis_index("sub")
    return leaf % 4, (leaf // 4) % 4, leaf // 16, core


def device(x, y, z, core):
    return (z * 16 + y * 4 + x, core)


def greet(partners):
    barrier = pltpu.get_barrier_semaphore()
    for partner in partners:
        pl.semaphore_signal(barrier, inc=1, device_id=partner, device_id_type=MESH)
    pl.semaphore_wait(barrier, len(partners))


def send(src, dst, send_sem, recv_sem, target):
    copy = pltpu.make_async_remote_copy(
        src_ref=src,
        dst_ref=dst,
        send_sem=send_sem,
        recv_sem=recv_sem,
        device_id=target,
        device_id_type=MESH,
    )
    copy.start()
    return copy


def features(coordinates, scale, ones_first):
    norm = -2.0 * jnp.sum(coordinates * coordinates, axis=0, keepdims=True)
    first = norm.astype(BF16).astype(F32)
    second = (norm - first).astype(BF16).astype(F32)
    third = norm - first - second
    row = lax.broadcasted_iota(jnp.int32, coordinates.shape, 0)
    start = 3 if ones_first else 0
    other = 0 if ones_first else 3
    tail = jnp.where((row >= other) & (row < other + 3), 1.0, 0.0)
    tail = jnp.where(row == start, first, tail)
    tail = jnp.where(row == start + 1, second, tail)
    tail = jnp.where(row == start + 2, third, tail)
    return jnp.concatenate([scale * coordinates, tail], axis=0)


def plane_kind(dz):
    return jnp.where((dz == 2) | (dz == 4) | (dz == 5), 0, 1)


def pick_slots(lists, x, y, z):
    lane = lax.broadcasted_iota(jnp.int32, (8, 128), 1)
    kind = lax.broadcasted_iota(jnp.int32, (8, 128), 0) // 4
    along, dz = lane // 8, lane % 8
    plane = ((z + dz) % 8) * 16
    block = jnp.where(
        kind == 0, plane + ((y + along) % 4) * 4 + x, plane + y * 4 + (x + along) % 4
    )
    named = jnp.where((lane < 32) & (plane_kind(dz) == kind), block, -1).astype(F32)
    hit = jnp.zeros((8, 128), F32)
    for side, length in ((0, 16), (1, 32)):
        entries = jnp.concatenate(
            [lists[k, at, side : side + 1, :] for k in range(2) for at in range(4)], axis=0
        ).astype(F32)
        for e in range(length):
            hit = jnp.where(named == jnp.broadcast_to(entries[:, e : e + 1], (8, 128)), 1.0, hit)
    place_of = lane.astype(F32)
    count = jnp.zeros((8, 128), F32)
    found = jnp.zeros((8, 128), F32)
    for slot in range(32):
        if slot % 8:
            here = jnp.broadcast_to(hit[:, slot : slot + 1], (8, 128))
            found = jnp.where((place_of == count) & (here > 0.5), float(slot), found)
            count = count + here
    return jnp.where(lane == 127, count, found).astype(jnp.int32)


def gather_kernel(
    points_in, omega_in, order_in, siblings_in, cousins_in,
    blocks, row_points, picks, tree_points,
    points, omega, order, siblings, cousins, load_sems, own, own_rows, own_lists, lists,
    z_send, z_recv, out_send, out_recv, far_send, far_recv,
    rows_send, rows_recv, list_send, list_recv,
):
    loads = [
        pltpu.make_async_copy(source, target, load_sems.at[k])
        for k, (source, target) in enumerate(
            [
                (omega_in, omega),
                (points_in, points),
                (order_in, order),
                (siblings_in, siblings),
                (cousins_in, cousins),
            ]
        )
    ]
    for copy in loads:
        copy.start()
    x, y, z, core = place()
    mate = 7 - 6 * (z % 2)
    upward, downward = device(x, y, (z + 1) % 8, core), device(x, y, (z + 7) % 8, core)
    plus = [device(x, (y + 1) % 4, z, core), device((x + 1) % 4, y, z, core)]
    minus = [device(x, (y + 3) % 4, z, core), device((x + 3) % 4, y, z, core)]
    along_x = [(d, c, device((x + d) % 4, y, z, (core + c) % 2)) for d in range(4) for c in range(2) if d or c]
    along_y = [(d, c, device(x, (y + d) % 4, z, (core + c) % 2)) for d in range(4) for c in range(2) if d or c]
    greet([upward, downward] + [who for _, _, who in along_x] + [who for _, _, who in along_y[1:]])

    loads[0].wait()
    own[0:ROWS, :] = omega[...].astype(F32).T.astype(BF16)
    loads[1].wait()
    columns = features(points[...].astype(F32), 1.0, False).astype(BF16)
    own[256:272, :] = columns[:, :128]
    own[272:288, :] = columns[:, 128:]
    halves = (pl.ds(0, SPAN // 2), pl.ds(SPAN // 2, SPAN // 2))

    def hop(k, src, dst, who):
        return send(src, dst, z_send.at[k], z_recv.at[k], who)

    hops = [hop(0, own, blocks.at[7], upward), hop(1, own, blocks.at[1], downward)]

    for copy in loads[2:]:
        copy.wait()
    local = order[...] % ROWS
    lane = lax.broadcasted_iota(jnp.int32, (ROWS, ROWS), 0)
    pick = jnp.where(lane == local, 1.0, 0.0).astype(BF16)
    mine = jnp.dot(points[...], pick, preferred_element_type=F32)
    tree_points[...] = mine
    own_rows[...] = features(mine, 4.0, True).astype(BF16)
    own_lists[...] = jnp.zeros_like(own_lists)
    own_lists[0:1, 0:16] = siblings[...]
    own_lists[1:2, 0:32] = cousins[...]
    small = []
    for kind, (at, partners) in enumerate(((x, along_x), (y, along_y))):
        row_points[kind, at * 2 + core] = own_rows[...]
        lists[kind, at] = own_lists[...]
        for k, (d, c, who) in enumerate(partners):
            target = row_points.at[kind, at * 2 + core]
            small.append(send(own_rows, target, rows_send.at[kind, k], rows_recv.at[kind, k], who))
            if not c:
                target = lists.at[kind, at]
                small.append(send(own_lists, target, list_send.at[kind, d], list_recv.at[kind, d], who))

    outs, fars = {}, []

    def fan_out(k, kind, dz):
        block = blocks.at[dz]
        outs[k] = (
            send(block, blocks.at[24 + dz], out_send.at[2 * k], out_recv.at[2 * k], plus[kind]),
            send(block, blocks.at[8 + dz], out_send.at[2 * k + 1], out_recv.at[2 * k + 1], minus[kind]),
        )

    def relay(k, kind, dz):
        for side, (at, half, who) in enumerate(((24, halves[0], plus[kind]), (8, halves[1], minus[kind]))):
            outs[k][side].wait_recv()
            fars.append(
                send(
                    blocks.at[at + dz, half], blocks.at[16 + dz, half],
                    far_send.at[2 * k + side], far_recv.at[2 * k + side], who,
                )
            )

    hops[0].wait_recv()
    hops.append(hop(2, blocks.at[7], blocks.at[6], upward))
    hops[1].wait_recv()
    hops.append(hop(3, blocks.at[1], blocks.at[2], downward))
    fan_out(0, 1, mate)
    hops[2].wait_recv()
    hops.append(hop(4, blocks.at[6], blocks.at[5], upward))
    fan_out(1, 1, 6)
    hops[3].wait_recv()
    hops.append(hop(5, blocks.at[2], blocks.at[3], downward))
    fan_out(2, 0, 2)
    relay(0, 1, mate)
    hops[4].wait_recv()
    hops.append(hop(6, blocks.at[5, halves[0]], blocks.at[4, halves[0]], upward))
    fan_out(3, 0, 5)
    hops[5].wait_recv()
    hops.append(hop(7, blocks.at[3, halves[1]], blocks.at[4, halves[1]], downward))
    fan_out(4, 1, 3)
    relay(1, 1, 6)
    relay(2, 0, 2)
    hops[6].wait_recv()
    hops[7].wait_recv()
    fan_out(5, 0, 4)
    relay(3, 0, 5)
    relay(4, 1, 3)
    relay(5, 0, 4)
    for copy in small:
        copy.wait()
    picks[...] = pick_slots(lists, x, y, z)
    for copy in fars:
        copy.wait()
    for copy in hops:
        copy.wait_send()
    for pair in outs.values():
        for copy in pair:
            copy.wait_send()


def gather(points, omega, order, siblings, cousins):
    dma = pltpu.SemaphoreType.DMA
    return pl.pallas_call(
        gather_kernel,
        out_shape=(
            jax.ShapeDtypeStruct((32, SPAN, 128), BF16),
            jax.ShapeDtypeStruct((2, 8, 16, ROWS), BF16),
            jax.ShapeDtypeStruct((8, 128), jnp.int32),
            jax.ShapeDtypeStruct((FEATS, ROWS), F32),
        ),
        in_specs=[HBM] * 5,
        out_specs=(VMEM,) * 4,
        scratch_shapes=[
            pltpu.VMEM((FEATS, ROWS), BF16),
            pltpu.VMEM((SAMPLES, ROWS), BF16),
            pltpu.VMEM((1, ROWS), jnp.int32),
            pltpu.VMEM((1, 16), jnp.int32),
            pltpu.VMEM((1, 32), jnp.int32),
            dma((5,)),
            pltpu.VMEM((SPAN, 128), BF16),
            pltpu.VMEM((16, ROWS), BF16),
            pltpu.VMEM((8, 128), jnp.int32),
            pltpu.VMEM((2, 4, 8, 128), jnp.int32),
            dma((8,)), dma((8,)), dma((12,)), dma((12,)), dma((12,)), dma((12,)),
            dma((2, 7)), dma((2, 7)), dma((2, 4)), dma((2, 4)),
        ],
        compiler_params=pltpu.CompilerParams(
            collective_id=0, has_side_effects=True, vmem_limit_bytes=32 << 20
        ),
        name="gather",
    )(points, omega, order, siblings, cousins)


def sample_kernel(blocks, row_points, picks, out, rows, even_tile, odd_tile, items):
    _, _, z, _ = place()

    total = 0
    for row in range(8):
        count = picks[row, 127]

        def note(step, at, row=row, count=count):
            items[at, 0] = row
            items[at, 1] = picks[row, 2 * step]
            paired = 2 * step + 1 < count
            items[at, 2] = jnp.where(paired, picks[row, 2 * step + 1], picks[row, 2 * step])
            items[at, 3] = jnp.where(paired, 2, 1)
            return at + 1

        total = lax.fori_loop(0, (count + 1) // 2, note, total)
    for extra in range(2):
        items[total + extra, 0] = 0
        items[total + extra, 1] = jnp.where(total > 0, items[0, 1], 6)
        items[total + extra, 2] = items[total + extra, 1]
        items[total + extra, 3] = 0

    out[...] = jnp.zeros_like(out)
    for row in range(8):
        for half in range(2):
            rows[row, half * ROWS : (half + 1) * ROWS, :] = (
                row_points[row // 4, 2 * (row % 4) + half].astype(F32).T.astype(BF16)
            )

    def kernel_tile(item, tile):
        columns = jnp.concatenate(
            [blocks[items[item, k], at : at + 16, :] for k in (1, 2) for at in (256, 272)], axis=1
        )
        exponent = jnp.dot(rows[items[item, 0]], columns, preferred_element_type=F32)
        tile[...] = jnp.exp(exponent).astype(BF16)

    def add(item, tile):
        weights = []
        for k in (1, 2):
            slot = items[item, k]
            sibling = ((z + slot % 8) % 8) // 4 == z // 4
            use = items[item, 3] >= k
            values = blocks[slot, 0:ROWS, :]
            near = jnp.where(use & sibling, 1.0, 0.0).astype(BF16)
            far = jnp.where(use & jnp.logical_not(sibling), 1.0, 0.0).astype(BF16)
            weights.append(jnp.concatenate([values * near, values * far], axis=1))
        terms = jnp.dot(tile[...], jnp.concatenate(weights, axis=0), preferred_element_type=F32)
        kind, at = items[item, 0] // 4, items[item, 0] % 4
        out[0, kind, at] += terms[0:ROWS]
        out[1, kind, at] += terms[ROWS:]

    kernel_tile(0, even_tile)

    def two_items(step, carry):
        kernel_tile(2 * step + 1, odd_tile)
        add(2 * step, even_tile)
        kernel_tile(2 * step + 2, even_tile)
        add(2 * step + 1, odd_tile)
        return carry

    lax.fori_loop(0, (total + 1) // 2, two_items, 0)


def sample(blocks, row_points, picks):
    return pl.pallas_call(
        sample_kernel,
        out_shape=jax.ShapeDtypeStruct((2, 2, 4, ROWS, RANK), F32),
        in_specs=[VMEM, VMEM, SMEM],
        out_specs=VMEM,
        scratch_shapes=[
            pltpu.VMEM((8, 2 * ROWS, 16), BF16),
            pltpu.VMEM((2 * ROWS, 2 * ROWS), BF16),
            pltpu.VMEM((2 * ROWS, 2 * ROWS), BF16),
            pltpu.SMEM((64, 4), jnp.int32),
        ],
        compiler_params=pltpu.CompilerParams(vmem_limit_bytes=32 << 20),
        name="sample",
    )(blocks, row_points, picks)


def collect_kernel(
    parts, skeleton, tree_points,
    samples, full_a, full_b,
    other_core, relay_out, relay_in, near_out, near_in, table, other_table, piece, pieces,
    core_send, core_recv, relay_sems, near_sems, table_sems, piece_send, piece_recv,
    z_send, z_recv, y_sems, x_sems, swap_sems,
):
    x, y, z, core = place()
    leaf = z * 16 + y * 4 + x
    node = z // 2
    other = device(x, y, z, 1 - core)
    mates = []
    for dz in range(2):
        for dy in range(4):
            for dx in range(4):
                if dz or dy or dx:
                    where = ((x + dx) % 4, (y + dy) % 4, node * 2 + (z + dz) % 2)
                    mates.append((dz * 16 + dy * 4 + dx, where, device(*where, core)))
    column = [device(x, y, (z + dz) % 8, core) for dz in range(1, 8)]
    strangers = [device(x, y, ((node + dn) % 4) * 2 + dz, core) for dn in range(1, 4) for dz in range(2)]
    greet([other] + [who for _, _, who in mates] + strangers)
    right, left = device((x + 1) % 4, y, z, core), device((x + 3) % 4, y, z, core)
    above, below = device(x, (y + 1) % 4, z, core), device(x, (y + 3) % 4, z, core)

    ahead, behind, across = (x + 1) % 4, (x + 3) % 4, (x + 2) % 4
    next_y, last_y = (y + 1) % 4, (y + 3) % 4
    order = [(across, (y + 2) % 4), (ahead, next_y), (behind, last_y), (x, y)]
    swap = {}
    for step, places in enumerate(order):
        for kind in range(2):
            at = places[kind]
            swap[step, kind] = send(
                parts.at[1 - core, kind, at], other_core.at[kind, at],
                core_send.at[kind, step], core_recv.at[kind, step], other,
            )

    def partial(step, kind):
        swap[step, kind].wait_recv()
        at = order[step][kind]
        return parts[core, kind, at] + other_core[kind, at]

    plus, minus = (right, above), (left, below)
    lower, upper = pl.ds(0, 128), pl.ds(128, 128)
    relays, nears = [], []
    for kind in range(2):
        relay_out[kind] = partial(0, kind).astype(LINK)
        for side, (rows_of, who) in enumerate(((lower, plus[kind]), (upper, minus[kind]))):
            relays.append(
                send(
                    relay_out.at[kind, rows_of], relay_in.at[kind, side],
                    relay_sems.at[0, kind, side], relay_sems.at[1, kind, side], who,
                )
            )

    def pass_on(kind, side, first, rows_of, who):
        ref = near_out.at[kind, side, rows_of]
        landing = near_in.at[kind, side, rows_of]
        nears.append(send(ref, landing, near_sems.at[0, kind, side, first], near_sems.at[1, kind, side, first], who))

    waiting = {}
    for kind in range(2):
        to_plus, to_minus = partial(1, kind), partial(2, kind)
        near_out[kind, 0, 128:256, :] = to_plus[128:256].astype(LINK)
        near_out[kind, 1, 0:128, :] = to_minus[0:128].astype(LINK)
        pass_on(kind, 0, 0, upper, plus[kind])
        pass_on(kind, 1, 0, lower, minus[kind])
        waiting[kind] = (to_plus[0:128], to_minus[128:256])
    for kind in range(2):
        relays[2 * kind].wait_recv()
        near_out[kind, 0, 0:128, :] = (waiting[kind][0] + relay_in[kind, 0].astype(F32)).astype(LINK)
        pass_on(kind, 0, 1, lower, plus[kind])
        relays[2 * kind + 1].wait_recv()
        near_out[kind, 1, 128:256, :] = (waiting[kind][1] + relay_in[kind, 1].astype(F32)).astype(LINK)
        pass_on(kind, 1, 1, upper, minus[kind])
    mine = partial(3, 0) + partial(3, 1)
    first_row = (leaf * 2 + core) * ROWS
    row = lax.broadcasted_iota(jnp.int32, (ROWS, RANK), 0) + first_row
    chosen = jnp.where(row == skeleton[pl.ds(node, 1), :], 1.0, 0.0)
    skeleton_points = jnp.dot(
        tree_points[...].astype(BF16), chosen.astype(BF16), preferred_element_type=F32
    )
    for copy in nears:
        copy.wait_recv()
    for kind in range(2):
        for side in range(2):
            mine = mine + near_in[kind, side].astype(F32)
    rows = mine
    samples[...] = rows

    table[0:256, :] = lax.dot_general(
        rows, rows, (((0,), (0,)), ((), ())), precision=HIGHEST, preferred_element_type=F32
    )
    table[128:256, 0:128] = jnp.zeros((128, 128), F32)
    table[128:136, 0:128] = skeleton_points[:, 0:128]
    table[136:144, 0:128] = skeleton_points[:, 128:256]
    table[256:512, :] = lax.dot_general(
        chosen, rows, (((0,), (0,)), ((), ())), precision=HIGHEST, preferred_element_type=F32
    )
    start = pl.multiple_of((1 - core) * 256, 256)
    swap_table = send(
        table.at[pl.ds(start, 256)], other_table, table_sems.at[0], table_sems.at[1], other
    )
    swap_table.wait()
    keep = pl.multiple_of(core * 256, 256)
    other_table[...] += table[pl.ds(keep, 256), :]

    def chunk(where):
        first = (where[0] * 8 + where[1] * 2 + where[2] % 2) * 8
        return other_table.at[pl.ds(pl.multiple_of(first, 8), 8)]

    spreads = []
    for slot, where, who in mates:
        spreads.append(
            send(chunk(where), pieces.at[slot], piece_send.at[slot], piece_recv.at[slot], who)
        )
    sums = chunk((x, y, z))[...]
    for copy in spreads:
        copy.wait_recv()
    for slot, _, _ in mates:
        sums = sums + pieces[slot]
    piece[0] = sums[:, 0:128]
    piece[1] = sums[:, 128:256]
    full_a[core, x, y, z] = sums[:, 0:128]
    full_b[core, y, x, z] = sums[:, 128:256]
    for copy in spreads:
        copy.wait_send()

    stages = []
    for k, who in enumerate(column):
        stages.append(send(piece.at[0], full_a.at[core, x, y, z], z_send.at[2 * k], z_recv.at[2 * k], who))
        stages.append(
            send(piece.at[1], full_b.at[core, y, x, z], z_send.at[2 * k + 1], z_recv.at[2 * k + 1], who)
        )
    for copy in stages:
        copy.wait()

    cuts8, cuts4 = (pl.ds(0, 4), pl.ds(4, 4)), (pl.ds(0, 2), pl.ds(2, 2))
    half_a, half_b = full_a.at[core], full_b.at[core]

    def push(ref, sems, k, who):
        return send(ref, ref, sems.at[2 * k], sems.at[2 * k + 1], who)

    first = [push(half_a.at[x, y], y_sems, 0, above), push(half_a.at[x, y], y_sems, 1, below)]
    second = [push(half_b.at[y, x], x_sems, 0, right), push(half_b.at[y, x], x_sems, 1, left)]
    first[0].wait_recv()
    first.append(push(half_a.at[x, last_y, cuts8[0]], y_sems, 2, above))
    second[0].wait_recv()
    second.append(push(half_b.at[y, behind, cuts8[0]], x_sems, 2, right))
    first[1].wait_recv()
    first.append(push(half_a.at[x, next_y, cuts8[1]], y_sems, 3, below))
    second[1].wait_recv()
    second.append(push(half_b.at[y, ahead, cuts8[1]], x_sems, 3, left))
    for copy in first[2:]:
        copy.wait_recv()
    first.append(push(half_a.at[x], x_sems, 4, right))
    first.append(push(half_a.at[x], x_sems, 5, left))
    for copy in second[2:]:
        copy.wait_recv()
    second.append(push(half_b.at[y], y_sems, 4, above))
    second.append(push(half_b.at[y], y_sems, 5, below))
    swaps = []

    def hand(ref):
        swaps.append(push(ref, swap_sems, len(swaps), other))

    hand(half_a.at[x])
    hand(half_b.at[y])
    first[4].wait_recv()
    first.append(push(half_a.at[behind, cuts4[0]], x_sems, 6, right))
    second[4].wait_recv()
    second.append(push(half_b.at[last_y, cuts4[0]], y_sems, 6, above))
    first[5].wait_recv()
    first.append(push(half_a.at[ahead, cuts4[1]], x_sems, 7, left))
    second[5].wait_recv()
    second.append(push(half_b.at[next_y, cuts4[1]], y_sems, 7, below))
    hand(half_a.at[behind])
    hand(half_b.at[last_y])
    hand(half_a.at[ahead])
    hand(half_b.at[next_y])
    for copy in first[6:]:
        copy.wait_recv()
    hand(half_a.at[across])
    for copy in second[6:]:
        copy.wait_recv()
    hand(half_b.at[(y + 2) % 4])
    for copy in first + second:
        copy.wait_send()
    for copy in swaps:
        copy.wait()
    for copy in relays + nears + list(swap.values()):
        copy.wait_send()


def collect(parts, skeleton, tree_points):
    dma = pltpu.SemaphoreType.DMA
    return pl.pallas_call(
        collect_kernel,
        out_shape=(
            jax.ShapeDtypeStruct((ROWS, RANK), F32),
            jax.ShapeDtypeStruct((2, 4, 4, 8, 8, 128), F32),
            jax.ShapeDtypeStruct((2, 4, 4, 8, 8, 128), F32),
        ),
        in_specs=[VMEM] * 3,
        out_specs=(VMEM,) * 3,
        scratch_shapes=[
            pltpu.VMEM((2, 4, ROWS, RANK), F32),
            pltpu.VMEM((2, ROWS, RANK), LINK),
            pltpu.VMEM((2, 2, 128, RANK), LINK),
            pltpu.VMEM((2, 2, ROWS, RANK), LINK),
            pltpu.VMEM((2, 2, ROWS, RANK), LINK),
            pltpu.VMEM((512, RANK), F32),
            pltpu.VMEM((256, RANK), F32),
            pltpu.VMEM((2, 8, 128), F32),
            pltpu.VMEM((32, 8, RANK), F32),
            dma((2, 4)), dma((2, 4)), dma((2, 2, 2)), dma((2, 2, 2, 2)), dma((2,)), dma((32,)), dma((32,)),
            dma((14,)), dma((14,)), dma((16,)), dma((16,)), dma((16,)),
        ],
        compiler_params=pltpu.CompilerParams(
            collective_id=1, has_side_effects=True, vmem_limit_bytes=32 << 20
        ),
        name="collect",
    )(parts, skeleton, tree_points)


def fold(factors, lines):
    a, b, c, d = (factor * values for factor, values in zip(factors, lines, strict=True))
    return (a + b) + (c + d)


def pivots(entry):
    def pair(a, b, c):
        scale = lax.rsqrt(a)
        return scale, b * scale, a * lax.rsqrt(a * (a * c - b * b))

    r0, l10, r1 = pair(entry(0, 0), entry(1, 0), entry(1, 1))
    l20, l30 = entry(2, 0) * r0, entry(3, 0) * r0
    l21, l31 = (entry(2, 1) - l20 * l10) * r1, (entry(3, 1) - l30 * l10) * r1
    r2, l32, r3 = pair(
        entry(2, 2) - (l20 * l20 + l21 * l21),
        entry(3, 2) - (l30 * l20 + l31 * l21),
        entry(3, 3) - (l30 * l30 + l31 * l31),
    )

    def solve(values):
        v0 = values[0] * r0
        v1 = (values[1] - v0 * l10) * r1
        v2 = (values[2] - (v0 * l20 + v1 * l21)) * r2
        v3 = ((values[3] - (v0 * l30 + v1 * l31)) - v2 * l32) * r3
        return [v0, v1, v2, v3]

    return solve


def finish_kernel(full_a, full_b, samples, basis, coupling, work, chosen):
    node = lax.axis_index("leaf") // 32
    row = lax.broadcasted_iota(jnp.int32, (RANK, RANK), 0)
    col = lax.broadcasted_iota(jnp.int32, (RANK, RANK), 1)
    skeleton_points, sizes = [], []
    for n in range(4):
        for at_x in range(4):
            for at_y in range(4):
                span = pl.ds(at_x * 64 + at_y * 16, 16)
                for kind, target in enumerate((work, chosen)):
                    planes = pl.ds(2 * n, 2)
                    target[n, span, 0:128] = full_a[kind, at_x, at_y, planes].reshape(16, 128)
                    target[n, span, 128:256] = full_b[kind, at_y, at_x, planes].reshape(16, 128)
        skeleton_points.append(
            jnp.concatenate([work[n, 128:136, 0:128], work[n, 136:144, 0:128]], axis=1)
        )
        gram = work[n]
        on_diagonal = jnp.where(row == col, gram, 0.0)
        trace = jnp.sum(jnp.sum(on_diagonal, axis=0, keepdims=True), axis=1, keepdims=True)
        work[n] = gram * (1.0 / trace) + jnp.where(row == col, 0.01, 0.0)
        sizes.append(lax.rsqrt(trace))

    middles = []
    for k in range(2):
        row_side = features(skeleton_points[2 * k], 4.0, True).T.astype(BF16)
        col_side = features(skeleton_points[2 * k + 1], 1.0, False).astype(BF16)
        kernel_skel = jnp.exp(jnp.dot(row_side, col_side, preferred_element_type=F32))
        right = jnp.dot(kernel_skel, chosen[2 * k + 1], precision=HIGH, preferred_element_type=F32)
        middles.append(
            lax.dot_general(
                chosen[2 * k], right, (((0,), (0,)), ((), ())),
                precision=HIGH, preferred_element_type=F32,
            )
        )

    lane8 = lax.broadcasted_iota(jnp.int32, (8, 128), 1)
    row8 = lax.broadcasted_iota(jnp.int32, (8, 128), 0)
    group8 = (lane8 // 32) * 32
    lane = lax.broadcasted_iota(jnp.int32, (32, 128), 1)
    for p in range(8):
        top = 32 * p
        aligned = (top // 128) * 128
        packed = jnp.zeros((32, 128), F32)
        for n in range(4):
            block = work[n, top : top + 32, aligned : aligned + 128]
            turn = (32 * n - (top - aligned)) % 128
            if turn:
                block = pltpu.roll(block, turn, 1)
            packed = jnp.where(lane // 32 == n, block, packed)
        left = [packed[8 * g : 8 * g + 8] for g in range(4)]
        inverse = [jnp.where(lane8 - group8 == row8 + 8 * g, 1.0, 0.0) for g in range(4)]
        for j in range(0, 32, 4):
            own, inner = j // 8, j % 8
            spread = {
                g: [
                    jnp.take_along_axis(left[g], group8 + (j + t), axis=1, mode="promise_in_bounds")
                    for t in range(4)
                ]
                for g in range(own, 4)
            }

            def line(tile, t, inner=inner):
                return jnp.broadcast_to(tile[inner + t : inner + t + 1, :], (8, 128))

            solve = pivots(lambda t, u: line(spread[own][u], t))
            left_rows = solve([line(left[own], t) for t in range(4)])
            inverse_rows = solve([line(inverse[own], t) for t in range(4)])
            for g in range(own, 4):
                if g == own and inner == 4:
                    continue
                factors = solve(spread[g])
                if g == own:
                    factors = [jnp.where(row8 > 3, factor, 0.0) for factor in factors]
                left[g] = left[g] - fold(factors, left_rows)
                inverse[g] = inverse[g] - fold(factors, inverse_rows)
            for t in range(4):
                inverse[own] = jnp.where(row8 == inner + t, inverse_rows[t], inverse[own])
        packed = jnp.concatenate(inverse, axis=0)
        diagonal = jnp.concatenate([jnp.where(lane // 32 == n, packed, 0.0) for n in range(4)], axis=0)
        stacked = jnp.concatenate([work[n, top : top + 32, :] for n in range(4)], axis=0)
        srow = lax.broadcasted_iota(jnp.int32, (128, RANK), 0)
        scol = lax.broadcasted_iota(jnp.int32, (128, RANK), 1)
        identity = jnp.where(srow % 32 == scol % 32, 1.0, 0.0)
        stacked = jnp.where(scol // 32 == p, identity, stacked)
        solved = jnp.dot(diagonal, stacked, precision=HIGHEST, preferred_element_type=F32)
        done = jnp.where(scol < top + 32, solved, 0.0)
        for n in range(4):
            work[n, top : top + 32, :] = done[32 * n : 32 * n + 32]
        rest = RANK - top - 32
        if rest:
            turned = solved.T[top + 32 :, :]
            tlane = lax.broadcasted_iota(jnp.int32, (rest, 128), 1)
            tcol = lax.broadcasted_iota(jnp.int32, (rest, RANK), 1)
            for n in range(4):
                update = jnp.dot(
                    jnp.where(tlane // 32 == n, turned, 0.0), solved,
                    precision=HIGHEST, preferred_element_type=F32,
                )
                work[n, top + 32 :, :] = jnp.where(tcol // 32 == p, 0.0, work[n, top + 32 :, :]) - update

    last = (((1,), (1,)), ((), ()))
    size = sum(jnp.where(node == n, sizes[n], 0.0) for n in range(4))
    basis[...] = (128.0 * size) * lax.dot_general(
        samples[...], work[node], last, precision=HIGH, preferred_element_type=F32
    )
    for k in range(2):
        half = jnp.dot(work[2 * k], middles[k], precision=HIGH, preferred_element_type=F32)
        coupling[k] = ((16384.0 / math.sqrt(RANK)) * sizes[2 * k] * sizes[2 * k + 1]) * lax.dot_general(
            half, work[2 * k + 1], last, precision=HIGH, preferred_element_type=F32
        )


def finish(full_a, full_b, samples):
    return pl.pallas_call(
        finish_kernel,
        out_shape=(
            jax.ShapeDtypeStruct((ROWS, RANK), F32),
            jax.ShapeDtypeStruct((2, RANK, RANK), F32),
        ),
        in_specs=[VMEM] * 3,
        out_specs=(VMEM,) * 2,
        scratch_shapes=[pltpu.VMEM((4, RANK, RANK), F32), pltpu.VMEM((4, RANK, RANK), F32)],
        compiler_params=pltpu.CompilerParams(vmem_limit_bytes=32 << 20),
        name="finish",
    )(full_a, full_b, samples)


def body(points, omega, tree_order, sibling_blocks, cousin_blocks, skeleton):
    blocks, row_points, picks, tree_points = gather(
        points, omega, tree_order.reshape(1, ROWS), sibling_blocks, cousin_blocks
    )
    parts = sample(blocks, row_points, picks)
    samples, full_a, full_b = collect(parts, skeleton, tree_points)
    return finish(full_a, full_b, samples)


def solution(mesh):
    return jax.shard_map(
        body,
        mesh=mesh,
        in_specs=(
            P(None, ("leaf", "sub")),
            P(None, ("leaf", "sub")),
            P(("leaf", "sub")),
            P("leaf", None),
            P("leaf", None),
            P(),
        ),
        out_specs=(P(("leaf", "sub"), None), P()),
        check_vma=False,
    )
```

```python
import functools
import math

import jax
import jax.numpy as jnp
from jax import lax
from jax.experimental import pallas as pl
from jax.experimental.pallas import tpu as pltpu
from jax.sharding import PartitionSpec as P

MESH = pl.DeviceIdType.MESH
HIGH = lax.Precision.HIGH
HIGHEST = lax.Precision.HIGHEST
F32 = jnp.float32
BF16 = jnp.bfloat16
VMEM = pl.BlockSpec(memory_space=pltpu.VMEM)
SMEM = pl.BlockSpec(memory_space=pltpu.SMEM)
HBM = pl.BlockSpec(memory_space=pltpu.HBM)

ROWS = 256
FEATS = 8
SAMPLES = 128
RANK = 256
SPAN = 288
LINK = BF16


def place():
    leaf = lax.axis_index("leaf")
    core = lax.axis_index("sub")
    return leaf % 4, (leaf // 4) % 4, leaf // 16, core


def device(x, y, z, core):
    return (z * 16 + y * 4 + x, core)


def greet(partners):
    barrier = pltpu.get_barrier_semaphore()
    for partner in partners:
        pl.semaphore_signal(barrier, inc=1, device_id=partner, device_id_type=MESH)
    pl.semaphore_wait(barrier, len(partners))


def send(src, dst, send_sem, recv_sem, target):
    copy = pltpu.make_async_remote_copy(
        src_ref=src,
        dst_ref=dst,
        send_sem=send_sem,
        recv_sem=recv_sem,
        device_id=target,
        device_id_type=MESH,
    )
    copy.start()
    return copy


def features(coordinates, scale, ones_first):
    norm = -2.0 * jnp.sum(coordinates * coordinates, axis=0, keepdims=True)
    first = norm.astype(BF16).astype(F32)
    second = (norm - first).astype(BF16).astype(F32)
    third = norm - first - second
    row = lax.broadcasted_iota(jnp.int32, coordinates.shape, 0)
    start = 3 if ones_first else 0
    other = 0 if ones_first else 3
    tail = jnp.where((row >= other) & (row < other + 3), 1.0, 0.0)
    tail = jnp.where(row == start, first, tail)
    tail = jnp.where(row == start + 1, second, tail)
    tail = jnp.where(row == start + 2, third, tail)
    return jnp.concatenate([scale * coordinates, tail], axis=0)


def plane_kind(dz):
    return jnp.where((dz == 2) | (dz == 4) | (dz == 5), 0, 1)


def pick_slots(lists, x, y, z):
    lane = lax.broadcasted_iota(jnp.int32, (8, 128), 1)
    kind = lax.broadcasted_iota(jnp.int32, (8, 128), 0) // 4
    along, dz = lane // 8, lane % 8
    plane = ((z + dz) % 8) * 16
    block = jnp.where(
        kind == 0, plane + ((y + along) % 4) * 4 + x, plane + y * 4 + (x + along) % 4
    )
    named = jnp.where((lane < 32) & (plane_kind(dz) == kind), block, -1).astype(F32)
    hit = jnp.zeros((8, 128), F32)
    for side, length in ((0, 16), (1, 32)):
        entries = jnp.concatenate(
            [lists[k, at, side : side + 1, :] for k in range(2) for at in range(4)], axis=0
        ).astype(F32)
        for e in range(length):
            hit = jnp.where(named == jnp.broadcast_to(entries[:, e : e + 1], (8, 128)), 1.0, hit)
    place_of = lane.astype(F32)
    count = jnp.zeros((8, 128), F32)
    found = jnp.zeros((8, 128), F32)
    for slot in range(32):
        if slot % 8:
            here = jnp.broadcast_to(hit[:, slot : slot + 1], (8, 128))
            found = jnp.where((place_of == count) & (here > 0.5), float(slot), found)
            count = count + here
    return jnp.where(lane == 127, count, found).astype(jnp.int32)


def gather_kernel(
    points_in, omega_in, order_in, siblings_in, cousins_in,
    blocks, row_points, picks, tree_points,
    points, omega, order, siblings, cousins, load_sems, own, own_rows, own_lists, lists,
    z_send, z_recv, out_send, out_recv, far_send, far_recv,
    rows_send, rows_recv, list_send, list_recv,
):
    loads = [
        pltpu.make_async_copy(source, target, load_sems.at[k])
        for k, (source, target) in enumerate(
            [
                (omega_in, omega),
                (points_in, points),
                (order_in, order),
                (siblings_in, siblings),
                (cousins_in, cousins),
            ]
        )
    ]
    for copy in loads:
        copy.start()
    x, y, z, core = place()
    mate = 7 - 6 * (z % 2)
    upward, downward = device(x, y, (z + 1) % 8, core), device(x, y, (z + 7) % 8, core)
    plus = [device(x, (y + 1) % 4, z, core), device((x + 1) % 4, y, z, core)]
    minus = [device(x, (y + 3) % 4, z, core), device((x + 3) % 4, y, z, core)]
    along_x = [(d, c, device((x + d) % 4, y, z, (core + c) % 2)) for d in range(4) for c in range(2) if d or c]
    along_y = [(d, c, device(x, (y + d) % 4, z, (core + c) % 2)) for d in range(4) for c in range(2) if d or c]
    greet([upward, downward] + [who for _, _, who in along_x] + [who for _, _, who in along_y[1:]])

    loads[0].wait()
    own[0:ROWS, :] = omega[...].astype(F32).T.astype(BF16)
    loads[1].wait()
    columns = features(points[...].astype(F32), 1.0, False).astype(BF16)
    own[256:272, :] = columns[:, :128]
    own[272:288, :] = columns[:, 128:]
    halves = (pl.ds(0, SPAN // 2), pl.ds(SPAN // 2, SPAN // 2))

    hops = {}

    def hop(source, source_dz, dz, half, who):
        ref = source if source_dz is None else source.at[source_dz]
        hops[dz, half] = send(
            ref.at[halves[half]], blocks.at[dz, halves[half]],
            z_send.at[dz, half], z_recv.at[dz, half], who,
        )

    for step in range(2):
        hop(own, None, 7, step, upward)
        hop(own, None, 1, 1 - step, downward)

    for copy in loads[2:]:
        copy.wait()
    local = order[...] % ROWS
    lane = lax.broadcasted_iota(jnp.int32, (ROWS, ROWS), 0)
    pick = jnp.where(lane == local, 1.0, 0.0).astype(BF16)
    mine = jnp.dot(points[...], pick, preferred_element_type=F32)
    tree_points[...] = mine
    own_rows[...] = features(mine, 4.0, True).astype(BF16)
    own_lists[...] = jnp.zeros_like(own_lists)
    own_lists[0:1, 0:16] = siblings[...]
    own_lists[1:2, 0:32] = cousins[...]
    small = []
    for kind, (at, partners) in enumerate(((x, along_x), (y, along_y))):
        row_points[kind, at * 2 + core] = own_rows[...]
        lists[kind, at] = own_lists[...]
        for k, (d, c, who) in enumerate(partners):
            target = row_points.at[kind, at * 2 + core]
            small.append(send(own_rows, target, rows_send.at[kind, k], rows_recv.at[kind, k], who))
            if not c:
                target = lists.at[kind, at]
                small.append(send(own_lists, target, list_send.at[kind, d], list_recv.at[kind, d], who))

    outs, fars = {}, []

    def fan_out(k, kind, dz, half):
        block = blocks.at[dz, halves[half]]
        for side, (at, who) in enumerate(((24, plus[kind]), (8, minus[kind]))):
            outs[k, side, half] = send(
                block, blocks.at[at + dz, halves[half]],
                out_send.at[k, side, half], out_recv.at[k, side, half], who,
            )

    def relay(k, kind, dz):
        for side, (at, who) in enumerate(((24, plus[kind]), (8, minus[kind]))):
            outs[k, side, side].wait_recv()
            fars.append(
                send(
                    blocks.at[at + dz, halves[side]], blocks.at[16 + dz, halves[side]],
                    far_send.at[k, side], far_recv.at[k, side], who,
                )
            )

    for step in range(2):
        hops[7, step].wait_recv()
        hop(blocks, 7, 6, step, upward)
        hops[1, 1 - step].wait_recv()
        hop(blocks, 1, 2, 1 - step, downward)
    for half in range(2):
        fan_out(0, 1, mate, half)
    for step in range(2):
        hops[6, step].wait_recv()
        hop(blocks, 6, 5, step, upward)
        fan_out(1, 1, 6, step)
        hops[2, 1 - step].wait_recv()
        hop(blocks, 2, 3, 1 - step, downward)
        fan_out(2, 0, 2, 1 - step)
    relay(0, 1, mate)
    hops[5, 0].wait_recv()
    hop(blocks, 5, 4, 0, upward)
    fan_out(3, 0, 5, 0)
    hops[3, 1].wait_recv()
    hop(blocks, 3, 4, 1, downward)
    fan_out(4, 1, 3, 1)
    hops[5, 1].wait_recv()
    fan_out(3, 0, 5, 1)
    hops[3, 0].wait_recv()
    fan_out(4, 1, 3, 0)
    relay(1, 1, 6)
    relay(2, 0, 2)
    for half in range(2):
        hops[4, half].wait_recv()
        fan_out(5, 0, 4, half)
    relay(3, 0, 5)
    relay(4, 1, 3)
    relay(5, 0, 4)
    for k in range(6):
        for side in range(2):
            outs[k, side, 1 - side].wait_recv()
    for copy in small:
        copy.wait()
    picks[...] = pick_slots(lists, x, y, z)
    for copy in fars:
        copy.wait()
    for copy in list(hops.values()) + list(outs.values()):
        copy.wait_send()


def gather(points, omega, order, siblings, cousins):
    dma = pltpu.SemaphoreType.DMA
    return pl.pallas_call(
        gather_kernel,
        out_shape=(
            jax.ShapeDtypeStruct((32, SPAN, 128), BF16),
            jax.ShapeDtypeStruct((2, 8, 16, ROWS), BF16),
            jax.ShapeDtypeStruct((8, 128), jnp.int32),
            jax.ShapeDtypeStruct((FEATS, ROWS), F32),
        ),
        in_specs=[HBM] * 5,
        out_specs=(VMEM,) * 4,
        scratch_shapes=[
            pltpu.VMEM((FEATS, ROWS), BF16),
            pltpu.VMEM((SAMPLES, ROWS), BF16),
            pltpu.VMEM((1, ROWS), jnp.int32),
            pltpu.VMEM((1, 16), jnp.int32),
            pltpu.VMEM((1, 32), jnp.int32),
            dma((5,)),
            pltpu.VMEM((SPAN, 128), BF16),
            pltpu.VMEM((16, ROWS), BF16),
            pltpu.VMEM((8, 128), jnp.int32),
            pltpu.VMEM((2, 4, 8, 128), jnp.int32),
            dma((8, 2)), dma((8, 2)), dma((6, 2, 2)), dma((6, 2, 2)), dma((6, 2)), dma((6, 2)),
            dma((2, 7)), dma((2, 7)), dma((2, 4)), dma((2, 4)),
        ],
        compiler_params=pltpu.CompilerParams(
            collective_id=0, has_side_effects=True, vmem_limit_bytes=32 << 20
        ),
        name="gather",
    )(points, omega, order, siblings, cousins)


def sample_kernel(blocks, row_points, picks, out, rows, even_tile, odd_tile, items):
    _, _, z, _ = place()

    total = 0
    for row in range(8):
        count = picks[row, 127]

        def note(step, at, row=row, count=count):
            items[at, 0] = row
            items[at, 1] = picks[row, 2 * step]
            paired = 2 * step + 1 < count
            items[at, 2] = jnp.where(paired, picks[row, 2 * step + 1], picks[row, 2 * step])
            items[at, 3] = jnp.where(paired, 2, 1)
            return at + 1

        total = lax.fori_loop(0, (count + 1) // 2, note, total)
    for extra in range(2):
        items[total + extra, 0] = 0
        items[total + extra, 1] = jnp.where(total > 0, items[0, 1], 6)
        items[total + extra, 2] = items[total + extra, 1]
        items[total + extra, 3] = 0

    out[...] = jnp.zeros_like(out)
    for row in range(8):
        for half in range(2):
            rows[row, half * ROWS : (half + 1) * ROWS, :] = (
                row_points[row // 4, 2 * (row % 4) + half].astype(F32).T.astype(BF16)
            )

    def kernel_tile(item, tile):
        columns = jnp.concatenate(
            [blocks[items[item, k], at : at + 16, :] for k in (1, 2) for at in (256, 272)], axis=1
        )
        exponent = jnp.dot(rows[items[item, 0]], columns, preferred_element_type=F32)
        tile[...] = jnp.exp(exponent).astype(BF16)

    def add(item, tile):
        weights = []
        for k in (1, 2):
            slot = items[item, k]
            sibling = ((z + slot % 8) % 8) // 4 == z // 4
            use = items[item, 3] >= k
            values = blocks[slot, 0:ROWS, :]
            near = jnp.where(use & sibling, 1.0, 0.0).astype(BF16)
            far = jnp.where(use & jnp.logical_not(sibling), 1.0, 0.0).astype(BF16)
            weights.append(jnp.concatenate([values * near, values * far], axis=1))
        terms = jnp.dot(tile[...], jnp.concatenate(weights, axis=0), preferred_element_type=F32)
        kind, at = items[item, 0] // 4, items[item, 0] % 4
        out[0, kind, at] += terms[0:ROWS]
        out[1, kind, at] += terms[ROWS:]

    kernel_tile(0, even_tile)

    def two_items(step, carry):
        kernel_tile(2 * step + 1, odd_tile)
        add(2 * step, even_tile)
        kernel_tile(2 * step + 2, even_tile)
        add(2 * step + 1, odd_tile)
        return carry

    lax.fori_loop(0, (total + 1) // 2, two_items, 0)


def sample(blocks, row_points, picks):
    return pl.pallas_call(
        sample_kernel,
        out_shape=jax.ShapeDtypeStruct((2, 2, 4, ROWS, RANK), F32),
        in_specs=[VMEM, VMEM, SMEM],
        out_specs=VMEM,
        scratch_shapes=[
            pltpu.VMEM((8, 2 * ROWS, 16), BF16),
            pltpu.VMEM((2 * ROWS, 2 * ROWS), BF16),
            pltpu.VMEM((2 * ROWS, 2 * ROWS), BF16),
            pltpu.SMEM((64, 4), jnp.int32),
        ],
        compiler_params=pltpu.CompilerParams(vmem_limit_bytes=32 << 20),
        name="sample",
    )(blocks, row_points, picks)


def collect_kernel(
    parts, skeleton, tree_points,
    samples, full_a, full_b,
    other_core, relay_out, relay_in, near_out, near_in, table, other_table, piece, pieces,
    core_send, core_recv, relay_sems, near_sems, table_sems, piece_send, piece_recv,
    z_send, z_recv, y_sems, x_sems,
):
    x, y, z, core = place()
    leaf = z * 16 + y * 4 + x
    node = z // 2
    other = device(x, y, z, 1 - core)
    mates = []
    for dz in range(2):
        for dy in range(4):
            for dx in range(4):
                if dz or dy or dx:
                    where = ((x + dx) % 4, (y + dy) % 4, node * 2 + (z + dz) % 2)
                    mates.append((dz * 16 + dy * 4 + dx, where, device(*where, core)))
    pair = z // 4
    column = [device(x, y, (z + dz) % 8, pair) for dz in range(8)]
    strangers = [
        device(x, y, ((node + dn) % 4) * 2 + dz, c) for dn in range(1, 4) for dz in range(2) for c in range(2)
    ]
    strangers.append(device(x, y, node * 2 + (z + 1) % 2, 1 - core))
    greet([other] + [who for _, _, who in mates] + strangers)
    right, left = device((x + 1) % 4, y, z, core), device((x + 3) % 4, y, z, core)
    above, below = device(x, (y + 1) % 4, z, core), device(x, (y + 3) % 4, z, core)

    ahead, behind, across = (x + 1) % 4, (x + 3) % 4, (x + 2) % 4
    next_y, last_y = (y + 1) % 4, (y + 3) % 4
    order = [(across, (y + 2) % 4), (ahead, next_y), (behind, last_y), (x, y)]
    swap = {}
    for step, places in enumerate(order):
        for kind in range(2):
            at = places[kind]
            swap[step, kind] = send(
                parts.at[1 - core, kind, at], other_core.at[kind, at],
                core_send.at[kind, step], core_recv.at[kind, step], other,
            )

    def partial(step, kind):
        swap[step, kind].wait_recv()
        at = order[step][kind]
        return parts[core, kind, at] + other_core[kind, at]

    plus, minus = (right, above), (left, below)
    lower, upper = pl.ds(0, 128), pl.ds(128, 128)
    relays, nears = [], []
    for kind in range(2):
        relay_out[kind] = partial(0, kind).astype(LINK)
        for side, (rows_of, who) in enumerate(((lower, plus[kind]), (upper, minus[kind]))):
            relays.append(
                send(
                    relay_out.at[kind, rows_of], relay_in.at[kind, side],
                    relay_sems.at[0, kind, side], relay_sems.at[1, kind, side], who,
                )
            )

    def pass_on(kind, side, first, rows_of, who):
        ref = near_out.at[kind, side, rows_of]
        landing = near_in.at[kind, side, rows_of]
        nears.append(send(ref, landing, near_sems.at[0, kind, side, first], near_sems.at[1, kind, side, first], who))

    waiting = {}
    for kind in range(2):
        to_plus, to_minus = partial(1, kind), partial(2, kind)
        near_out[kind, 0, 128:256, :] = to_plus[128:256].astype(LINK)
        near_out[kind, 1, 0:128, :] = to_minus[0:128].astype(LINK)
        pass_on(kind, 0, 0, upper, plus[kind])
        pass_on(kind, 1, 0, lower, minus[kind])
        waiting[kind] = (to_plus[0:128], to_minus[128:256])
    for kind in range(2):
        relays[2 * kind].wait_recv()
        near_out[kind, 0, 0:128, :] = (waiting[kind][0] + relay_in[kind, 0].astype(F32)).astype(LINK)
        pass_on(kind, 0, 1, lower, plus[kind])
        relays[2 * kind + 1].wait_recv()
        near_out[kind, 1, 128:256, :] = (waiting[kind][1] + relay_in[kind, 1].astype(F32)).astype(LINK)
        pass_on(kind, 1, 1, upper, minus[kind])
    mine = partial(3, 0) + partial(3, 1)
    first_row = (leaf * 2 + core) * ROWS
    row = lax.broadcasted_iota(jnp.int32, (ROWS, RANK), 0) + first_row
    chosen = jnp.where(row == skeleton[pl.ds(node, 1), :], 1.0, 0.0)
    skeleton_points = jnp.dot(
        tree_points[...].astype(BF16), chosen.astype(BF16), preferred_element_type=F32
    )
    for copy in nears:
        copy.wait_recv()
    for kind in range(2):
        for side in range(2):
            mine = mine + near_in[kind, side].astype(F32)
    rows = mine
    samples[...] = rows

    table[0:256, :] = lax.dot_general(
        rows, rows, (((0,), (0,)), ((), ())), precision=HIGHEST, preferred_element_type=F32
    )
    table[128:256, 0:128] = jnp.zeros((128, 128), F32)
    table[128:136, 0:128] = skeleton_points[:, 0:128]
    table[136:144, 0:128] = skeleton_points[:, 128:256]
    table[256:512, :] = lax.dot_general(
        chosen, rows, (((0,), (0,)), ((), ())), precision=HIGHEST, preferred_element_type=F32
    )
    start = pl.multiple_of((1 - core) * 256, 256)
    swap_table = send(
        table.at[pl.ds(start, 256)], other_table, table_sems.at[0], table_sems.at[1], other
    )
    swap_table.wait()
    keep = pl.multiple_of(core * 256, 256)
    other_table[...] += table[pl.ds(keep, 256), :]

    def chunk(where):
        first = (where[0] * 8 + where[1] * 2 + where[2] % 2) * 8
        return other_table.at[pl.ds(pl.multiple_of(first, 8), 8)]

    spreads = []
    for slot, where, who in mates:
        spreads.append(
            send(chunk(where), pieces.at[slot], piece_send.at[slot], piece_recv.at[slot], who)
        )
    sums = chunk((x, y, z))[...]
    for copy in spreads:
        copy.wait_recv()
    for slot, _, _ in mates:
        sums = sums + pieces[slot]
    piece[0] = sums[:, 0:128]
    piece[1] = sums[:, 128:256]
    for copy in spreads:
        copy.wait_send()

    home_a, home_b = full_a.at[x, y, z % 4, core], full_b.at[y, x, z % 4, core]

    def drop(dz, half):
        return pltpu.make_async_remote_copy(
            src_ref=piece.at[half],
            dst_ref=(home_a, home_b)[half],
            send_sem=z_send.at[dz, half],
            recv_sem=z_recv.at[z % 4, core, half],
            device_id=column[dz],
            device_id_type=MESH,
        )

    def arrival(plane, c, half):
        landing = (full_a.at[x, y, plane, c], full_b.at[y, x, plane, c])[half]
        return pltpu.make_async_remote_copy(
            src_ref=piece.at[half],
            dst_ref=landing,
            send_sem=z_send.at[0, half],
            recv_sem=z_recv.at[plane, c, half],
            device_id=other,
            device_id_type=MESH,
        )

    for dz in (4, 3, 5, 2, 6, 1, 7):
        for half in range(2):
            drop(dz, half).start()

    @pl.when(pair == core)
    def _():
        home_a[...] = piece[0]
        home_b[...] = piece[1]

    @pl.when(pair != core)
    def _():
        for half in range(2):
            drop(0, half).start()

    for plane in range(4):
        for c in range(2):

            @pl.when((core * 4 + plane != z) | (core != c))
            def _(plane=plane, c=c):
                for half in range(2):
                    arrival(plane, c, half).wait_recv()

    cuts = (pl.ds(0, 2), pl.ds(2, 2))

    def push(ref, sems, k, who):
        return send(ref, ref, sems.at[2 * k], sems.at[2 * k + 1], who)

    def ring(at, sems, first_k, forward, backward):
        return [
            push(at.at[cuts[0]], sems, first_k, forward),
            push(at.at[cuts[1]], sems, first_k + 1, backward),
            push(at.at[cuts[1]], sems, first_k + 2, forward),
            push(at.at[cuts[0]], sems, first_k + 3, backward),
        ]

    def pass_along(copies, sems, first_k, before, after, forward, backward):
        copies[0].wait_recv()
        copies.append(push(before.at[cuts[0]], sems, first_k + 4, forward))
        copies[1].wait_recv()
        copies.append(push(after.at[cuts[1]], sems, first_k + 5, backward))

    first = ring(full_a.at[x, y], y_sems, 0, above, below)
    second = ring(full_b.at[y, x], x_sems, 0, right, left)
    pass_along(first, y_sems, 0, full_a.at[x, last_y], full_a.at[x, next_y], above, below)
    pass_along(second, x_sems, 0, full_b.at[y, behind], full_b.at[y, ahead], right, left)
    for copy in first[2:6]:
        copy.wait_recv()
    third = ring(full_a.at[x], x_sems, 6, right, left)
    for copy in second[2:6]:
        copy.wait_recv()
    fourth = ring(full_b.at[y], y_sems, 6, above, below)
    pass_along(third, x_sems, 6, full_a.at[behind], full_a.at[ahead], right, left)
    pass_along(fourth, y_sems, 6, full_b.at[last_y], full_b.at[next_y], above, below)
    for copy in third[2:] + fourth[2:]:
        copy.wait_recv()
    for copy in first + second + third + fourth:
        copy.wait_send()
    for dz in range(1, 8):
        for half in range(2):
            drop(dz, half).wait_send()

    @pl.when(pair != core)
    def _():
        for half in range(2):
            drop(0, half).wait_send()

    for copy in relays + nears + list(swap.values()):
        copy.wait_send()


def collect(parts, skeleton, tree_points):
    dma = pltpu.SemaphoreType.DMA
    return pl.pallas_call(
        collect_kernel,
        out_shape=(
            jax.ShapeDtypeStruct((ROWS, RANK), F32),
            jax.ShapeDtypeStruct((4, 4, 4, 2, 8, 128), F32),
            jax.ShapeDtypeStruct((4, 4, 4, 2, 8, 128), F32),
        ),
        in_specs=[VMEM] * 3,
        out_specs=(VMEM,) * 3,
        scratch_shapes=[
            pltpu.VMEM((2, 4, ROWS, RANK), F32),
            pltpu.VMEM((2, ROWS, RANK), LINK),
            pltpu.VMEM((2, 2, 128, RANK), LINK),
            pltpu.VMEM((2, 2, ROWS, RANK), LINK),
            pltpu.VMEM((2, 2, ROWS, RANK), LINK),
            pltpu.VMEM((512, RANK), F32),
            pltpu.VMEM((256, RANK), F32),
            pltpu.VMEM((2, 8, 128), F32),
            pltpu.VMEM((32, 8, RANK), F32),
            dma((2, 4)), dma((2, 4)), dma((2, 2, 2)), dma((2, 2, 2, 2)), dma((2,)), dma((32,)), dma((32,)),
            dma((8, 2)), dma((4, 2, 2)), dma((24,)), dma((24,)),
        ],
        compiler_params=pltpu.CompilerParams(
            collective_id=1, has_side_effects=True, vmem_limit_bytes=32 << 20
        ),
        name="collect",
    )(parts, skeleton, tree_points)


def fold(factors, lines):
    a, b, c, d = (factor * values for factor, values in zip(factors, lines, strict=True))
    return (a + b) + (c + d)


def pivots(entry):
    def pair(a, b, c):
        scale = lax.rsqrt(a)
        return scale, b * scale, a * lax.rsqrt(a * (a * c - b * b))

    r0, l10, r1 = pair(entry(0, 0), entry(1, 0), entry(1, 1))
    l20, l30 = entry(2, 0) * r0, entry(3, 0) * r0
    l21, l31 = (entry(2, 1) - l20 * l10) * r1, (entry(3, 1) - l30 * l10) * r1
    r2, l32, r3 = pair(
        entry(2, 2) - (l20 * l20 + l21 * l21),
        entry(3, 2) - (l30 * l20 + l31 * l21),
        entry(3, 3) - (l30 * l30 + l31 * l31),
    )

    def solve(values):
        v0 = values[0] * r0
        v1 = (values[1] - v0 * l10) * r1
        v2 = (values[2] - (v0 * l20 + v1 * l21)) * r2
        v3 = ((values[3] - (v0 * l30 + v1 * l31)) - v2 * l32) * r3
        return [v0, v1, v2, v3]

    return solve


def finish_kernel(
    full_a, full_b, samples, basis, coupling, work, chosen, factor_out, factor_in, factor_sems, coupling_sems
):
    x, y, z, core = place()
    other = device(x, y, z, 1 - core)
    greet([other])
    node = z // 2
    row = lax.broadcasted_iota(jnp.int32, (RANK, RANK), 0)
    col = lax.broadcasted_iota(jnp.int32, (RANK, RANK), 1)
    skeleton_points, sizes = [], []
    for n in range(2):
        for at_x in range(4):
            for at_y in range(4):
                span = pl.ds(at_x * 64 + at_y * 16, 16)
                planes = pl.ds(2 * n, 2)
                for kind, target in enumerate((work, chosen)):
                    target[n, span, 0:128] = full_a[at_x, at_y, planes, kind].reshape(16, 128)
                    target[n, span, 128:256] = full_b[at_y, at_x, planes, kind].reshape(16, 128)
        skeleton_points.append(
            jnp.concatenate([work[n, 128:136, 0:128], work[n, 136:144, 0:128]], axis=1)
        )
        gram = work[n]
        on_diagonal = jnp.where(row == col, gram, 0.0)
        trace = jnp.sum(jnp.sum(on_diagonal, axis=0, keepdims=True), axis=1, keepdims=True)
        work[n] = gram * (1.0 / trace) + jnp.where(row == col, 0.01, 0.0)
        sizes.append(lax.rsqrt(trace))

    row_side = features(skeleton_points[0], 4.0, True).T.astype(BF16)
    col_side = features(skeleton_points[1], 1.0, False).astype(BF16)
    kernel_skel = jnp.exp(jnp.dot(row_side, col_side, preferred_element_type=F32))
    right = jnp.dot(kernel_skel, chosen[1], precision=HIGH, preferred_element_type=F32)
    middle = lax.dot_general(
        chosen[0], right, (((0,), (0,)), ((), ())), precision=HIGH, preferred_element_type=F32
    )

    lane8 = lax.broadcasted_iota(jnp.int32, (8, 128), 1)
    row8 = lax.broadcasted_iota(jnp.int32, (8, 128), 0)
    group8 = (lane8 // 64) * 64
    lane = lax.broadcasted_iota(jnp.int32, (64, 128), 1)
    for p in range(4):
        top = 64 * p
        aligned = (top // 128) * 128
        packed = []
        for n in range(2):
            block = work[n, top : top + 64, aligned : aligned + 128]
            packed.append(pltpu.roll(block, 64, 1) if (64 * n - top) % 128 else block)
        packed = jnp.where(lane < 64, packed[0], packed[1])
        left = [packed[8 * g : 8 * g + 8] for g in range(8)]
        inverse = [jnp.where(lane8 - group8 == row8 + 8 * g, 1.0, 0.0) for g in range(8)]
        for j in range(0, 64, 4):
            own, inner = j // 8, j % 8
            spread = {
                g: [
                    jnp.take_along_axis(left[g], group8 + (j + t), axis=1, mode="promise_in_bounds")
                    for t in range(4)
                ]
                for g in range(own, 8)
            }

            def line(tile, t, inner=inner):
                return jnp.broadcast_to(tile[inner + t : inner + t + 1, :], (8, 128))

            solve = pivots(lambda t, u: line(spread[own][u], t))
            left_rows = solve([line(left[own], t) for t in range(4)])
            inverse_rows = solve([line(inverse[own], t) for t in range(4)])
            for g in range(own, 8):
                if g == own and inner == 4:
                    continue
                factors = solve(spread[g])
                if g == own:
                    factors = [jnp.where(row8 > 3, factor, 0.0) for factor in factors]
                left[g] = left[g] - fold(factors, left_rows)
                inverse[g] = inverse[g] - fold(factors, inverse_rows)
            for t in range(4):
                inverse[own] = jnp.where(row8 == inner + t, inverse_rows[t], inverse[own])
        packed = jnp.concatenate(inverse, axis=0)
        diagonal = jnp.concatenate([jnp.where(lane < 64, packed, 0.0), jnp.where(lane < 64, 0.0, packed)], axis=0)
        stacked = jnp.concatenate([work[n, top : top + 64, :] for n in range(2)], axis=0)
        srow = lax.broadcasted_iota(jnp.int32, (128, RANK), 0)
        scol = lax.broadcasted_iota(jnp.int32, (128, RANK), 1)
        identity = jnp.where(srow % 64 == scol % 64, 1.0, 0.0)
        stacked = jnp.where(scol // 64 == p, identity, stacked)
        solved = jnp.dot(diagonal, stacked, precision=HIGH, preferred_element_type=F32)
        done = jnp.where(scol < top + 64, solved, 0.0)
        for n in range(2):
            work[n, top : top + 64, :] = done[64 * n : 64 * n + 64]
        rest = RANK - top - 64
        if rest:
            turned = solved.T[top + 64 :, :]
            tlane = lax.broadcasted_iota(jnp.int32, (rest, 128), 1)
            tcol = lax.broadcasted_iota(jnp.int32, (rest, RANK), 1)
            for n in range(2):
                update = jnp.dot(
                    jnp.where(tlane // 64 == n, turned, 0.0), solved,
                    precision=HIGH, preferred_element_type=F32,
                )
                work[n, top + 64 :, :] = jnp.where(tcol // 64 == p, 0.0, work[n, top + 64 :, :]) - update

    size = jnp.where(node % 2 == 0, sizes[0], sizes[1])
    factor_out[...] = work[node % 2] * size
    factor_copy = send(factor_out, factor_in, factor_sems.at[0], factor_sems.at[1], other)
    last = (((1,), (1,)), ((), ()))
    half = jnp.dot(work[0], middle, precision=HIGH, preferred_element_type=F32)
    coupling[core] = ((16384.0 / math.sqrt(RANK)) * sizes[0] * sizes[1]) * lax.dot_general(
        half, work[1], last, precision=HIGH, preferred_element_type=F32
    )
    coupling_copy = send(
        coupling.at[core], coupling.at[core], coupling_sems.at[0], coupling_sems.at[1], other
    )
    factor_copy.wait_recv()
    factor = jnp.where(node // 2 == core, factor_out[...], factor_in[...])
    basis[...] = 128.0 * lax.dot_general(
        samples[...], factor, last, precision=HIGH, preferred_element_type=F32
    )
    factor_copy.wait_send()
    coupling_copy.wait()


def finish(full_a, full_b, samples):
    matrix = pltpu.VMEM((RANK, RANK), F32)
    dma = pltpu.SemaphoreType.DMA
    return pl.pallas_call(
        finish_kernel,
        out_shape=(
            jax.ShapeDtypeStruct((ROWS, RANK), F32),
            jax.ShapeDtypeStruct((2, RANK, RANK), F32),
        ),
        in_specs=[VMEM] * 3,
        out_specs=(VMEM,) * 2,
        scratch_shapes=[
            pltpu.VMEM((2, RANK, RANK), F32),
            pltpu.VMEM((2, RANK, RANK), F32),
            matrix,
            matrix,
            dma((2,)),
            dma((2,)),
        ],
        compiler_params=pltpu.CompilerParams(
            collective_id=2, has_side_effects=True, vmem_limit_bytes=32 << 20
        ),
        name="finish",
    )(full_a, full_b, samples)


def body(points, omega, tree_order, sibling_blocks, cousin_blocks, skeleton):
    blocks, row_points, picks, tree_points = gather(
        points, omega, tree_order.reshape(1, ROWS), sibling_blocks, cousin_blocks
    )
    parts = sample(blocks, row_points, picks)
    samples, full_a, full_b = collect(parts, skeleton, tree_points)
    return finish(full_a, full_b, samples)


def solution(mesh):
    return jax.shard_map(
        body,
        mesh=mesh,
        in_specs=(
            P(None, ("leaf", "sub")),
            P(None, ("leaf", "sub")),
            P(("leaf", "sub")),
            P("leaf", None),
            P("leaf", None),
            P(),
        ),
        out_specs=(P(("leaf", "sub"), None), P()),
        check_vma=False,
    )
```

```python
import math

import jax
import jax.numpy as jnp
from jax import lax
from jax.experimental import pallas as pl
from jax.experimental.pallas import tpu as pltpu
from jax.sharding import PartitionSpec as P

MESH = pl.DeviceIdType.MESH
HIGH = lax.Precision.HIGH
HIGHEST = lax.Precision.HIGHEST
F32 = jnp.float32
BF16 = jnp.bfloat16
VMEM = pl.BlockSpec(memory_space=pltpu.VMEM)
HBM = pl.BlockSpec(memory_space=pltpu.HBM)

ROWS = 256
FEATS = 8
SAMPLES = 128
RANK = 256
SPAN = 288
LINK = BF16
VMEM_LIMIT = 60 << 20


def place():
    leaf = lax.axis_index("leaf")
    core = lax.axis_index("sub")
    return leaf % 4, (leaf // 4) % 4, leaf // 16, core


def device(x, y, z, core):
    return (z * 16 + y * 4 + x, core)


def send(src, dst, send_sem, recv_sem, target):
    copy = pltpu.make_async_remote_copy(
        src_ref=src,
        dst_ref=dst,
        send_sem=send_sem,
        recv_sem=recv_sem,
        device_id=target,
        device_id_type=MESH,
    )
    copy.start()
    return copy


def features(coordinates, scale, ones_first):
    norm = -2.0 * jnp.sum(coordinates * coordinates, axis=0, keepdims=True)
    first = norm.astype(BF16).astype(F32)
    second = (norm - first).astype(BF16).astype(F32)
    third = norm - first - second
    row = lax.broadcasted_iota(jnp.int32, coordinates.shape, 0)
    start = 3 if ones_first else 0
    other = 0 if ones_first else 3
    tail = jnp.where((row >= other) & (row < other + 3), 1.0, 0.0)
    tail = jnp.where(row == start, first, tail)
    tail = jnp.where(row == start + 1, second, tail)
    tail = jnp.where(row == start + 2, third, tail)
    return jnp.concatenate([scale * coordinates, tail], axis=0)


def fold(factors, lines):
    a, b, c, d = (factor * values for factor, values in zip(factors, lines, strict=True))
    return (a + b) + (c + d)


def pivots(entry):
    def pair(a, b, c):
        scale = lax.rsqrt(a)
        return scale, b * scale, a * lax.rsqrt(a * (a * c - b * b))

    r0, l10, r1 = pair(entry(0, 0), entry(1, 0), entry(1, 1))
    l20, l30 = entry(2, 0) * r0, entry(3, 0) * r0
    l21, l31 = (entry(2, 1) - l20 * l10) * r1, (entry(3, 1) - l30 * l10) * r1
    r2, l32, r3 = pair(
        entry(2, 2) - (l20 * l20 + l21 * l21),
        entry(3, 2) - (l30 * l20 + l31 * l21),
        entry(3, 3) - (l30 * l30 + l31 * l31),
    )

    def solve(values):
        v0 = values[0] * r0
        v1 = (values[1] - v0 * l10) * r1
        v2 = (values[2] - (v0 * l20 + v1 * l21)) * r2
        v3 = ((values[3] - (v0 * l30 + v1 * l31)) - v2 * l32) * r3
        return [v0, v1, v2, v3]

    return solve


MATE = 0
USE = [
    (MATE, 0), (6, 0), (2, 0), (5, 0), (MATE, 1), (MATE, 3), (6, 1), (6, 3),
    (3, 0), (3, 1), (MATE, 2), (6, 2), (3, 3), (3, 2), (2, 1), (2, 3),
    (5, 1), (5, 3), (2, 2), (5, 2), (4, 0), (4, 1), (4, 3), (4, 2),
]
SLOT = {block: slot for slot, block in enumerate(USE)}
KIND = {MATE: 1, 6: 1, 3: 1, 2: 0, 5: 0, 4: 0}


def make_masks(lists, near_mask, far_mask, x, y, z):
    lane = lax.broadcasted_iota(jnp.int32, (8, 128), 1)
    group = lax.broadcasted_iota(jnp.int32, (8, 128), 0) // 4
    named = jnp.full((8, 128), -1, jnp.int32)
    near = jnp.zeros((8, 128), F32)
    for slot, (dz, along) in enumerate(USE):
        plane = (z + (dz or 7 - 6 * (z % 2))) % 8
        if KIND[dz]:
            block = plane * 16 + y * 4 + (x + along) % 4
        else:
            block = plane * 16 + ((y + along) % 4) * 4 + x
        named = jnp.where((lane == slot) & (group == KIND[dz]), block, named)
        near = jnp.where(lane == slot, jnp.where(plane // 4 == z // 4, 1.0, 0.0), near)
    named = named.astype(F32)
    hit = jnp.zeros((8, 128), F32)
    for side, length in ((0, 16), (1, 32)):
        entries = jnp.concatenate(
            [lists[k, at, side : side + 1, :] for k in range(2) for at in range(4)], axis=0
        ).astype(F32)
        for e in range(length):
            hit = jnp.where(named == jnp.broadcast_to(entries[:, e : e + 1], (8, 128)), 1.0, hit)
    near_hit, far_hit = (hit * near).T, (hit * (1.0 - near)).T
    for r in range(8):
        near_mask[r] = jnp.broadcast_to(near_hit[0:32, r : r + 1], (32, 128))
        far_mask[r] = jnp.broadcast_to(far_hit[0:32, r : r + 1], (32, 128))


def whole_kernel(
    points_in, omega_in, order_in, siblings_in, cousins_in, skeleton_in,
    basis, coupling,
    points, omega, tree_order, siblings, cousins, skeleton, load_sems,
    blocks, row_points, lists, own, own_rows, own_lists, near_mask, far_mask, rows, even_tile, odd_tile, parts,
    hop_send, hop_recv, out_send, out_recv, far_send, far_recv, rows_send, rows_recv, list_send, list_recv,
    other_core, relay_out, relay_in, near_out, near_in, table, other_table, piece, pieces, full_a, full_b,
    core_send, core_recv, relay_sems, near_sems, table_sems, piece_send, piece_recv,
    z_send, z_recv, y_sems, x_sems,
    work, chosen, factor_out, factor_in, factor_sems, coupling_sems,
):
    loads = [
        pltpu.make_async_copy(source, target, load_sems.at[k])
        for k, (source, target) in enumerate(
            [
                (omega_in, omega),
                (points_in, points),
                (order_in, tree_order),
                (siblings_in, siblings),
                (cousins_in, cousins),
                (skeleton_in, skeleton),
            ]
        )
    ]
    for copy in loads:
        copy.start()
    x, y, z, core = place()
    leaf = z * 16 + y * 4 + x
    node, pair = z // 2, z // 4
    other = device(x, y, z, 1 - core)
    right, left_side = device((x + 1) % 4, y, z, core), device((x + 3) % 4, y, z, core)
    above, below = device(x, (y + 1) % 4, z, core), device(x, (y + 3) % 4, z, core)
    upward, downward = device(x, y, (z + 1) % 8, core), device(x, y, (z + 7) % 8, core)
    mates = []
    for dz in range(2):
        for dy in range(4):
            for dx in range(4):
                if dz or dy or dx:
                    where = ((x + dx) % 4, (y + dy) % 4, node * 2 + (z + dz) % 2)
                    mates.append((dz * 16 + dy * 4 + dx, where, device(*where, core)))
    column = [device(x, y, (z + dz) % 8, pair) for dz in range(8)]
    along_x = [device((x + d) % 4, y, z, core) for d in range(4)]
    along_y = [device(x, (y + d) % 4, z, core) for d in range(4)]
    partners = [who for _, _, who in mates] + [other]
    partners += [
        device(x, y, ((node + dn) % 4) * 2 + dz, c) for dn in range(1, 4) for dz in range(2) for c in range(2)
    ]
    partners.append(device(x, y, node * 2 + (z + 1) % 2, 1 - core))
    barrier = pltpu.get_barrier_semaphore()
    for partner in partners:
        pl.semaphore_signal(barrier, inc=1, device_id=partner, device_id_type=MESH)

    loads[0].wait()
    own[0:ROWS, :] = omega[...].astype(F32).T.astype(BF16)
    loads[1].wait()
    columns = features(points[...].astype(F32), 1.0, False).astype(BF16)
    own[256:272, :] = columns[:, :128]
    own[272:288, :] = columns[:, 128:]
    halves = (pl.ds(0, SPAN // 2), pl.ds(SPAN // 2, SPAN // 2))
    pl.semaphore_wait(barrier, len(partners))

    from_below, from_above = 24 * (z % 2), 24 * ((z + 1) % 2)
    hops = {}

    def hop(ref, slot, key, half, who):
        hops[key, half] = send(
            ref.at[halves[half]], blocks.at[slot, halves[half]],
            hop_send.at[key, half], hop_recv.at[key, half], who,
        )

    for step in range(2):
        hop(own, from_above, 7, step, upward)
        hop(own, from_below, 1, 1 - step, downward)

    for copy in loads[2:]:
        copy.wait()
    local = tree_order[...] % ROWS
    lane = lax.broadcasted_iota(jnp.int32, (ROWS, ROWS), 0)
    pick = jnp.where(lane == local, 1.0, 0.0).astype(BF16)
    mine = jnp.dot(points[...], pick, preferred_element_type=F32)
    own_rows[...] = features(mine, 4.0, True).astype(BF16)
    own_lists[...] = jnp.zeros_like(own_lists)
    own_lists[0:1, 0:16] = siblings[...]
    own_lists[1:2, 0:32] = cousins[...]
    small = []
    for kind, (at, line) in enumerate(((x, along_x), (y, along_y))):
        row_points[kind, at, core] = own_rows[...]
        lists[kind, at] = own_lists[...]
        for d in range(1, 4):
            target = row_points.at[kind, at, core]
            small.append(send(own_rows, target, rows_send.at[kind, d], rows_recv.at[kind, d], line[d]))
            target = lists.at[kind, at]
            small.append(send(own_lists, target, list_send.at[kind, d], list_recv.at[kind, d], line[d]))
    parts[...] = jnp.zeros_like(parts)

    plus, minus = (above, right), (below, left_side)
    outs, fars = {}, {}

    def fan_out(k, dz, half):
        kind = KIND[dz]
        block = blocks.at[SLOT[dz, 0], halves[half]]
        for side, (at, who) in enumerate(((SLOT[dz, 3], plus[kind]), (SLOT[dz, 1], minus[kind]))):
            outs[k, side, half] = send(
                block, blocks.at[at, halves[half]], out_send.at[k, side, half], out_recv.at[k, side, half], who
            )

    def relay(k, dz):
        kind = KIND[dz]
        for side, (at, who) in enumerate(((SLOT[dz, 3], plus[kind]), (SLOT[dz, 1], minus[kind]))):
            outs[k, side, side].wait_recv()
            fars[k, side] = send(
                blocks.at[at, halves[side]], blocks.at[SLOT[dz, 2], halves[side]],
                far_send.at[k, side], far_recv.at[k, side], who,
            )

    def landed(*ks):
        for k in ks:
            for side in range(2):
                outs[k, side, 1 - side].wait_recv()

    def passed(*ks):
        for k in ks:
            for side in range(2):
                fars[k, side].wait_recv()

    for step in range(2):
        hops[7, step].wait_recv()
        hop(blocks.at[from_below], SLOT[6, 0], 6, step, upward)
        hops[1, 1 - step].wait_recv()
        hop(blocks.at[from_above], SLOT[2, 0], 2, 1 - step, downward)
    for half in range(2):
        fan_out(0, MATE, half)
    for copy in small:
        copy.wait_recv()
    swap_rows = send(row_points.at[:, :, core], row_points.at[:, :, core], rows_send.at[0, 0], rows_recv.at[0, 0], other)
    make_masks(lists, near_mask, far_mask, x, y, z)
    for step in range(2):
        hops[6, step].wait_recv()
        hop(blocks.at[SLOT[6, 0]], SLOT[5, 0], 5, step, upward)
        fan_out(1, 6, step)
        hops[2, 1 - step].wait_recv()
        hop(blocks.at[SLOT[2, 0]], SLOT[3, 0], 3, 1 - step, downward)
        fan_out(2, 2, 1 - step)
    swap_rows.wait()
    for r in range(8):
        for half in range(2):
            rows[r, half * ROWS : (half + 1) * ROWS, :] = row_points[r // 4, r % 4, half].astype(F32).T.astype(BF16)

    def kernel_tile(r, use, tile):
        columns = jnp.concatenate(
            [blocks[2 * use + k, at : at + 16, :] for k in range(2) for at in (256, 272)], axis=1
        )
        exponent = jnp.dot(rows[r], columns, preferred_element_type=F32)
        tile[...] = jnp.exp(exponent).astype(BF16)

    def add(kind, at, use, tile):
        r = kind * 4 + at
        weights = []
        for k in range(2):
            slot = 2 * use + k
            values = blocks[slot, 0:ROWS, :]
            near = near_mask[r, pl.ds(slot, 1), :].astype(BF16)
            far = far_mask[r, pl.ds(slot, 1), :].astype(BF16)
            weights.append(jnp.concatenate([values * near, values * far], axis=1))
        terms = jnp.dot(tile[...], jnp.concatenate(weights, axis=0), preferred_element_type=F32)
        parts[0, kind, at] += terms[0:ROWS]
        parts[1, kind, at] += terms[ROWS:]

    def batch(kind, count, item):
        at, use = item(0)
        kernel_tile(kind * 4 + at, use, even_tile)

        def two_steps(step, carry):
            at0, use0 = item(2 * step)
            at1, use1 = item(2 * step + 1)
            at2, use2 = item((2 * step + 2) % count)
            kernel_tile(kind * 4 + at1, use1, odd_tile)
            add(kind, at0, use0, even_tile)
            kernel_tile(kind * 4 + at2, use2, even_tile)
            add(kind, at1, use1, odd_tile)
            return carry

        lax.fori_loop(0, count // 2, two_steps, 0)

    batch(1, 4, lambda i: (i, 0))
    relay(0, MATE)
    hops[5, 0].wait_recv()
    hop(blocks.at[SLOT[5, 0]], SLOT[4, 0], 4, 0, upward)
    fan_out(3, 5, 0)
    hops[3, 1].wait_recv()
    hop(blocks.at[SLOT[3, 0]], SLOT[4, 0], 4, 1, downward)
    fan_out(4, 3, 1)
    hops[5, 1].wait_recv()
    fan_out(3, 5, 1)
    hops[3, 0].wait_recv()
    fan_out(4, 3, 0)
    batch(0, 4, lambda i: (i, 1))
    relay(1, 6)
    relay(2, 2)
    for half in range(2):
        hops[4, half].wait_recv()
        fan_out(5, 4, half)
    landed(0, 1)
    batch(1, 8, lambda i: (i % 4, 2 + i // 4))
    relay(3, 5)
    relay(4, 3)
    relay(5, 4)
    landed(4)
    passed(0, 1)
    batch(1, 8, lambda i: (i % 4, 4 + i // 4))
    passed(4)
    batch(1, 4, lambda i: (i, 6))

    ahead, behind, across = (x + 1) % 4, (x + 3) % 4, (x + 2) % 4
    next_y, last_y = (y + 1) % 4, (y + 3) % 4
    order = [(across, (y + 2) % 4), (ahead, next_y), (behind, last_y), (x, y)]
    swap = {}

    def give(step, kind):
        at = order[step][kind]
        swap[step, kind] = send(
            parts.at[1 - core, kind, at], other_core.at[kind, at],
            core_send.at[kind, step], core_recv.at[kind, step], other,
        )


    def partial(step, kind):
        swap[step, kind].wait_recv()
        at = order[step][kind]
        return parts[core, kind, at] + other_core[kind, at]

    forward, backward = (right, above), (left_side, below)
    lower, upper = pl.ds(0, 128), pl.ds(128, 128)
    relays, nears = {}, []

    def pass_on(kind, side, first, rows_of, who):
        ref = near_out.at[kind, side, rows_of]
        landing = near_in.at[kind, side, rows_of]
        nears.append(send(ref, landing, near_sems.at[0, kind, side, first], near_sems.at[1, kind, side, first], who))

    def start_sum(kind):
        relay_out[kind] = partial(0, kind).astype(LINK)
        for side, (rows_of, who) in enumerate(((lower, forward[kind]), (upper, backward[kind]))):
            relays[kind, side] = send(
                relay_out.at[kind, rows_of], relay_in.at[kind, side],
                relay_sems.at[0, kind, side], relay_sems.at[1, kind, side], who,
            )

    def middle_sum(kind):
        near_out[kind, 0] = partial(1, kind).astype(LINK)
        pass_on(kind, 0, 0, upper, forward[kind])
        near_out[kind, 1] = partial(2, kind).astype(LINK)
        pass_on(kind, 1, 0, lower, backward[kind])

    def end_sum(kind):
        relays[kind, 0].wait_recv()
        near_out[kind, 0, 0:128, :] = (
            parts[core, kind, order[1][kind], 0:128, :]
            + other_core[kind, order[1][kind], 0:128, :]
            + relay_in[kind, 0].astype(F32)
        ).astype(LINK)
        pass_on(kind, 0, 1, lower, forward[kind])
        relays[kind, 1].wait_recv()
        near_out[kind, 1, 128:256, :] = (
            parts[core, kind, order[2][kind], 128:256, :]
            + other_core[kind, order[2][kind], 128:256, :]
            + relay_in[kind, 1].astype(F32)
        ).astype(LINK)
        pass_on(kind, 1, 1, upper, backward[kind])

    for step in range(4):
        give(step, 1)
    landed(2, 3, 5)
    passed(2, 3, 5)
    batch(0, 10, lambda i: ((x + 2 + 3 * (i // 5)) % 4, 7 + i % 5))
    give(0, 0)
    give(1, 0)
    start_sum(1)
    middle_sum(1)
    batch(0, 10, lambda i: ((x + 3 + i // 5) % 4, 7 + i % 5))
    give(2, 0)
    give(3, 0)
    start_sum(0)
    end_sum(1)
    middle_sum(0)
    end_sum(0)
    total = partial(3, 1) + partial(3, 0)
    first_row = (leaf * 2 + core) * ROWS
    row = lax.broadcasted_iota(jnp.int32, (ROWS, RANK), 0) + first_row
    picked = jnp.where(row == skeleton[pl.ds(node, 1), :], 1.0, 0.0)
    own_skeleton = jnp.dot(
        mine.astype(BF16), picked.astype(BF16), preferred_element_type=F32
    )
    for copy in nears:
        copy.wait_recv()
    for kind in range(2):
        for side in range(2):
            total = total + near_in[kind, side].astype(F32)
    rows_here = total

    table[0:256, :] = lax.dot_general(
        rows_here, rows_here, (((0,), (0,)), ((), ())), precision=HIGHEST, preferred_element_type=F32
    )
    table[128:256, 0:128] = jnp.zeros((128, 128), F32)
    table[128:136, 0:128] = own_skeleton[:, 0:128]
    table[136:144, 0:128] = own_skeleton[:, 128:256]
    table[256:512, :] = lax.dot_general(
        picked, rows_here, (((0,), (0,)), ((), ())), precision=HIGHEST, preferred_element_type=F32
    )
    start = pl.multiple_of((1 - core) * 256, 256)
    swap_table = send(
        table.at[pl.ds(start, 256)], other_table, table_sems.at[0], table_sems.at[1], other
    )
    swap_table.wait()
    keep = pl.multiple_of(core * 256, 256)
    other_table[...] += table[pl.ds(keep, 256), :]

    def chunk(where):
        first = (where[0] * 8 + where[1] * 2 + where[2] % 2) * 8
        return other_table.at[pl.ds(pl.multiple_of(first, 8), 8)]

    spreads = []
    for slot, where, who in mates:
        spreads.append(
            send(chunk(where), pieces.at[slot], piece_send.at[slot], piece_recv.at[slot], who)
        )
    sums = chunk((x, y, z))[...]
    for copy in spreads:
        copy.wait_recv()
    for slot, _, _ in mates:
        sums = sums + pieces[slot]
    piece[0] = sums[:, 0:128]
    piece[1] = sums[:, 128:256]
    for copy in spreads:
        copy.wait_send()

    home_a, home_b = full_a.at[x, y, z % 4, core], full_b.at[y, x, z % 4, core]

    def drop(dz, half):
        return pltpu.make_async_remote_copy(
            src_ref=piece.at[half],
            dst_ref=(home_a, home_b)[half],
            send_sem=z_send.at[dz, half],
            recv_sem=z_recv.at[z % 4, core, half],
            device_id=column[dz],
            device_id_type=MESH,
        )

    def arrival(plane, c, half):
        landing = (full_a.at[x, y, plane, c], full_b.at[y, x, plane, c])[half]
        return pltpu.make_async_remote_copy(
            src_ref=piece.at[half],
            dst_ref=landing,
            send_sem=z_send.at[0, half],
            recv_sem=z_recv.at[plane, c, half],
            device_id=other,
            device_id_type=MESH,
        )

    for dz in (4, 3, 5, 2, 6, 1, 7):
        for half in range(2):
            drop(dz, half).start()

    @pl.when(pair == core)
    def _():
        home_a[...] = piece[0]
        home_b[...] = piece[1]

    @pl.when(pair != core)
    def _():
        for half in range(2):
            drop(0, half).start()

    for plane in range(4):
        for c in range(2):

            @pl.when((core * 4 + plane != z) | (core != c))
            def _(plane=plane, c=c):
                for half in range(2):
                    arrival(plane, c, half).wait_recv()

    cuts = (pl.ds(0, 2), pl.ds(2, 2))

    def push(ref, sems, k, who):
        return send(ref, ref, sems.at[2 * k], sems.at[2 * k + 1], who)

    def ring(at, sems, first_k, forward, backward):
        return [
            push(at.at[cuts[0]], sems, first_k, forward),
            push(at.at[cuts[1]], sems, first_k + 1, backward),
            push(at.at[cuts[1]], sems, first_k + 2, forward),
            push(at.at[cuts[0]], sems, first_k + 3, backward),
        ]

    def pass_along(copies, sems, first_k, before, after, forward, backward):
        copies[0].wait_recv()
        copies.append(push(before.at[cuts[0]], sems, first_k + 4, forward))
        copies[1].wait_recv()
        copies.append(push(after.at[cuts[1]], sems, first_k + 5, backward))

    first = ring(full_a.at[x, y], y_sems, 0, above, below)
    second = ring(full_b.at[y, x], x_sems, 0, right, left_side)
    pass_along(first, y_sems, 0, full_a.at[x, last_y], full_a.at[x, next_y], above, below)
    pass_along(second, x_sems, 0, full_b.at[y, behind], full_b.at[y, ahead], right, left_side)
    for copy in first[2:6]:
        copy.wait_recv()
    third = ring(full_a.at[x], x_sems, 6, right, left_side)
    for copy in second[2:6]:
        copy.wait_recv()
    fourth = ring(full_b.at[y], y_sems, 6, above, below)
    pass_along(third, x_sems, 6, full_a.at[behind], full_a.at[ahead], right, left_side)
    pass_along(fourth, y_sems, 6, full_b.at[last_y], full_b.at[next_y], above, below)
    for copy in third[2:] + fourth[2:]:
        copy.wait_recv()
    for copy in first + second + third + fourth:
        copy.wait_send()
    for dz in range(1, 8):
        for half in range(2):
            drop(dz, half).wait_send()

    @pl.when(pair != core)
    def _():
        for half in range(2):
            drop(0, half).wait_send()

    row = lax.broadcasted_iota(jnp.int32, (RANK, RANK), 0)
    col = lax.broadcasted_iota(jnp.int32, (RANK, RANK), 1)
    skeleton_points, sizes = [], []
    for n in range(2):
        for at_x in range(4):
            for at_y in range(4):
                span = pl.ds(at_x * 64 + at_y * 16, 16)
                planes = pl.ds(2 * n, 2)
                for kind, target in enumerate((work, chosen)):
                    target[n, span, 0:128] = full_a[at_x, at_y, planes, kind].reshape(16, 128)
                    target[n, span, 128:256] = full_b[at_y, at_x, planes, kind].reshape(16, 128)
        skeleton_points.append(
            jnp.concatenate([work[n, 128:136, 0:128], work[n, 136:144, 0:128]], axis=1)
        )
        gram = work[n]
        on_diagonal = jnp.where(row == col, gram, 0.0)
        trace = jnp.sum(jnp.sum(on_diagonal, axis=0, keepdims=True), axis=1, keepdims=True)
        work[n] = gram * (1.0 / trace) + jnp.where(row == col, 0.01, 0.0)
        sizes.append(lax.rsqrt(trace))

    row_side = features(skeleton_points[0], 4.0, True).T.astype(BF16)
    col_side = features(skeleton_points[1], 1.0, False).astype(BF16)
    kernel_skel = jnp.exp(jnp.dot(row_side, col_side, preferred_element_type=F32))
    right = jnp.dot(kernel_skel, chosen[1], precision=HIGH, preferred_element_type=F32)
    middle = lax.dot_general(
        chosen[0], right, (((0,), (0,)), ((), ())), precision=HIGH, preferred_element_type=F32
    )

    lane8 = lax.broadcasted_iota(jnp.int32, (8, 128), 1)
    row8 = lax.broadcasted_iota(jnp.int32, (8, 128), 0)
    group8 = (lane8 // 64) * 64
    lane = lax.broadcasted_iota(jnp.int32, (64, 128), 1)
    for p in range(4):
        top = 64 * p
        aligned = (top // 128) * 128
        packed = []
        for n in range(2):
            block = work[n, top : top + 64, aligned : aligned + 128]
            packed.append(pltpu.roll(block, 64, 1) if (64 * n - top) % 128 else block)
        packed = jnp.where(lane < 64, packed[0], packed[1])
        left = [packed[8 * g : 8 * g + 8] for g in range(8)]
        inverse = [jnp.where(lane8 - group8 == row8 + 8 * g, 1.0, 0.0) for g in range(8)]
        for j in range(0, 64, 4):
            own, inner = j // 8, j % 8
            spread = {
                g: [
                    jnp.take_along_axis(left[g], group8 + (j + t), axis=1, mode="promise_in_bounds")
                    for t in range(4)
                ]
                for g in range(own, 8)
            }

            def line(tile, t, inner=inner):
                return jnp.broadcast_to(tile[inner + t : inner + t + 1, :], (8, 128))

            solve = pivots(lambda t, u: line(spread[own][u], t))
            left_rows = solve([line(left[own], t) for t in range(4)])
            inverse_rows = solve([line(inverse[own], t) for t in range(4)])
            for g in range(own, 8):
                if g == own and inner == 4:
                    continue
                factors = solve(spread[g])
                if g == own:
                    factors = [jnp.where(row8 > 3, factor, 0.0) for factor in factors]
                left[g] = left[g] - fold(factors, left_rows)
                inverse[g] = inverse[g] - fold(factors, inverse_rows)
            for t in range(4):
                inverse[own] = jnp.where(row8 == inner + t, inverse_rows[t], inverse[own])
        packed = jnp.concatenate(inverse, axis=0)
        diagonal = jnp.concatenate([jnp.where(lane < 64, packed, 0.0), jnp.where(lane < 64, 0.0, packed)], axis=0)
        stacked = jnp.concatenate([work[n, top : top + 64, :] for n in range(2)], axis=0)
        srow = lax.broadcasted_iota(jnp.int32, (128, RANK), 0)
        scol = lax.broadcasted_iota(jnp.int32, (128, RANK), 1)
        identity = jnp.where(srow % 64 == scol % 64, 1.0, 0.0)
        stacked = jnp.where(scol // 64 == p, identity, stacked)
        solved = jnp.dot(diagonal, stacked, precision=HIGH, preferred_element_type=F32)
        done = jnp.where(scol < top + 64, solved, 0.0)
        for n in range(2):
            work[n, top : top + 64, :] = done[64 * n : 64 * n + 64]
        rest = RANK - top - 64
        if rest:
            turned = solved.T[top + 64 :, :]
            tlane = lax.broadcasted_iota(jnp.int32, (rest, 128), 1)
            tcol = lax.broadcasted_iota(jnp.int32, (rest, RANK), 1)
            for n in range(2):
                update = jnp.dot(
                    jnp.where(tlane // 64 == n, turned, 0.0), solved,
                    precision=HIGH, preferred_element_type=F32,
                )
                work[n, top + 64 :, :] = jnp.where(tcol // 64 == p, 0.0, work[n, top + 64 :, :]) - update

    size = jnp.where(node % 2 == 0, sizes[0], sizes[1])
    factor_out[...] = work[node % 2] * size
    factor_copy = send(factor_out, factor_in, factor_sems.at[0], factor_sems.at[1], other)
    last = (((1,), (1,)), ((), ()))
    half = jnp.dot(work[0], middle, precision=HIGH, preferred_element_type=F32)
    coupling[core] = ((16384.0 / math.sqrt(RANK)) * sizes[0] * sizes[1]) * lax.dot_general(
        half, work[1], last, precision=HIGH, preferred_element_type=F32
    )
    coupling_copy = send(
        coupling.at[core], coupling.at[core], coupling_sems.at[0], coupling_sems.at[1], other
    )
    factor_copy.wait_recv()
    factor = jnp.where(node // 2 == core, factor_out[...], factor_in[...])
    basis[...] = 128.0 * lax.dot_general(
        rows_here, factor, last, precision=HIGH, preferred_element_type=F32
    )
    factor_copy.wait_send()
    coupling_copy.wait()


    for copy in list(relays.values()) + nears + list(swap.values()) + small:
        copy.wait_send()
    for copy in list(hops.values()) + list(outs.values()) + list(fars.values()):
        copy.wait_send()


def whole(*arguments):
    dma = pltpu.SemaphoreType.DMA

    def block(*shape, kind=F32):
        return pltpu.VMEM(shape, kind)

    i32 = jnp.int32
    return pl.pallas_call(
        whole_kernel,
        out_shape=(
            jax.ShapeDtypeStruct((ROWS, RANK), F32),
            jax.ShapeDtypeStruct((2, RANK, RANK), F32),
        ),
        in_specs=[HBM] * 6,
        out_specs=(VMEM,) * 2,
        scratch_shapes=[
            block(FEATS, ROWS, kind=BF16), block(SAMPLES, ROWS, kind=BF16), block(1, ROWS, kind=i32),
            block(1, 16, kind=i32), block(1, 32, kind=i32), block(4, RANK, kind=i32), dma((6,)),
            block(25, SPAN, 128, kind=BF16), block(2, 4, 2, 16, ROWS, kind=BF16), block(2, 4, 8, 128, kind=i32),
            block(SPAN, 128, kind=BF16), block(16, ROWS, kind=BF16), block(8, 128, kind=i32),
            block(8, 32, 128), block(8, 32, 128), block(8, 2 * ROWS, 16, kind=BF16),
            block(2 * ROWS, 2 * ROWS, kind=BF16), block(2 * ROWS, 2 * ROWS, kind=BF16), block(2, 2, 4, ROWS, RANK),
            dma((8, 2)), dma((8, 2)), dma((6, 2, 2)), dma((6, 2, 2)), dma((6, 2)), dma((6, 2)),
            dma((2, 4)), dma((2, 4)), dma((2, 4)), dma((2, 4)),
            block(2, 4, ROWS, RANK), block(2, ROWS, RANK, kind=LINK), block(2, 2, 128, RANK, kind=LINK),
            block(2, 2, ROWS, RANK, kind=LINK), block(2, 2, ROWS, RANK, kind=LINK),
            block(512, RANK), block(256, RANK), block(2, 8, 128), block(32, 8, RANK),
            block(4, 4, 4, 2, 8, 128), block(4, 4, 4, 2, 8, 128),
            dma((2, 4)), dma((2, 4)), dma((2, 2, 2)), dma((2, 2, 2, 2)), dma((2,)), dma((32,)), dma((32,)),
            dma((8, 2)), dma((4, 2, 2)), dma((24,)), dma((24,)),
            block(2, RANK, RANK), block(2, RANK, RANK), block(RANK, RANK), block(RANK, RANK), dma((2,)), dma((2,)),
        ],
        compiler_params=pltpu.CompilerParams(
            collective_id=0, has_side_effects=True, vmem_limit_bytes=VMEM_LIMIT
        ),
        name="whole",
    )(*arguments)


def body(points, omega, tree_order, sibling_blocks, cousin_blocks, skeleton):
    return whole(points, omega, tree_order.reshape(1, ROWS), sibling_blocks, cousin_blocks, skeleton)


def solution(mesh):
    return jax.shard_map(
        body,
        mesh=mesh,
        in_specs=(
            P(None, ("leaf", "sub")),
            P(None, ("leaf", "sub")),
            P(("leaf", "sub")),
            P("leaf", None),
            P("leaf", None),
            P(),
        ),
        out_specs=(P(("leaf", "sub"), None), P()),
        check_vma=False,
    )
```

```python
import math

import jax
import jax.numpy as jnp
from jax import lax
from jax.experimental import pallas as pl
from jax.experimental.pallas import tpu as pltpu
from jax.sharding import PartitionSpec as P

MESH = pl.DeviceIdType.MESH
HIGH = lax.Precision.HIGH
HIGHEST = lax.Precision.HIGHEST
F32 = jnp.float32
BF16 = jnp.bfloat16
VMEM = pl.BlockSpec(memory_space=pltpu.VMEM)
HBM = pl.BlockSpec(memory_space=pltpu.HBM)

ROWS = 256
FEATS = 8
SAMPLES = 128
RANK = 256
SPAN = 288
LINK = BF16
VMEM_LIMIT = 60 << 20


def place():
    leaf = lax.axis_index("leaf")
    core = lax.axis_index("sub")
    return leaf % 4, (leaf // 4) % 4, leaf // 16, core


def device(x, y, z, core):
    return (z * 16 + y * 4 + x, core)


def send(src, dst, send_sem, recv_sem, target):
    copy = pltpu.make_async_remote_copy(
        src_ref=src,
        dst_ref=dst,
        send_sem=send_sem,
        recv_sem=recv_sem,
        device_id=target,
        device_id_type=MESH,
    )
    copy.start()
    return copy


def features(coordinates, scale, ones_first):
    norm = -2.0 * jnp.sum(coordinates * coordinates, axis=0, keepdims=True)
    first = norm.astype(BF16).astype(F32)
    second = (norm - first).astype(BF16).astype(F32)
    third = norm - first - second
    row = lax.broadcasted_iota(jnp.int32, coordinates.shape, 0)
    start = 3 if ones_first else 0
    other = 0 if ones_first else 3
    tail = jnp.where((row >= other) & (row < other + 3), 1.0, 0.0)
    tail = jnp.where(row == start, first, tail)
    tail = jnp.where(row == start + 1, second, tail)
    tail = jnp.where(row == start + 2, third, tail)
    return jnp.concatenate([scale * coordinates, tail], axis=0)


def fold(factors, lines):
    a, b, c, d = (factor * values for factor, values in zip(factors, lines, strict=True))
    return (a + b) + (c + d)


def pivots(entry):
    def pair(a, b, c):
        scale = lax.rsqrt(a)
        return scale, b * scale, a * lax.rsqrt(a * (a * c - b * b))

    r0, l10, r1 = pair(entry(0, 0), entry(1, 0), entry(1, 1))
    l20, l30 = entry(2, 0) * r0, entry(3, 0) * r0
    l21, l31 = (entry(2, 1) - l20 * l10) * r1, (entry(3, 1) - l30 * l10) * r1
    r2, l32, r3 = pair(
        entry(2, 2) - (l20 * l20 + l21 * l21),
        entry(3, 2) - (l30 * l20 + l31 * l21),
        entry(3, 3) - (l30 * l30 + l31 * l31),
    )

    def solve(values):
        v0 = values[0] * r0
        v1 = (values[1] - v0 * l10) * r1
        v2 = (values[2] - (v0 * l20 + v1 * l21)) * r2
        v3 = ((values[3] - (v0 * l30 + v1 * l31)) - v2 * l32) * r3
        return [v0, v1, v2, v3]

    return solve


MATE = 0
USE = [
    (MATE, 0), (6, 0), (2, 0), (5, 0), (MATE, 1), (MATE, 3), (6, 1), (6, 3),
    (3, 0), (3, 1), (MATE, 2), (6, 2), (3, 3), (3, 2), (2, 1), (2, 3),
    (5, 1), (5, 3), (2, 2), (5, 2), (4, 0), (4, 1), (4, 3), (4, 2),
]
SLOT = {block: slot for slot, block in enumerate(USE)}
KIND = {MATE: 1, 6: 1, 3: 1, 2: 0, 5: 0, 4: 0}


def make_masks(lists, near_mask, far_mask, x, y, z):
    lane = lax.broadcasted_iota(jnp.int32, (8, 128), 1)
    group = lax.broadcasted_iota(jnp.int32, (8, 128), 0) // 4
    named = jnp.full((8, 128), -1, jnp.int32)
    near = jnp.zeros((8, 128), F32)
    for slot, (dz, along) in enumerate(USE):
        plane = (z + (dz or 7 - 6 * (z % 2))) % 8
        if KIND[dz]:
            block = plane * 16 + y * 4 + (x + along) % 4
        else:
            block = plane * 16 + ((y + along) % 4) * 4 + x
        named = jnp.where((lane == slot) & (group == KIND[dz]), block, named)
        near = jnp.where(lane == slot, jnp.where(plane // 4 == z // 4, 1.0, 0.0), near)
    named = named.astype(F32)
    hit = jnp.zeros((8, 128), F32)
    for side, length in ((0, 16), (1, 32)):
        entries = jnp.concatenate(
            [lists[k, at, side : side + 1, :] for k in range(2) for at in range(4)], axis=0
        ).astype(F32)
        for e in range(length):
            hit = jnp.where(named == jnp.broadcast_to(entries[:, e : e + 1], (8, 128)), 1.0, hit)
    near_hit, far_hit = (hit * near).T, (hit * (1.0 - near)).T
    for r in range(8):
        near_mask[r] = jnp.broadcast_to(near_hit[0:32, r : r + 1], (32, 128))
        far_mask[r] = jnp.broadcast_to(far_hit[0:32, r : r + 1], (32, 128))


def whole_kernel(
    points_in, omega_in, order_in, siblings_in, cousins_in, skeleton_in,
    basis, coupling,
    points, omega, tree_order, siblings, cousins, skeleton, load_sems,
    blocks, row_points, lists, own, own_rows, own_lists, near_mask, far_mask, rows, even_tile, odd_tile, parts,
    hop_send, hop_recv, out_send, out_recv, far_send, far_recv, rows_send, rows_recv, list_send, list_recv,
    other_core, relay_out, relay_in, near_out, near_in, table, other_table, piece, pieces, landing, full_a, full_b,
    core_send, core_recv, relay_sems, near_sems, table_sems, piece_send, piece_recv,
    z_send, z_recv, y_sems, x_sems,
    work, chosen, factor_out, factor_in, factor_sems, coupling_sems,
):
    loads = [
        pltpu.make_async_copy(source, target, load_sems.at[k])
        for k, (source, target) in enumerate(
            [
                (omega_in, omega),
                (points_in, points),
                (order_in, tree_order),
                (siblings_in, siblings),
                (cousins_in, cousins),
                (skeleton_in, skeleton),
            ]
        )
    ]
    for copy in loads:
        copy.start()
    x, y, z, core = place()
    leaf = z * 16 + y * 4 + x
    node, pair = z // 2, z // 4
    other = device(x, y, z, 1 - core)
    right, left_side = device((x + 1) % 4, y, z, core), device((x + 3) % 4, y, z, core)
    above, below = device(x, (y + 1) % 4, z, core), device(x, (y + 3) % 4, z, core)
    upward, downward = device(x, y, (z + 1) % 8, core), device(x, y, (z + 7) % 8, core)
    mates = []
    for dz in range(2):
        for dy in range(4):
            for dx in range(4):
                if dz or dy or dx:
                    where = ((x + dx) % 4, (y + dy) % 4, node * 2 + (z + dz) % 2)
                    mates.append((dz * 16 + dy * 4 + dx, where, device(*where, core)))
    column = [device(x, y, (z + dz) % 8, pair) for dz in range(8)]
    along_x = [device((x + d) % 4, y, z, core) for d in range(4)]
    along_y = [device(x, (y + d) % 4, z, core) for d in range(4)]
    partners = [who for _, _, who in mates] + [other]
    partners += [
        device(x, y, ((node + dn) % 4) * 2 + dz, c) for dn in range(1, 4) for dz in range(2) for c in range(2)
    ]
    partners.append(device(x, y, node * 2 + (z + 1) % 2, 1 - core))
    barrier = pltpu.get_barrier_semaphore()
    for partner in partners:
        pl.semaphore_signal(barrier, inc=1, device_id=partner, device_id_type=MESH)

    loads[0].wait()
    own[0:ROWS, :] = omega[...].astype(F32).T.astype(BF16)
    loads[1].wait()
    columns = features(points[...].astype(F32), 1.0, False).astype(BF16)
    own[256:272, :] = columns[:, :128]
    own[272:288, :] = columns[:, 128:]
    halves = (pl.ds(0, SPAN // 2), pl.ds(SPAN // 2, SPAN // 2))
    pl.semaphore_wait(barrier, len(partners))

    from_below, from_above = 24 * (z % 2), 24 * ((z + 1) % 2)
    hops = {}

    def hop(ref, slot, key, half, who):
        hops[key, half] = send(
            ref.at[halves[half]], blocks.at[slot, halves[half]],
            hop_send.at[key, half], hop_recv.at[key, half], who,
        )

    for step in range(2):
        hop(own, from_above, 7, step, upward)
        hop(own, from_below, 1, 1 - step, downward)

    for copy in loads[2:]:
        copy.wait()
    local = tree_order[...] % ROWS
    lane = lax.broadcasted_iota(jnp.int32, (ROWS, ROWS), 0)
    pick = jnp.where(lane == local, 1.0, 0.0).astype(BF16)
    mine = jnp.dot(points[...], pick, preferred_element_type=F32)
    own_rows[...] = features(mine, 4.0, True).astype(BF16)
    own_lists[...] = jnp.zeros_like(own_lists)
    own_lists[0:1, 0:16] = siblings[...]
    own_lists[1:2, 0:32] = cousins[...]
    small = []
    for kind, (at, line) in enumerate(((x, along_x), (y, along_y))):
        row_points[kind, at, core] = own_rows[...]
        lists[kind, at] = own_lists[...]
        for d in range(1, 4):
            target = row_points.at[kind, at, core]
            small.append(send(own_rows, target, rows_send.at[kind, d], rows_recv.at[kind, d], line[d]))
            target = lists.at[kind, at]
            small.append(send(own_lists, target, list_send.at[kind, d], list_recv.at[kind, d], line[d]))
    parts[...] = jnp.zeros_like(parts)

    plus, minus = (above, right), (below, left_side)
    outs, fars = {}, {}

    def fan_out(k, dz, half):
        kind = KIND[dz]
        block = blocks.at[SLOT[dz, 0], halves[half]]
        for side, (at, who) in enumerate(((SLOT[dz, 3], plus[kind]), (SLOT[dz, 1], minus[kind]))):
            outs[k, side, half] = send(
                block, blocks.at[at, halves[half]], out_send.at[k, side, half], out_recv.at[k, side, half], who
            )

    def relay(k, dz):
        kind = KIND[dz]
        for side, (at, who) in enumerate(((SLOT[dz, 3], plus[kind]), (SLOT[dz, 1], minus[kind]))):
            outs[k, side, side].wait_recv()
            fars[k, side] = send(
                blocks.at[at, halves[side]], blocks.at[SLOT[dz, 2], halves[side]],
                far_send.at[k, side], far_recv.at[k, side], who,
            )

    def landed(*ks):
        for k in ks:
            for side in range(2):
                outs[k, side, 1 - side].wait_recv()

    def passed(*ks):
        for k in ks:
            for side in range(2):
                fars[k, side].wait_recv()

    for step in range(2):
        hops[7, step].wait_recv()
        hop(blocks.at[from_below], SLOT[6, 0], 6, step, upward)
        hops[1, 1 - step].wait_recv()
        hop(blocks.at[from_above], SLOT[2, 0], 2, 1 - step, downward)
    for half in range(2):
        fan_out(0, MATE, half)
    for copy in small:
        copy.wait_recv()
    swap_rows = send(row_points.at[:, :, core], row_points.at[:, :, core], rows_send.at[0, 0], rows_recv.at[0, 0], other)
    make_masks(lists, near_mask, far_mask, x, y, z)
    for step in range(2):
        hops[6, step].wait_recv()
        hop(blocks.at[SLOT[6, 0]], SLOT[5, 0], 5, step, upward)
        fan_out(1, 6, step)
        hops[2, 1 - step].wait_recv()
        hop(blocks.at[SLOT[2, 0]], SLOT[3, 0], 3, 1 - step, downward)
        fan_out(2, 2, 1 - step)
    swap_rows.wait()
    for r in range(8):
        for half in range(2):
            rows[r, half * ROWS : (half + 1) * ROWS, :] = row_points[r // 4, r % 4, half].astype(F32).T.astype(BF16)

    def kernel_tile(r, use, tile):
        columns = jnp.concatenate(
            [blocks[2 * use + k, at : at + 16, :] for k in range(2) for at in (256, 272)], axis=1
        )
        exponent = jnp.dot(rows[r], columns, preferred_element_type=F32)
        tile[...] = jnp.exp(exponent).astype(BF16)

    def add(kind, at, use, tile):
        r = kind * 4 + at
        weights = []
        for k in range(2):
            slot = 2 * use + k
            values = blocks[slot, 0:ROWS, :]
            near = near_mask[r, pl.ds(slot, 1), :].astype(BF16)
            far = far_mask[r, pl.ds(slot, 1), :].astype(BF16)
            weights.append(jnp.concatenate([values * near, values * far], axis=1))
        terms = jnp.dot(tile[...], jnp.concatenate(weights, axis=0), preferred_element_type=F32)
        parts[0, kind, at] += terms[0:ROWS]
        parts[1, kind, at] += terms[ROWS:]

    def batch(kind, count, item):
        at, use = item(0)
        kernel_tile(kind * 4 + at, use, even_tile)

        def two_steps(step, carry):
            at0, use0 = item(2 * step)
            at1, use1 = item(2 * step + 1)
            at2, use2 = item(2 * step + 2)
            kernel_tile(kind * 4 + at1, use1, odd_tile)
            add(kind, at0, use0, even_tile)
            kernel_tile(kind * 4 + at2, use2, even_tile)
            add(kind, at1, use1, odd_tile)
            return carry

        lax.fori_loop(0, (count - 1) // 2, two_steps, 0)
        if count % 2:
            add(kind, *item(count - 1), even_tile)
        else:
            at, use = item(count - 1)
            kernel_tile(kind * 4 + at, use, odd_tile)
            add(kind, *item(count - 2), even_tile)
            add(kind, at, use, odd_tile)

    batch(1, 4, lambda i: (i, 0))
    relay(0, MATE)
    hops[5, 0].wait_recv()
    hop(blocks.at[SLOT[5, 0]], SLOT[4, 0], 4, 0, upward)
    fan_out(3, 5, 0)
    hops[3, 1].wait_recv()
    hop(blocks.at[SLOT[3, 0]], SLOT[4, 0], 4, 1, downward)
    fan_out(4, 3, 1)
    hops[5, 1].wait_recv()
    fan_out(3, 5, 1)
    hops[3, 0].wait_recv()
    fan_out(4, 3, 0)
    batch(0, 4, lambda i: (i, 1))
    relay(1, 6)
    relay(2, 2)
    for half in range(2):
        hops[4, half].wait_recv()
        fan_out(5, 4, half)
    landed(0, 1)
    batch(1, 8, lambda i: (i % 4, 2 + i // 4))
    relay(3, 5)
    relay(4, 3)
    relay(5, 4)
    landed(4)
    passed(0, 1)
    batch(1, 8, lambda i: (i % 4, 4 + i // 4))
    passed(4)
    batch(1, 4, lambda i: (i, 6))

    ahead, behind, across = (x + 1) % 4, (x + 3) % 4, (x + 2) % 4
    next_y, last_y = (y + 1) % 4, (y + 3) % 4
    order = [(across, (y + 2) % 4), (ahead, next_y), (behind, last_y), (x, y)]
    swap = {}

    def give(step, kind):
        at = order[step][kind]
        swap[step, kind] = send(
            parts.at[1 - core, kind, at], other_core.at[kind, at],
            core_send.at[kind, step], core_recv.at[kind, step], other,
        )


    def partial(step, kind):
        swap[step, kind].wait_recv()
        at = order[step][kind]
        return parts[core, kind, at] + other_core[kind, at]

    forward, backward = (right, above), (left_side, below)
    lower, upper = pl.ds(0, 128), pl.ds(128, 128)
    relays, nears = {}, []

    def pass_on(kind, side, first, rows_of, who):
        ref = near_out.at[kind, side, rows_of]
        target = near_in.at[kind, side, rows_of]
        nears.append(send(ref, target, near_sems.at[0, kind, side, first], near_sems.at[1, kind, side, first], who))

    def start_sum(kind):
        relay_out[kind] = partial(0, kind).astype(LINK)
        for side, (rows_of, who) in enumerate(((lower, forward[kind]), (upper, backward[kind]))):
            relays[kind, side] = send(
                relay_out.at[kind, rows_of], relay_in.at[kind, side],
                relay_sems.at[0, kind, side], relay_sems.at[1, kind, side], who,
            )

    def middle_sum(kind, side):
        near_out[kind, side] = partial(1 + side, kind).astype(LINK)
        pass_on(kind, side, 0, (upper, lower)[side], (forward, backward)[side][kind])

    def end_sum(kind):
        relays[kind, 0].wait_recv()
        near_out[kind, 0, 0:128, :] = (
            parts[core, kind, order[1][kind], 0:128, :]
            + other_core[kind, order[1][kind], 0:128, :]
            + relay_in[kind, 0].astype(F32)
        ).astype(LINK)
        pass_on(kind, 0, 1, lower, forward[kind])
        relays[kind, 1].wait_recv()
        near_out[kind, 1, 128:256, :] = (
            parts[core, kind, order[2][kind], 128:256, :]
            + other_core[kind, order[2][kind], 128:256, :]
            + relay_in[kind, 1].astype(F32)
        ).astype(LINK)
        pass_on(kind, 1, 1, upper, backward[kind])

    for step in range(4):
        give(step, 1)
    landed(2, 3, 5)
    passed(2, 3, 5)

    def last_batch(step):
        at = order[step][0]
        batch(0, 5, lambda i: (at, 7 + i))
        give(step, 0)

    last_batch(0)
    start_sum(1)
    middle_sum(1, 0)
    middle_sum(1, 1)
    last_batch(1)
    start_sum(0)
    last_batch(2)
    end_sum(1)
    middle_sum(0, 0)
    last_batch(3)
    middle_sum(0, 1)
    end_sum(0)
    total = partial(3, 1) + partial(3, 0)
    first_row = (leaf * 2 + core) * ROWS
    row = lax.broadcasted_iota(jnp.int32, (ROWS, RANK), 0) + first_row
    picked = jnp.where(row == skeleton[pl.ds(node, 1), :], 1.0, 0.0)
    own_skeleton = jnp.dot(
        mine.astype(BF16), picked.astype(BF16), preferred_element_type=F32
    )
    for copy in nears:
        copy.wait_recv()
    for kind in range(2):
        for side in range(2):
            total = total + near_in[kind, side].astype(F32)
    rows_here = total

    table[0:256, :] = lax.dot_general(
        rows_here, rows_here, (((0,), (0,)), ((), ())), precision=HIGHEST, preferred_element_type=F32
    )
    table[128:256, 0:128] = jnp.zeros((128, 128), F32)
    table[128:136, 0:128] = own_skeleton[:, 0:128]
    table[136:144, 0:128] = own_skeleton[:, 128:256]
    table[256:512, :] = lax.dot_general(
        picked, rows_here, (((0,), (0,)), ((), ())), precision=HIGHEST, preferred_element_type=F32
    )
    start = pl.multiple_of((1 - core) * 256, 256)
    swap_table = send(
        table.at[pl.ds(start, 256)], other_table, table_sems.at[0], table_sems.at[1], other
    )
    swap_table.wait()
    keep = pl.multiple_of(core * 256, 256)
    other_table[...] += table[pl.ds(keep, 256), :]

    def chunk(where):
        first = (where[0] * 8 + where[1] * 2 + where[2] % 2) * 8
        return other_table.at[pl.ds(pl.multiple_of(first, 8), 8)]

    spreads = []
    for slot, where, who in sorted(mates, key=lambda mate: -sum(min(d, 4 - d) for d in (mate[0] // 16, mate[0] // 4 % 4, mate[0] % 4))):
        spreads.append(
            send(chunk(where), pieces.at[slot], piece_send.at[slot], piece_recv.at[slot], who)
        )
    sums = chunk((x, y, z))[...]
    for copy in spreads:
        copy.wait_recv()
    for slot, _, _ in mates:
        sums = sums + pieces[slot]
    piece[0] = sums[:, 0:128]
    piece[1] = sums[:, 128:256]
    for copy in spreads:
        copy.wait_send()

    def drop(dz):
        return pltpu.make_async_remote_copy(
            src_ref=piece,
            dst_ref=landing.at[z % 4, core],
            send_sem=z_send.at[dz],
            recv_sem=z_recv.at[z % 4, core],
            device_id=column[dz],
            device_id_type=MESH,
        )

    for dz in (4, 3, 5, 2, 6, 1, 7):
        drop(dz).start()

    @pl.when(pair == core)
    def _():
        landing[z % 4, core] = piece[...]

    @pl.when(pair != core)
    def _():
        drop(0).start()

    def fan(ref, sems, first, line):
        return [
            send(ref, ref, sems.at[0, first + d - 1], sems.at[1, first + d - 1], line[d]) for d in (2, 1, 3)
        ]

    def first_leg(c):
        for plane in range(4):

            @pl.when((core * 4 + plane != z) | (core != c))
            def _(plane=plane):
                pltpu.make_async_remote_copy(
                    src_ref=piece,
                    dst_ref=landing.at[plane, c],
                    send_sem=z_send.at[0],
                    recv_sem=z_recv.at[plane, c],
                    device_id=other,
                    device_id_type=MESH,
                ).wait_recv()

        full_a[c, x, y] = landing[:, c, 0]
        full_b[c, y, x] = landing[:, c, 1]
        return fan(full_a.at[c, x, y], y_sems, 6 * c, along_y) + fan(full_b.at[c, y, x], x_sems, 6 * c, along_x)

    def second_leg(c, copies):
        for copy in copies:
            copy.wait_recv()
        return fan(full_a.at[c, x], x_sems, 6 * c + 3, along_x) + fan(full_b.at[c, y], y_sems, 6 * c + 3, along_y)

    legs = [first_leg(0)]
    legs.append(second_leg(0, legs[0]))
    legs.append(first_leg(1))
    for copy in legs[1]:
        copy.wait_recv()

    row = lax.broadcasted_iota(jnp.int32, (RANK, RANK), 0)
    col = lax.broadcasted_iota(jnp.int32, (RANK, RANK), 1)
    skeleton_points, sizes = [], []
    for n in range(2):
        for at_x in range(4):
            for at_y in range(4):
                span = pl.ds(at_x * 64 + at_y * 16, 16)
                planes = pl.ds(2 * n, 2)
                work[n, span, 0:128] = full_a[0, at_x, at_y, planes].reshape(16, 128)
                work[n, span, 128:256] = full_b[0, at_y, at_x, planes].reshape(16, 128)
        skeleton_points.append(
            jnp.concatenate([work[n, 128:136, 0:128], work[n, 136:144, 0:128]], axis=1)
        )
        gram = work[n]
        on_diagonal = jnp.where(row == col, gram, 0.0)
        trace = jnp.sum(jnp.sum(on_diagonal, axis=0, keepdims=True), axis=1, keepdims=True)
        work[n] = gram * (1.0 / trace) + jnp.where(row == col, 0.01, 0.0)
        sizes.append(lax.rsqrt(trace))

    row_side = features(skeleton_points[0], 4.0, True).T.astype(BF16)
    col_side = features(skeleton_points[1], 1.0, False).astype(BF16)
    kernel_skel = jnp.exp(jnp.dot(row_side, col_side, preferred_element_type=F32))

    lane8 = lax.broadcasted_iota(jnp.int32, (8, 128), 1)
    row8 = lax.broadcasted_iota(jnp.int32, (8, 128), 0)
    group8 = (lane8 // 64) * 64
    lane = lax.broadcasted_iota(jnp.int32, (64, 128), 1)
    for p in range(4):
        top = 64 * p
        aligned = (top // 128) * 128
        packed = []
        for n in range(2):
            block = work[n, top : top + 64, aligned : aligned + 128]
            packed.append(pltpu.roll(block, 64, 1) if (64 * n - top) % 128 else block)
        packed = jnp.where(lane < 64, packed[0], packed[1])
        left = [packed[8 * g : 8 * g + 8] for g in range(8)]
        inverse = [jnp.where(lane8 - group8 == row8 + 8 * g, 1.0, 0.0) for g in range(8)]
        for j in range(0, 64, 4):
            own, inner = j // 8, j % 8
            spread = {
                g: [
                    jnp.take_along_axis(left[g], group8 + (j + t), axis=1, mode="promise_in_bounds")
                    for t in range(4)
                ]
                for g in range(own, 8)
            }

            def line(tile, t, inner=inner):
                return jnp.broadcast_to(tile[inner + t : inner + t + 1, :], (8, 128))

            solve = pivots(lambda t, u: line(spread[own][u], t))
            left_rows = solve([line(left[own], t) for t in range(4)])
            inverse_rows = solve([line(inverse[own], t) for t in range(4)])
            for g in range(own, 8):
                if g == own and inner == 4:
                    continue
                factors = solve(spread[g])
                if g == own:
                    factors = [jnp.where(row8 > 3, factor, 0.0) for factor in factors]
                left[g] = left[g] - fold(factors, left_rows)
                inverse[g] = inverse[g] - fold(factors, inverse_rows)
            for t in range(4):
                inverse[own] = jnp.where(row8 == inner + t, inverse_rows[t], inverse[own])
        packed = jnp.concatenate(inverse, axis=0)
        diagonal = jnp.concatenate([jnp.where(lane < 64, packed, 0.0), jnp.where(lane < 64, 0.0, packed)], axis=0)
        stacked = jnp.concatenate([work[n, top : top + 64, :] for n in range(2)], axis=0)
        srow = lax.broadcasted_iota(jnp.int32, (128, RANK), 0)
        scol = lax.broadcasted_iota(jnp.int32, (128, RANK), 1)
        identity = jnp.where(srow % 64 == scol % 64, 1.0, 0.0)
        stacked = jnp.where(scol // 64 == p, identity, stacked)
        solved = jnp.dot(diagonal, stacked, precision=HIGH, preferred_element_type=F32)
        done = jnp.where(scol < top + 64, solved, 0.0)
        for n in range(2):
            work[n, top : top + 64, :] = done[64 * n : 64 * n + 64]
        rest = RANK - top - 64
        if rest:
            turned = solved.T[top + 64 :, :]
            tlane = lax.broadcasted_iota(jnp.int32, (rest, 128), 1)
            tcol = lax.broadcasted_iota(jnp.int32, (rest, RANK), 1)
            for n in range(2):
                update = jnp.dot(
                    jnp.where(tlane // 64 == n, turned, 0.0), solved,
                    precision=HIGH, preferred_element_type=F32,
                )
                work[n, top + 64 :, :] = jnp.where(tcol // 64 == p, 0.0, work[n, top + 64 :, :]) - update
        if p == 0:
            legs.append(second_leg(1, legs[2]))
        if p == 1:
            for copy in legs[3]:
                copy.wait_recv()
            for n in range(2):
                for at_x in range(4):
                    for at_y in range(4):
                        span = pl.ds(at_x * 64 + at_y * 16, 16)
                        planes = pl.ds(2 * n, 2)
                        chosen[n, span, 0:128] = full_a[1, at_x, at_y, planes].reshape(16, 128)
                        chosen[n, span, 128:256] = full_b[1, at_y, at_x, planes].reshape(16, 128)
            right_part = jnp.dot(kernel_skel, chosen[1], precision=HIGH, preferred_element_type=F32)
            middle = lax.dot_general(
                chosen[0], right_part, (((0,), (0,)), ((), ())), precision=HIGH, preferred_element_type=F32
            )

    size = jnp.where(node % 2 == 0, sizes[0], sizes[1])
    factor_out[...] = work[node % 2] * size
    factor_copy = send(factor_out, factor_in, factor_sems.at[0], factor_sems.at[1], other)
    last = (((1,), (1,)), ((), ()))
    half = jnp.dot(work[0], middle, precision=HIGH, preferred_element_type=F32)
    coupling[core] = ((16384.0 / math.sqrt(RANK)) * sizes[0] * sizes[1]) * lax.dot_general(
        half, work[1], last, precision=HIGH, preferred_element_type=F32
    )
    coupling_copy = send(
        coupling.at[core], coupling.at[core], coupling_sems.at[0], coupling_sems.at[1], other
    )
    factor_copy.wait_recv()
    factor = jnp.where(node // 2 == core, factor_out[...], factor_in[...])
    basis[...] = 128.0 * lax.dot_general(
        rows_here, factor, last, precision=HIGH, preferred_element_type=F32
    )
    factor_copy.wait_send()
    coupling_copy.wait()


    for copy in list(relays.values()) + nears + list(swap.values()) + small + sum(legs, []):
        copy.wait_send()
    for dz in range(1, 8):
        drop(dz).wait_send()

    @pl.when(pair != core)
    def _():
        drop(0).wait_send()

    for copy in list(hops.values()) + list(outs.values()) + list(fars.values()):
        copy.wait_send()


def whole(*arguments):
    dma = pltpu.SemaphoreType.DMA

    def block(*shape, kind=F32):
        return pltpu.VMEM(shape, kind)

    i32 = jnp.int32
    return pl.pallas_call(
        whole_kernel,
        out_shape=(
            jax.ShapeDtypeStruct((ROWS, RANK), F32),
            jax.ShapeDtypeStruct((2, RANK, RANK), F32),
        ),
        in_specs=[HBM] * 6,
        out_specs=(VMEM,) * 2,
        scratch_shapes=[
            block(FEATS, ROWS, kind=BF16), block(SAMPLES, ROWS, kind=BF16), block(1, ROWS, kind=i32),
            block(1, 16, kind=i32), block(1, 32, kind=i32), block(4, RANK, kind=i32), dma((6,)),
            block(25, SPAN, 128, kind=BF16), block(2, 4, 2, 16, ROWS, kind=BF16), block(2, 4, 8, 128, kind=i32),
            block(SPAN, 128, kind=BF16), block(16, ROWS, kind=BF16), block(8, 128, kind=i32),
            block(8, 32, 128), block(8, 32, 128), block(8, 2 * ROWS, 16, kind=BF16),
            block(2 * ROWS, 2 * ROWS, kind=BF16), block(2 * ROWS, 2 * ROWS, kind=BF16), block(2, 2, 4, ROWS, RANK),
            dma((8, 2)), dma((8, 2)), dma((6, 2, 2)), dma((6, 2, 2)), dma((6, 2)), dma((6, 2)),
            dma((2, 4)), dma((2, 4)), dma((2, 4)), dma((2, 4)),
            block(2, 4, ROWS, RANK), block(2, ROWS, RANK, kind=LINK), block(2, 2, 128, RANK, kind=LINK),
            block(2, 2, ROWS, RANK, kind=LINK), block(2, 2, ROWS, RANK, kind=LINK),
            block(512, RANK), block(256, RANK), block(2, 8, 128), block(32, 8, RANK),
            block(4, 2, 2, 8, 128), block(2, 4, 4, 4, 8, 128), block(2, 4, 4, 4, 8, 128),
            dma((2, 4)), dma((2, 4)), dma((2, 2, 2)), dma((2, 2, 2, 2)), dma((2,)), dma((32,)), dma((32,)),
            dma((8,)), dma((4, 2)), dma((2, 12)), dma((2, 12)),
            block(2, RANK, RANK), block(2, RANK, RANK), block(RANK, RANK), block(RANK, RANK), dma((2,)), dma((2,)),
        ],
        compiler_params=pltpu.CompilerParams(
            collective_id=0, has_side_effects=True, vmem_limit_bytes=VMEM_LIMIT
        ),
        name="whole",
    )(*arguments)


def body(points, omega, tree_order, sibling_blocks, cousin_blocks, skeleton):
    return whole(points, omega, tree_order.reshape(1, ROWS), sibling_blocks, cousin_blocks, skeleton)


def solution(mesh):
    return jax.shard_map(
        body,
        mesh=mesh,
        in_specs=(
            P(None, ("leaf", "sub")),
            P(None, ("leaf", "sub")),
            P(("leaf", "sub")),
            P("leaf", None),
            P("leaf", None),
            P(),
        ),
        out_specs=(P(("leaf", "sub"), None), P()),
        check_vma=False,
    )
```

```python
import math

import jax
import jax.numpy as jnp
from jax import lax
from jax.experimental import pallas as pl
from jax.experimental.pallas import tpu as pltpu
from jax.sharding import PartitionSpec as P

MESH = pl.DeviceIdType.MESH
HIGH = lax.Precision.HIGH
HIGHEST = lax.Precision.HIGHEST
F32 = jnp.float32
BF16 = jnp.bfloat16
HBM = pl.BlockSpec(memory_space=pltpu.HBM)

ROWS = 256
FEATS = 8
SAMPLES = 128
RANK = 256
SPAN = 288
LINK = BF16
VMEM_LIMIT = 60 << 20


def place():
    leaf = lax.axis_index("leaf")
    core = lax.axis_index("sub")
    return leaf % 4, (leaf // 4) % 4, leaf // 16, core


def device(x, y, z, core):
    return (z * 16 + y * 4 + x, core)


def send(src, dst, send_sem, recv_sem, target):
    copy = pltpu.make_async_remote_copy(
        src_ref=src,
        dst_ref=dst,
        send_sem=send_sem,
        recv_sem=recv_sem,
        device_id=target,
        device_id_type=MESH,
    )
    copy.start()
    return copy


def features(coordinates, scale, ones_first):
    norm = -2.0 * jnp.sum(coordinates * coordinates, axis=0, keepdims=True)
    first = norm.astype(BF16).astype(F32)
    second = (norm - first).astype(BF16).astype(F32)
    third = norm - first - second
    row = lax.broadcasted_iota(jnp.int32, coordinates.shape, 0)
    start = 3 if ones_first else 0
    other = 0 if ones_first else 3
    tail = jnp.where((row >= other) & (row < other + 3), 1.0, 0.0)
    tail = jnp.where(row == start, first, tail)
    tail = jnp.where(row == start + 1, second, tail)
    tail = jnp.where(row == start + 2, third, tail)
    return jnp.concatenate([scale * coordinates, tail], axis=0)


def fold(factors, lines):
    a, b, c, d = (factor * values for factor, values in zip(factors, lines, strict=True))
    return (a + b) + (c + d)


def pivots(entry):
    def pair(a, b, c):
        scale = lax.rsqrt(a)
        return scale, b * scale, a * lax.rsqrt(a * (a * c - b * b))

    r0, l10, r1 = pair(entry(0, 0), entry(1, 0), entry(1, 1))
    l20, l30 = entry(2, 0) * r0, entry(3, 0) * r0
    l21, l31 = (entry(2, 1) - l20 * l10) * r1, (entry(3, 1) - l30 * l10) * r1
    r2, l32, r3 = pair(
        entry(2, 2) - (l20 * l20 + l21 * l21),
        entry(3, 2) - (l30 * l20 + l31 * l21),
        entry(3, 3) - (l30 * l30 + l31 * l31),
    )

    def solve(values):
        v0 = values[0] * r0
        v1 = (values[1] - v0 * l10) * r1
        v2 = (values[2] - (v0 * l20 + v1 * l21)) * r2
        v3 = ((values[3] - (v0 * l30 + v1 * l31)) - v2 * l32) * r3
        return [v0, v1, v2, v3]

    return solve


MATE = 0
USE = [
    (MATE, 0), (6, 0), (2, 0), (5, 0), (MATE, 1), (MATE, 3), (6, 1), (6, 3),
    (3, 0), (3, 1), (MATE, 2), (6, 2), (3, 3), (3, 2), (2, 1), (2, 3),
    (5, 1), (5, 3), (2, 2), (5, 2), (4, 0), (4, 1), (4, 3), (4, 2),
]
SLOT = {block: slot for slot, block in enumerate(USE)}
KIND = {MATE: 1, 6: 1, 3: 1, 2: 0, 5: 0, 4: 0}


def make_masks(lists, near_mask, far_mask, x, y, z):
    lane = lax.broadcasted_iota(jnp.int32, (8, 128), 1)
    group = lax.broadcasted_iota(jnp.int32, (8, 128), 0) // 4
    named = jnp.full((8, 128), -1, jnp.int32)
    near = jnp.zeros((8, 128), F32)
    for slot, (dz, along) in enumerate(USE):
        plane = (z + (dz or 7 - 6 * (z % 2))) % 8
        if KIND[dz]:
            block = plane * 16 + y * 4 + (x + along) % 4
        else:
            block = plane * 16 + ((y + along) % 4) * 4 + x
        named = jnp.where((lane == slot) & (group == KIND[dz]), block, named)
        near = jnp.where(lane == slot, jnp.where(plane // 4 == z // 4, 1.0, 0.0), near)
    named = named.astype(F32)
    hit = jnp.zeros((8, 128), F32)
    for side, length in ((0, 16), (1, 32)):
        entries = jnp.concatenate(
            [lists[k, at, side : side + 1, :] for k in range(2) for at in range(4)], axis=0
        ).astype(F32)
        for e in range(length):
            hit = jnp.where(named == jnp.broadcast_to(entries[:, e : e + 1], (8, 128)), 1.0, hit)
    near_hit, far_hit = (hit * near).T, (hit * (1.0 - near)).T
    for r in range(8):
        near_mask[r] = jnp.broadcast_to(near_hit[0:32, r : r + 1], (32, 128))
        far_mask[r] = jnp.broadcast_to(far_hit[0:32, r : r + 1], (32, 128))


def whole_kernel(
    points_in, omega_in, order_in, siblings_in, cousins_in, skeleton_in,
    basis, coupling,
    points, omega, tree_order, siblings, cousins, skeleton, load_sems,
    blocks, row_points, lists, own, own_rows, own_lists, near_mask, far_mask, rows, even_tile, odd_tile, parts,
    hop_send, hop_recv, out_send, out_recv, far_send, far_recv, rows_send, rows_recv, list_send, list_recv,
    other_core, relay_out, relay_in, near_out, near_in, table, sums, piece, pieces, landing, full_a, full_b,
    core_send, core_recv, relay_sems, near_sems, table_sems, piece_send, piece_recv,
    z_send, z_recv, y_sems, x_sems,
    work, chosen, factor_out, factor_in, coupling_out, basis_out, factor_sems, coupling_sems, result_sems,
):
    loads = [
        pltpu.make_async_copy(source, target, load_sems.at[k])
        for k, (source, target) in enumerate(
            [
                (omega_in, omega),
                (points_in, points),
                (order_in, tree_order),
                (siblings_in, siblings),
                (cousins_in, cousins),
                (skeleton_in, skeleton),
            ]
        )
    ]
    for copy in loads:
        copy.start()
    x, y, z, core = place()
    leaf = z * 16 + y * 4 + x
    node, pair = z // 2, z // 4
    other = device(x, y, z, 1 - core)
    right, left_side = device((x + 1) % 4, y, z, core), device((x + 3) % 4, y, z, core)
    above, below = device(x, (y + 1) % 4, z, core), device(x, (y + 3) % 4, z, core)
    upward, downward = device(x, y, (z + 1) % 8, core), device(x, y, (z + 7) % 8, core)
    mates = []
    for dz in range(2):
        for dy in range(4):
            for dx in range(4):
                if dz or dy or dx:
                    where = ((x + dx) % 4, (y + dy) % 4, node * 2 + (z + dz) % 2)
                    mates.append((dz * 16 + dy * 4 + dx, where, device(*where, core)))
    column = [device(x, y, (z + dz) % 8, pair) for dz in range(8)]
    along_x = [device((x + d) % 4, y, z, core) for d in range(4)]
    along_y = [device(x, (y + d) % 4, z, core) for d in range(4)]
    partners = [who for _, _, who in mates] + [other]
    partners += [
        device(x, y, ((node + dn) % 4) * 2 + dz, c) for dn in range(1, 4) for dz in range(2) for c in range(2)
    ]
    partners.append(device(x, y, node * 2 + (z + 1) % 2, 1 - core))
    barrier = pltpu.get_barrier_semaphore()
    for partner in partners:
        pl.semaphore_signal(barrier, inc=1, device_id=partner, device_id_type=MESH)

    loads[0].wait()
    own[0:ROWS, :] = omega[...].astype(F32).T.astype(BF16)
    loads[1].wait()
    columns = features(points[...].astype(F32), 1.0, False).astype(BF16)
    own[256:272, :] = columns[:, :128]
    own[272:288, :] = columns[:, 128:]
    halves = (pl.ds(0, SPAN // 2), pl.ds(SPAN // 2, SPAN // 2))
    pl.semaphore_wait(barrier, len(partners))

    from_below, from_above = 24 * (z % 2), 24 * ((z + 1) % 2)
    hops = {}

    def hop(ref, slot, key, half, who):
        hops[key, half] = send(
            ref.at[halves[half]], blocks.at[slot, halves[half]],
            hop_send.at[key, half], hop_recv.at[key, half], who,
        )

    for step in range(2):
        hop(own, from_above, 7, step, upward)
        hop(own, from_below, 1, 1 - step, downward)

    for copy in loads[2:]:
        copy.wait()
    local = tree_order[...] % ROWS
    lane = lax.broadcasted_iota(jnp.int32, (ROWS, ROWS), 0)
    pick = jnp.where(lane == local, 1.0, 0.0).astype(BF16)
    mine = jnp.dot(points[...], pick, preferred_element_type=F32)
    own_rows[...] = features(mine, 4.0, True).astype(BF16)
    own_lists[...] = jnp.zeros_like(own_lists)
    own_lists[0:1, 0:16] = siblings[...]
    own_lists[1:2, 0:32] = cousins[...]
    small = []
    for kind, (at, line) in enumerate(((x, along_x), (y, along_y))):
        row_points[kind, at, core] = own_rows[...]
        lists[kind, at] = own_lists[...]
        for d in range(1, 4):
            target = row_points.at[kind, at, core]
            small.append(send(own_rows, target, rows_send.at[kind, d], rows_recv.at[kind, d], line[d]))
            target = lists.at[kind, at]
            small.append(send(own_lists, target, list_send.at[kind, d], list_recv.at[kind, d], line[d]))
    parts[...] = jnp.zeros_like(parts)

    plus, minus = (above, right), (below, left_side)
    outs, fars = {}, {}

    def fan_out(k, dz, half):
        kind = KIND[dz]
        block = blocks.at[SLOT[dz, 0], halves[half]]
        for side, (at, who) in enumerate(((SLOT[dz, 3], plus[kind]), (SLOT[dz, 1], minus[kind]))):
            outs[k, side, half] = send(
                block, blocks.at[at, halves[half]], out_send.at[k, side, half], out_recv.at[k, side, half], who
            )

    def relay(k, dz):
        kind = KIND[dz]
        for side, (at, who) in enumerate(((SLOT[dz, 3], plus[kind]), (SLOT[dz, 1], minus[kind]))):
            outs[k, side, side].wait_recv()
            fars[k, side] = send(
                blocks.at[at, halves[side]], blocks.at[SLOT[dz, 2], halves[side]],
                far_send.at[k, side], far_recv.at[k, side], who,
            )

    def landed(*ks):
        for k in ks:
            for side in range(2):
                outs[k, side, 1 - side].wait_recv()

    def passed(*ks):
        for k in ks:
            for side in range(2):
                fars[k, side].wait_recv()

    for step in range(2):
        hops[7, step].wait_recv()
        hop(blocks.at[from_below], SLOT[6, 0], 6, step, upward)
        hops[1, 1 - step].wait_recv()
        hop(blocks.at[from_above], SLOT[2, 0], 2, 1 - step, downward)
    for half in range(2):
        fan_out(0, MATE, half)
    for copy in small:
        copy.wait_recv()
    swap_rows = send(row_points.at[:, :, core], row_points.at[:, :, core], rows_send.at[0, 0], rows_recv.at[0, 0], other)
    make_masks(lists, near_mask, far_mask, x, y, z)
    for step in range(2):
        hops[6, step].wait_recv()
        hop(blocks.at[SLOT[6, 0]], SLOT[5, 0], 5, step, upward)
        fan_out(1, 6, step)
        hops[2, 1 - step].wait_recv()
        hop(blocks.at[SLOT[2, 0]], SLOT[3, 0], 3, 1 - step, downward)
        fan_out(2, 2, 1 - step)
    swap_rows.wait()
    for r in range(8):
        for half in range(2):
            rows[r, half * ROWS : (half + 1) * ROWS, :] = row_points[r // 4, r % 4, half].astype(F32).T.astype(BF16)

    def kernel_tile(r, use, tile):
        columns = jnp.concatenate(
            [blocks[2 * use + k, at : at + 16, :] for k in range(2) for at in (256, 272)], axis=1
        )
        exponent = jnp.dot(rows[r], columns, preferred_element_type=F32)
        tile[...] = jnp.exp(exponent).astype(BF16)

    def add(kind, at, use, tile):
        r = kind * 4 + at
        weights = []
        for k in range(2):
            slot = 2 * use + k
            values = blocks[slot, 0:ROWS, :]
            near = near_mask[r, pl.ds(slot, 1), :].astype(BF16)
            far = far_mask[r, pl.ds(slot, 1), :].astype(BF16)
            weights.append(jnp.concatenate([values * near, values * far], axis=1))
        terms = jnp.dot(tile[...], jnp.concatenate(weights, axis=0), preferred_element_type=F32)
        parts[0, kind, at] += terms[0:ROWS]
        parts[1, kind, at] += terms[ROWS:]

    def batch(kind, count, item):
        at, use = item(0)
        kernel_tile(kind * 4 + at, use, even_tile)

        def two_steps(step, carry):
            at0, use0 = item(2 * step)
            at1, use1 = item(2 * step + 1)
            at2, use2 = item(2 * step + 2)
            kernel_tile(kind * 4 + at1, use1, odd_tile)
            add(kind, at0, use0, even_tile)
            kernel_tile(kind * 4 + at2, use2, even_tile)
            add(kind, at1, use1, odd_tile)
            return carry

        lax.fori_loop(0, (count - 1) // 2, two_steps, 0)
        if count % 2:
            add(kind, *item(count - 1), even_tile)
        else:
            at, use = item(count - 1)
            kernel_tile(kind * 4 + at, use, odd_tile)
            add(kind, *item(count - 2), even_tile)
            add(kind, at, use, odd_tile)

    batch(1, 4, lambda i: (i, 0))
    relay(0, MATE)
    hops[5, 0].wait_recv()
    hop(blocks.at[SLOT[5, 0]], SLOT[4, 0], 4, 0, upward)
    fan_out(3, 5, 0)
    hops[3, 1].wait_recv()
    hop(blocks.at[SLOT[3, 0]], SLOT[4, 0], 4, 1, downward)
    fan_out(4, 3, 1)
    hops[5, 1].wait_recv()
    fan_out(3, 5, 1)
    hops[3, 0].wait_recv()
    fan_out(4, 3, 0)
    batch(0, 4, lambda i: (i, 1))
    relay(1, 6)
    relay(2, 2)
    for half in range(2):
        hops[4, half].wait_recv()
        fan_out(5, 4, half)
    landed(0, 1)
    batch(1, 8, lambda i: (i % 4, 2 + i // 4))
    relay(3, 5)
    relay(4, 3)
    relay(5, 4)
    landed(4)
    passed(0, 1)
    batch(1, 8, lambda i: (i % 4, 4 + i // 4))
    passed(4)
    batch(1, 4, lambda i: (i, 6))

    ahead, behind, across = (x + 1) % 4, (x + 3) % 4, (x + 2) % 4
    next_y, last_y = (y + 1) % 4, (y + 3) % 4
    order = [(across, (y + 2) % 4), (ahead, next_y), (behind, last_y), (x, y)]
    swap = {}

    def give(step, kind):
        at = order[step][kind]
        swap[step, kind] = send(
            parts.at[1 - core, kind, at], other_core.at[kind, at],
            core_send.at[kind, step], core_recv.at[kind, step], other,
        )


    def partial(step, kind):
        swap[step, kind].wait_recv()
        at = order[step][kind]
        return parts[core, kind, at] + other_core[kind, at]

    forward, backward = (right, above), (left_side, below)
    lower, upper = pl.ds(0, 128), pl.ds(128, 128)
    relays, nears = {}, []

    def pass_on(kind, side, first, rows_of, who):
        ref = near_out.at[kind, side, rows_of]
        target = near_in.at[kind, side, rows_of]
        nears.append(send(ref, target, near_sems.at[0, kind, side, first], near_sems.at[1, kind, side, first], who))

    def start_sum(kind):
        relay_out[kind] = partial(0, kind).astype(LINK)
        for side, (rows_of, who) in enumerate(((lower, forward[kind]), (upper, backward[kind]))):
            relays[kind, side] = send(
                relay_out.at[kind, rows_of], relay_in.at[kind, side],
                relay_sems.at[0, kind, side], relay_sems.at[1, kind, side], who,
            )

    def middle_sum(kind, side):
        near_out[kind, side] = partial(1 + side, kind).astype(LINK)
        pass_on(kind, side, 0, (upper, lower)[side], (forward, backward)[side][kind])

    def end_sum(kind):
        relays[kind, 0].wait_recv()
        near_out[kind, 0, 0:128, :] = (
            parts[core, kind, order[1][kind], 0:128, :]
            + other_core[kind, order[1][kind], 0:128, :]
            + relay_in[kind, 0].astype(F32)
        ).astype(LINK)
        pass_on(kind, 0, 1, lower, forward[kind])
        relays[kind, 1].wait_recv()
        near_out[kind, 1, 128:256, :] = (
            parts[core, kind, order[2][kind], 128:256, :]
            + other_core[kind, order[2][kind], 128:256, :]
            + relay_in[kind, 1].astype(F32)
        ).astype(LINK)
        pass_on(kind, 1, 1, upper, backward[kind])

    for step in range(4):
        give(step, 1)
    landed(2, 3, 5)
    passed(2, 3, 5)

    def last_batch(step, first=0, count=5):
        at = order[step][0]
        batch(0, count, lambda i: (at, 7 + first + i))
        if first + count == 5:
            give(step, 0)

    last_batch(0)
    start_sum(1)
    middle_sum(1, 0)
    middle_sum(1, 1)
    last_batch(1)
    start_sum(0)
    end_sum(1)
    last_batch(2)
    middle_sum(0, 0)
    last_batch(3, 0, 3)
    middle_sum(0, 1)
    end_sum(0)
    last_batch(3, 3, 2)
    total = partial(3, 1) + partial(3, 0)
    first_row = (leaf * 2 + core) * ROWS
    row = lax.broadcasted_iota(jnp.int32, (ROWS, RANK), 0) + first_row
    picked = jnp.where(row == skeleton[pl.ds(node, 1), :], 1.0, 0.0)
    own_skeleton = jnp.dot(
        mine.astype(BF16), picked.astype(BF16), preferred_element_type=F32
    )
    for copy in nears:
        copy.wait_recv()
    for kind in range(2):
        for side in range(2):
            total = total + near_in[kind, side].astype(F32)
    rows_here = total

    def product(c, first):
        values = lax.dot_general(
            first, rows_here, (((0,), (0,)), ((), ())), precision=HIGH, preferred_element_type=F32
        )
        table[c, 0] = values[:, 0:128]
        table[c, 1] = values[:, 128:256]

    def swap_table(c):
        return send(table.at[c, 1 - core], sums.at[c], table_sems.at[0, c], table_sems.at[1, c], other)

    def spread_table(c):
        swaps[c].wait_recv()
        sums[c] += table[c, core]
        copies = []
        for slot, where, who in far_first:
            copies.append(
                send(chunk(c, where), pieces.at[c, slot], piece_send.at[c, slot], piece_recv.at[c, slot], who)
            )
        return copies

    def chunk(c, where):
        first = (where[0] * 8 + where[1] * 2 + where[2] % 2) * 8
        return sums.at[c, pl.ds(pl.multiple_of(first, 8), 8)]

    def reach(mate):
        return sum(min(d, 4 - d) for d in (mate[0] // 16, mate[0] // 4 % 4, mate[0] % 4))

    def drop(c, dz):
        return pltpu.make_async_remote_copy(
            src_ref=piece.at[c],
            dst_ref=landing.at[c, z % 4, core],
            send_sem=z_send.at[c, dz],
            recv_sem=z_recv.at[c, z % 4, core],
            device_id=column[dz],
            device_id_type=MESH,
        )

    def collect_chunk(c):
        result = chunk(c, (x, y, z))[...]
        for copy in spreads[c]:
            copy.wait_recv()
        for slot, _, _ in mates:
            result = result + pieces[c, slot]
        piece[c] = result
        for dz in (4, 3, 5, 2, 6, 1, 7):
            drop(c, dz).start()

        @pl.when(pair == core)
        def _():
            landing[c, z % 4, core] = piece[c]

        @pl.when(pair != core)
        def _():
            drop(c, 0).start()

    far_first = sorted(mates, key=reach, reverse=True)
    product(0, rows_here)
    table[0, 0, 128:256, :] = jnp.zeros((128, 128), F32)
    table[0, 0, 128:136, :] = own_skeleton[:, 0:128]
    table[0, 0, 136:144, :] = own_skeleton[:, 128:256]
    swaps = [swap_table(0)]
    product(1, picked)
    swaps.append(swap_table(1))
    spreads = [spread_table(0)]
    spreads.append(spread_table(1))
    collect_chunk(0)
    collect_chunk(1)

    def fan(ref, sems, first, line):
        return [
            send(ref, ref, sems.at[0, first + d - 1], sems.at[1, first + d - 1], line[d]) for d in (2, 1, 3)
        ]

    def first_leg(c):
        for plane in range(4):
            for half in range(2):

                @pl.when((core * 4 + plane != z) | (core != half))
                def _(plane=plane, half=half):
                    pltpu.make_async_remote_copy(
                        src_ref=piece.at[c],
                        dst_ref=landing.at[c, plane, half],
                        send_sem=z_send.at[c, 0],
                        recv_sem=z_recv.at[c, plane, half],
                        device_id=other,
                        device_id_type=MESH,
                    ).wait_recv()

        full_a[c, x, y] = landing[c, :, 0]
        full_b[c, y, x] = landing[c, :, 1]
        return fan(full_a.at[c, x, y], y_sems, 6 * c, along_y) + fan(full_b.at[c, y, x], x_sems, 6 * c, along_x)

    def second_leg(c, copies):
        for copy in copies:
            copy.wait_recv()
        return fan(full_a.at[c, x], x_sems, 6 * c + 3, along_x) + fan(full_b.at[c, y], y_sems, 6 * c + 3, along_y)

    legs = [first_leg(0)]
    legs.append(second_leg(0, legs[0]))
    legs.append(first_leg(1))
    for copy in legs[1]:
        copy.wait_recv()

    row = lax.broadcasted_iota(jnp.int32, (RANK, RANK), 0)
    col = lax.broadcasted_iota(jnp.int32, (RANK, RANK), 1)
    skeleton_points, sizes = [], []
    for n in range(2):
        for at_x in range(4):
            for at_y in range(4):
                span = pl.ds(at_x * 64 + at_y * 16, 16)
                planes = pl.ds(2 * n, 2)
                work[n, span, 0:128] = full_a[0, at_x, at_y, planes].reshape(16, 128)
                work[n, span, 128:256] = full_b[0, at_y, at_x, planes].reshape(16, 128)
        skeleton_points.append(
            jnp.concatenate([work[n, 128:136, 0:128], work[n, 136:144, 0:128]], axis=1)
        )
        gram = work[n]
        on_diagonal = jnp.where(row == col, gram, 0.0)
        trace = jnp.sum(jnp.sum(on_diagonal, axis=0, keepdims=True), axis=1, keepdims=True)
        work[n] = gram * (1.0 / trace) + jnp.where(row == col, 0.01, 0.0)
        sizes.append(lax.rsqrt(trace))

    row_side = features(skeleton_points[0], 4.0, True).T.astype(BF16)
    col_side = features(skeleton_points[1], 1.0, False).astype(BF16)
    kernel_skel = jnp.exp(jnp.dot(row_side, col_side, preferred_element_type=F32))

    lane8 = lax.broadcasted_iota(jnp.int32, (8, 128), 1)
    row8 = lax.broadcasted_iota(jnp.int32, (8, 128), 0)
    group8 = (lane8 // 64) * 64
    lane = lax.broadcasted_iota(jnp.int32, (64, 128), 1)
    for p in range(4):
        top = 64 * p
        aligned = (top // 128) * 128
        packed = []
        for n in range(2):
            block = work[n, top : top + 64, aligned : aligned + 128]
            packed.append(pltpu.roll(block, 64, 1) if (64 * n - top) % 128 else block)
        packed = jnp.where(lane < 64, packed[0], packed[1])
        left = [packed[8 * g : 8 * g + 8] for g in range(8)]
        inverse = [jnp.where(lane8 - group8 == row8 + 8 * g, 1.0, 0.0) for g in range(8)]
        for j in range(0, 64, 4):
            own, inner = j // 8, j % 8
            spread = {
                g: [
                    jnp.take_along_axis(left[g], group8 + (j + t), axis=1, mode="promise_in_bounds")
                    for t in range(4)
                ]
                for g in range(own, 8)
            }

            def line(tile, t, inner=inner):
                return jnp.broadcast_to(tile[inner + t : inner + t + 1, :], (8, 128))

            solve = pivots(lambda t, u: line(spread[own][u], t))
            left_rows = solve([line(left[own], t) for t in range(4)])
            inverse_rows = solve([line(inverse[own], t) for t in range(4)])
            for g in range(own, 8):
                if g == own and inner == 4:
                    continue
                factors = solve(spread[g])
                if g == own:
                    factors = [jnp.where(row8 > 3, factor, 0.0) for factor in factors]
                left[g] = left[g] - fold(factors, left_rows)
                inverse[g] = inverse[g] - fold(factors, inverse_rows)
            for t in range(4):
                inverse[own] = jnp.where(row8 == inner + t, inverse_rows[t], inverse[own])
        packed = jnp.concatenate(inverse, axis=0)
        diagonal = jnp.concatenate([jnp.where(lane < 64, packed, 0.0), jnp.where(lane < 64, 0.0, packed)], axis=0)
        stacked = jnp.concatenate([work[n, top : top + 64, :] for n in range(2)], axis=0)
        srow = lax.broadcasted_iota(jnp.int32, (128, RANK), 0)
        scol = lax.broadcasted_iota(jnp.int32, (128, RANK), 1)
        identity = jnp.where(srow % 64 == scol % 64, 1.0, 0.0)
        stacked = jnp.where(scol // 64 == p, identity, stacked)
        solved = jnp.dot(diagonal, stacked, precision=HIGH, preferred_element_type=F32)
        done = jnp.where(scol < top + 64, solved, 0.0)
        for n in range(2):
            work[n, top : top + 64, :] = done[64 * n : 64 * n + 64]
        rest = RANK - top - 64
        if rest:
            turned = solved.T[top + 64 :, :]
            tlane = lax.broadcasted_iota(jnp.int32, (rest, 128), 1)
            tcol = lax.broadcasted_iota(jnp.int32, (rest, RANK), 1)
            for n in range(2):
                update = jnp.dot(
                    jnp.where(tlane // 64 == n, turned, 0.0), solved,
                    precision=HIGH, preferred_element_type=F32,
                )
                work[n, top + 64 :, :] = jnp.where(tcol // 64 == p, 0.0, work[n, top + 64 :, :]) - update
        if p == 0:
            legs.append(second_leg(1, legs[2]))
        if p == 2:
            for copy in legs[3]:
                copy.wait_recv()
            for n in range(2):
                for at_x in range(4):
                    for at_y in range(4):
                        span = pl.ds(at_x * 64 + at_y * 16, 16)
                        planes = pl.ds(2 * n, 2)
                        chosen[n, span, 0:128] = full_a[1, at_x, at_y, planes].reshape(16, 128)
                        chosen[n, span, 128:256] = full_b[1, at_y, at_x, planes].reshape(16, 128)
            right_part = jnp.dot(kernel_skel, chosen[1], precision=HIGH, preferred_element_type=F32)
            middle = lax.dot_general(
                chosen[0], right_part, (((0,), (0,)), ((), ())), precision=HIGH, preferred_element_type=F32
            )

    size = jnp.where(node % 2 == 0, sizes[0], sizes[1])
    factor_out[...] = work[node % 2] * size
    factor_copy = send(factor_out, factor_in, factor_sems.at[0], factor_sems.at[1], other)
    last = (((1,), (1,)), ((), ()))
    half = jnp.dot(work[0], middle, precision=HIGH, preferred_element_type=F32)
    coupling_out[...] = ((16384.0 / math.sqrt(RANK)) * sizes[0] * sizes[1]) * lax.dot_general(
        half, work[1], last, precision=HIGH, preferred_element_type=F32
    )
    coupling_copy = send(
        coupling_out, coupling.at[core], coupling_sems.at[0], coupling_sems.at[1], other
    )
    results = [pltpu.make_async_copy(coupling_out, coupling.at[core], result_sems.at[0])]
    results[0].start()
    factor_copy.wait_recv()
    factor = jnp.where(node // 2 == core, factor_out[...], factor_in[...])
    basis_out[...] = 128.0 * lax.dot_general(
        rows_here, factor, last, precision=HIGH, preferred_element_type=F32
    )
    results.append(pltpu.make_async_copy(basis_out, basis, result_sems.at[1]))
    results[1].start()
    factor_copy.wait_send()
    coupling_copy.wait()
    for copy in results:
        copy.wait()

    for copy in list(relays.values()) + nears + list(swap.values()) + small + sum(legs, []):
        copy.wait_send()
    for c in range(2):
        swaps[c].wait_send()
        for copy in spreads[c]:
            copy.wait_send()
        for dz in range(1, 8):
            drop(c, dz).wait_send()

        @pl.when(pair != core)
        def _(c=c):
            drop(c, 0).wait_send()

    for copy in list(hops.values()) + list(outs.values()) + list(fars.values()):
        copy.wait_send()


def whole(*arguments):
    dma = pltpu.SemaphoreType.DMA

    def block(*shape, kind=F32):
        return pltpu.VMEM(shape, kind)

    i32 = jnp.int32
    return pl.pallas_call(
        whole_kernel,
        out_shape=(
            jax.ShapeDtypeStruct((ROWS, RANK), F32),
            jax.ShapeDtypeStruct((2, RANK, RANK), F32),
        ),
        in_specs=[HBM] * 6,
        out_specs=(HBM,) * 2,
        scratch_shapes=[
            block(FEATS, ROWS, kind=BF16), block(SAMPLES, ROWS, kind=BF16), block(1, ROWS, kind=i32),
            block(1, 16, kind=i32), block(1, 32, kind=i32), block(4, RANK, kind=i32), dma((6,)),
            block(25, SPAN, 128, kind=BF16), block(2, 4, 2, 16, ROWS, kind=BF16), block(2, 4, 8, 128, kind=i32),
            block(SPAN, 128, kind=BF16), block(16, ROWS, kind=BF16), block(8, 128, kind=i32),
            block(8, 32, 128), block(8, 32, 128), block(8, 2 * ROWS, 16, kind=BF16),
            block(2 * ROWS, 2 * ROWS, kind=BF16), block(2 * ROWS, 2 * ROWS, kind=BF16), block(2, 2, 4, ROWS, RANK),
            dma((8, 2)), dma((8, 2)), dma((6, 2, 2)), dma((6, 2, 2)), dma((6, 2)), dma((6, 2)),
            dma((2, 4)), dma((2, 4)), dma((2, 4)), dma((2, 4)),
            block(2, 4, ROWS, RANK), block(2, ROWS, RANK, kind=LINK), block(2, 2, 128, RANK, kind=LINK),
            block(2, 2, ROWS, RANK, kind=LINK), block(2, 2, ROWS, RANK, kind=LINK),
            block(2, 2, RANK, 128), block(2, RANK, 128), block(2, 8, 128), block(2, 32, 8, 128),
            block(2, 4, 2, 8, 128), block(2, 4, 4, 4, 8, 128), block(2, 4, 4, 4, 8, 128),
            dma((2, 4)), dma((2, 4)), dma((2, 2, 2)), dma((2, 2, 2, 2)), dma((2, 2)), dma((2, 32)), dma((2, 32)),
            dma((2, 8)), dma((2, 4, 2)), dma((2, 12)), dma((2, 12)),
            block(2, RANK, RANK), block(2, RANK, RANK), block(RANK, RANK), block(RANK, RANK), block(RANK, RANK),
            block(ROWS, RANK), dma((2,)), dma((2,)), dma((2,)),
        ],
        compiler_params=pltpu.CompilerParams(
            collective_id=0, has_side_effects=True, vmem_limit_bytes=VMEM_LIMIT
        ),
        name="whole",
    )(*arguments)


def body(points, omega, tree_order, sibling_blocks, cousin_blocks, skeleton):
    return whole(points, omega, tree_order.reshape(1, ROWS), sibling_blocks, cousin_blocks, skeleton)


def solution(mesh):
    return jax.shard_map(
        body,
        mesh=mesh,
        in_specs=(
            P(None, ("leaf", "sub")),
            P(None, ("leaf", "sub")),
            P(("leaf", "sub")),
            P("leaf", None),
            P("leaf", None),
            P(),
        ),
        out_specs=(P(("leaf", "sub"), None), P()),
        check_vma=False,
    )
```

```python
import math

import jax
import jax.numpy as jnp
from jax import lax
from jax.experimental import pallas as pl
from jax.experimental.pallas import tpu as pltpu
from jax.sharding import PartitionSpec as P

MESH = pl.DeviceIdType.MESH
HIGH = lax.Precision.HIGH
HIGHEST = lax.Precision.HIGHEST
F32 = jnp.float32
BF16 = jnp.bfloat16
HBM = pl.BlockSpec(memory_space=pltpu.HBM)
VMEM = pl.BlockSpec(memory_space=pltpu.VMEM)

ROWS = 256
FEATS = 8
SAMPLES = 128
RANK = 256
SPAN = 288
LINK = BF16
VMEM_LIMIT = 40 << 20


def place():
    leaf = lax.axis_index("leaf")
    core = lax.axis_index("sub")
    return leaf % 4, (leaf // 4) % 4, leaf // 16, core


def device(x, y, z, core):
    return (z * 16 + y * 4 + x, core)


def send(src, dst, send_sem, recv_sem, target):
    copy = pltpu.make_async_remote_copy(
        src_ref=src,
        dst_ref=dst,
        send_sem=send_sem,
        recv_sem=recv_sem,
        device_id=target,
        device_id_type=MESH,
    )
    copy.start()
    return copy


def features(coordinates, scale, ones_first):
    norm = -2.0 * jnp.sum(coordinates * coordinates, axis=0, keepdims=True)
    first = norm.astype(BF16).astype(F32)
    second = (norm - first).astype(BF16).astype(F32)
    third = norm - first - second
    row = lax.broadcasted_iota(jnp.int32, coordinates.shape, 0)
    start = 3 if ones_first else 0
    other = 0 if ones_first else 3
    tail = jnp.where((row >= other) & (row < other + 3), 1.0, 0.0)
    tail = jnp.where(row == start, first, tail)
    tail = jnp.where(row == start + 1, second, tail)
    tail = jnp.where(row == start + 2, third, tail)
    return jnp.concatenate([scale * coordinates, tail], axis=0)


def fold(factors, lines):
    terms = [factor * values for factor, values in zip(factors, lines, strict=True)]
    while len(terms) > 1:
        terms = [a + b for a, b in zip(terms[::2], terms[1::2], strict=True)]
    return terms[0]


def pivots(entry):
    left = {(t, u): entry(t, u) for t in range(8) for u in range(t + 1)}
    scale, lower = {}, {}
    for t in range(0, 8, 2):
        a, b, c = left[t, t], left[t + 1, t], left[t + 1, t + 1]
        scale[t] = lax.rsqrt(a)
        lower[t + 1, t] = b * scale[t]
        scale[t + 1] = a * lax.rsqrt(a * (a * c - b * b))
        for i in range(t + 2, 8):
            lower[i, t] = left[i, t] * scale[t]
            lower[i, t + 1] = (left[i, t + 1] - lower[i, t] * lower[t + 1, t]) * scale[t + 1]
        for i in range(t + 2, 8):
            for k in range(t + 2, i + 1):
                left[i, k] = left[i, k] - (lower[i, t] * lower[k, t] + lower[i, t + 1] * lower[k, t + 1])

    def solve(values):
        values = list(values)
        for t in range(0, 8, 2):
            values[t] = values[t] * scale[t]
            values[t + 1] = (values[t + 1] - values[t] * lower[t + 1, t]) * scale[t + 1]
            for i in range(t + 2, 8):
                values[i] = values[i] - (values[t] * lower[i, t] + values[t + 1] * lower[i, t + 1])
        return values

    return solve


MATE = 0
USE = [
    (MATE, 0), (6, 0), (2, 0), (5, 0), (MATE, 1), (MATE, 3), (6, 1), (6, 3),
    (3, 0), (3, 1), (MATE, 2), (6, 2), (3, 3), (3, 2), (2, 1), (2, 3),
    (5, 1), (5, 3), (2, 2), (5, 2), (4, 0), (4, 1), (4, 3), (4, 2),
]
SLOT = {block: slot for slot, block in enumerate(USE)}
KIND = {MATE: 1, 6: 1, 3: 1, 2: 0, 5: 0, 4: 0}


def make_masks(lists, near_mask, far_mask, x, y, z):
    lane = lax.broadcasted_iota(jnp.int32, (8, 128), 1)
    group = lax.broadcasted_iota(jnp.int32, (8, 128), 0) // 4
    named = jnp.full((8, 128), -1, jnp.int32)
    near = jnp.zeros((8, 128), F32)
    for slot, (dz, along) in enumerate(USE):
        plane = (z + (dz or 7 - 6 * (z % 2))) % 8
        if KIND[dz]:
            block = plane * 16 + y * 4 + (x + along) % 4
        else:
            block = plane * 16 + ((y + along) % 4) * 4 + x
        named = jnp.where((lane == slot) & (group == KIND[dz]), block, named)
        near = jnp.where(lane == slot, jnp.where(plane // 4 == z // 4, 1.0, 0.0), near)
    named = named.astype(F32)
    hit = jnp.zeros((8, 128), F32)
    for side, length in ((0, 16), (1, 32)):
        entries = jnp.concatenate(
            [lists[k, at, side : side + 1, :] for k in range(2) for at in range(4)], axis=0
        ).astype(F32)
        for e in range(length):
            hit = jnp.where(named == jnp.broadcast_to(entries[:, e : e + 1], (8, 128)), 1.0, hit)
    near_hit, far_hit = (hit * near).T, (hit * (1.0 - near)).T
    for r in range(8):
        near_mask[r] = jnp.broadcast_to(near_hit[0:32, r : r + 1], (32, 128))
        far_mask[r] = jnp.broadcast_to(far_hit[0:32, r : r + 1], (32, 128))


def whole_kernel(
    points_in, omega_in, order_in, siblings_in, cousins_in, skeleton_in,
    basis, coupling,
    points, omega, tree_order, siblings, cousins, skeleton, load_sems,
    blocks, row_points, lists, own, own_rows, own_lists, near_mask, far_mask, rows, even_tile, odd_tile, parts,
    hop_send, hop_recv, out_send, out_recv, far_send, far_recv, rows_send, rows_recv, list_send, list_recv,
    other_core, relay_out, relay_in, near_out, near_in, table, sums, piece, pieces, landing, full_a, full_b,
    core_send, core_recv, relay_sems, near_sems, table_sems, piece_send, piece_recv,
    z_send, z_recv, y_sems, x_sems,
    work, chosen, factor_out, factor_in, factor_sems, coupling_sems,
):
    loads = [
        pltpu.make_async_copy(source, target, load_sems.at[k])
        for k, (source, target) in enumerate(
            [
                (omega_in, omega),
                (points_in, points),
                (order_in, tree_order),
                (siblings_in, siblings),
                (cousins_in, cousins),
                (skeleton_in, skeleton),
            ]
        )
    ]
    for copy in loads:
        copy.start()
    x, y, z, core = place()
    leaf = z * 16 + y * 4 + x
    node, pair = z // 2, z // 4
    other = device(x, y, z, 1 - core)
    right, left_side = device((x + 1) % 4, y, z, core), device((x + 3) % 4, y, z, core)
    above, below = device(x, (y + 1) % 4, z, core), device(x, (y + 3) % 4, z, core)
    upward, downward = device(x, y, (z + 1) % 8, core), device(x, y, (z + 7) % 8, core)
    mates = []
    for dz in range(2):
        for dy in range(4):
            for dx in range(4):
                if dz or dy or dx:
                    where = ((x + dx) % 4, (y + dy) % 4, node * 2 + (z + dz) % 2)
                    mates.append((dz * 16 + dy * 4 + dx, where, device(*where, core)))
    column = [device(x, y, (z + dz) % 8, pair) for dz in range(8)]
    along_x = [device((x + d) % 4, y, z, core) for d in range(4)]
    along_y = [device(x, (y + d) % 4, z, core) for d in range(4)]
    partners = [who for _, _, who in mates] + [other]
    partners += [
        device(x, y, ((node + dn) % 4) * 2 + dz, c) for dn in range(1, 4) for dz in range(2) for c in range(2)
    ]
    partners.append(device(x, y, node * 2 + (z + 1) % 2, 1 - core))
    barrier = pltpu.get_barrier_semaphore()
    for partner in partners:
        pl.semaphore_signal(barrier, inc=1, device_id=partner, device_id_type=MESH)

    loads[0].wait()
    own[0:ROWS, :] = omega[...].astype(F32).T.astype(BF16)
    loads[1].wait()
    columns = features(points[...].astype(F32), 1.0, False).astype(BF16)
    own[256:272, :] = columns[:, :128]
    own[272:288, :] = columns[:, 128:]
    halves = (pl.ds(0, SPAN // 2), pl.ds(SPAN // 2, SPAN // 2))
    pl.semaphore_wait(barrier, len(partners))

    from_below, from_above = 24 * (z % 2), 24 * ((z + 1) % 2)
    hops = {}

    def hop(ref, slot, key, half, who):
        hops[key, half] = send(
            ref.at[halves[half]], blocks.at[slot, halves[half]],
            hop_send.at[key, half], hop_recv.at[key, half], who,
        )

    for step in range(2):
        hop(own, from_above, 7, step, upward)
        hop(own, from_below, 1, 1 - step, downward)

    for copy in loads[2:]:
        copy.wait()
    local = tree_order[...] % ROWS
    lane = lax.broadcasted_iota(jnp.int32, (ROWS, ROWS), 0)
    pick = jnp.where(lane == local, 1.0, 0.0).astype(BF16)
    mine = jnp.dot(points[...], pick, preferred_element_type=F32)
    own_rows[...] = features(mine, 4.0, True).astype(BF16)
    own_lists[...] = jnp.zeros_like(own_lists)
    own_lists[0:1, 0:16] = siblings[...]
    own_lists[1:2, 0:32] = cousins[...]
    small = []
    for kind, (at, line) in enumerate(((x, along_x), (y, along_y))):
        row_points[kind, at, core] = own_rows[...]
        lists[kind, at] = own_lists[...]
        for d in range(1, 4):
            target = row_points.at[kind, at, core]
            small.append(send(own_rows, target, rows_send.at[kind, d], rows_recv.at[kind, d], line[d]))
            target = lists.at[kind, at]
            small.append(send(own_lists, target, list_send.at[kind, d], list_recv.at[kind, d], line[d]))
    parts[...] = jnp.zeros_like(parts)

    plus, minus = (above, right), (below, left_side)
    outs, fars = {}, {}

    def fan_out(k, dz, half):
        kind = KIND[dz]
        block = blocks.at[SLOT[dz, 0], halves[half]]
        for side, (at, who) in enumerate(((SLOT[dz, 3], plus[kind]), (SLOT[dz, 1], minus[kind]))):
            outs[k, side, half] = send(
                block, blocks.at[at, halves[half]], out_send.at[k, side, half], out_recv.at[k, side, half], who
            )

    def relay(k, dz):
        kind = KIND[dz]
        for side, (at, who) in enumerate(((SLOT[dz, 3], plus[kind]), (SLOT[dz, 1], minus[kind]))):
            outs[k, side, side].wait_recv()
            fars[k, side] = send(
                blocks.at[at, halves[side]], blocks.at[SLOT[dz, 2], halves[side]],
                far_send.at[k, side], far_recv.at[k, side], who,
            )

    def landed(*ks):
        for k in ks:
            for side in range(2):
                outs[k, side, 1 - side].wait_recv()

    def passed(*ks):
        for k in ks:
            for side in range(2):
                fars[k, side].wait_recv()

    for step in range(2):
        hops[7, step].wait_recv()
        hop(blocks.at[from_below], SLOT[6, 0], 6, step, upward)
        hops[1, 1 - step].wait_recv()
        hop(blocks.at[from_above], SLOT[2, 0], 2, 1 - step, downward)
    for half in range(2):
        fan_out(0, MATE, half)
    for copy in small:
        copy.wait_recv()
    swap_rows = send(row_points.at[:, :, core], row_points.at[:, :, core], rows_send.at[0, 0], rows_recv.at[0, 0], other)
    make_masks(lists, near_mask, far_mask, x, y, z)
    for step in range(2):
        hops[6, step].wait_recv()
        hop(blocks.at[SLOT[6, 0]], SLOT[5, 0], 5, step, upward)
        fan_out(1, 6, step)
        hops[2, 1 - step].wait_recv()
        hop(blocks.at[SLOT[2, 0]], SLOT[3, 0], 3, 1 - step, downward)
        fan_out(2, 2, 1 - step)
    swap_rows.wait()
    for r in range(8):
        for half in range(2):
            rows[r, half * ROWS : (half + 1) * ROWS, :] = row_points[r // 4, r % 4, half].astype(F32).T.astype(BF16)

    def kernel_tile(r, use, tile):
        columns = jnp.concatenate(
            [blocks[2 * use + k, at : at + 16, :] for k in range(2) for at in (256, 272)], axis=1
        )
        exponent = jnp.dot(rows[r], columns, preferred_element_type=F32)
        tile[...] = jnp.exp(exponent).astype(BF16)

    def add(kind, at, use, tile):
        r = kind * 4 + at
        weights = []
        for k in range(2):
            slot = 2 * use + k
            values = blocks[slot, 0:ROWS, :]
            near = near_mask[r, pl.ds(slot, 1), :].astype(BF16)
            far = far_mask[r, pl.ds(slot, 1), :].astype(BF16)
            weights.append(jnp.concatenate([values * near, values * far], axis=1))
        terms = jnp.dot(tile[...], jnp.concatenate(weights, axis=0), preferred_element_type=F32)
        parts[0, kind, at] += terms[0:ROWS]
        parts[1, kind, at] += terms[ROWS:]

    def batch(kind, count, item):
        at, use = item(0)
        kernel_tile(kind * 4 + at, use, even_tile)

        def two_steps(step, carry):
            at0, use0 = item(2 * step)
            at1, use1 = item(2 * step + 1)
            at2, use2 = item(2 * step + 2)
            kernel_tile(kind * 4 + at1, use1, odd_tile)
            add(kind, at0, use0, even_tile)
            kernel_tile(kind * 4 + at2, use2, even_tile)
            add(kind, at1, use1, odd_tile)
            return carry

        lax.fori_loop(0, (count - 1) // 2, two_steps, 0)
        if count % 2:
            add(kind, *item(count - 1), even_tile)
        else:
            at, use = item(count - 1)
            kernel_tile(kind * 4 + at, use, odd_tile)
            add(kind, *item(count - 2), even_tile)
            add(kind, at, use, odd_tile)

    batch(1, 4, lambda i: (i, 0))
    relay(0, MATE)
    hops[5, 0].wait_recv()
    hop(blocks.at[SLOT[5, 0]], SLOT[4, 0], 4, 0, upward)
    fan_out(3, 5, 0)
    hops[3, 1].wait_recv()
    hop(blocks.at[SLOT[3, 0]], SLOT[4, 0], 4, 1, downward)
    fan_out(4, 3, 1)
    hops[5, 1].wait_recv()
    fan_out(3, 5, 1)
    hops[3, 0].wait_recv()
    fan_out(4, 3, 0)
    batch(0, 4, lambda i: (i, 1))
    relay(1, 6)
    relay(2, 2)
    for half in range(2):
        hops[4, half].wait_recv()
        fan_out(5, 4, half)
    landed(0, 1)
    batch(1, 8, lambda i: (i % 4, 2 + i // 4))
    relay(3, 5)
    relay(4, 3)
    relay(5, 4)
    landed(4)
    passed(0, 1)
    batch(1, 8, lambda i: (i % 4, 4 + i // 4))
    passed(4)
    batch(1, 4, lambda i: (i, 6))

    ahead, behind, across = (x + 1) % 4, (x + 3) % 4, (x + 2) % 4
    next_y, last_y = (y + 1) % 4, (y + 3) % 4
    order = [(across, (y + 2) % 4), (ahead, next_y), (behind, last_y), (x, y)]
    swap = {}

    def give(step, kind):
        at = order[step][kind]
        swap[step, kind] = send(
            parts.at[1 - core, kind, at], other_core.at[kind, at],
            core_send.at[kind, step], core_recv.at[kind, step], other,
        )


    def partial(step, kind):
        swap[step, kind].wait_recv()
        at = order[step][kind]
        return parts[core, kind, at] + other_core[kind, at]

    forward, backward = (right, above), (left_side, below)
    lower, upper = pl.ds(0, 128), pl.ds(128, 128)
    relays, nears = {}, []

    def pass_on(kind, side, first, rows_of, who):
        ref = near_out.at[kind, side, rows_of]
        target = near_in.at[kind, side, rows_of]
        nears.append(send(ref, target, near_sems.at[0, kind, side, first], near_sems.at[1, kind, side, first], who))

    def start_sum(kind):
        relay_out[kind] = partial(0, kind).astype(LINK)
        for side, (rows_of, who) in enumerate(((lower, forward[kind]), (upper, backward[kind]))):
            relays[kind, side] = send(
                relay_out.at[kind, rows_of], relay_in.at[kind, side],
                relay_sems.at[0, kind, side], relay_sems.at[1, kind, side], who,
            )

    def middle_sum(kind, side):
        near_out[kind, side] = partial(1 + side, kind).astype(LINK)
        pass_on(kind, side, 0, (upper, lower)[side], (forward, backward)[side][kind])

    def end_sum(kind):
        relays[kind, 0].wait_recv()
        near_out[kind, 0, 0:128, :] = (
            parts[core, kind, order[1][kind], 0:128, :]
            + other_core[kind, order[1][kind], 0:128, :]
            + relay_in[kind, 0].astype(F32)
        ).astype(LINK)
        pass_on(kind, 0, 1, lower, forward[kind])
        relays[kind, 1].wait_recv()
        near_out[kind, 1, 128:256, :] = (
            parts[core, kind, order[2][kind], 128:256, :]
            + other_core[kind, order[2][kind], 128:256, :]
            + relay_in[kind, 1].astype(F32)
        ).astype(LINK)
        pass_on(kind, 1, 1, upper, backward[kind])

    for step in range(4):
        give(step, 1)
    landed(2, 3, 5)
    passed(2, 3, 5)

    def last_batch(step, first=0, count=5):
        at = order[step][0]
        batch(0, count, lambda i: (at, 7 + first + i))
        if first + count == 5:
            give(step, 0)

    last_batch(0)
    start_sum(1)
    middle_sum(1, 0)
    middle_sum(1, 1)
    last_batch(1)
    start_sum(0)
    end_sum(1)
    last_batch(2)
    middle_sum(0, 0)
    last_batch(3, 0, 3)
    middle_sum(0, 1)
    end_sum(0)
    last_batch(3, 3, 2)
    total = partial(3, 1) + partial(3, 0)
    first_row = (leaf * 2 + core) * ROWS
    row = lax.broadcasted_iota(jnp.int32, (ROWS, RANK), 0) + first_row
    picked = jnp.where(row == skeleton[pl.ds(node, 1), :], 1.0, 0.0)
    own_skeleton = jnp.dot(
        mine.astype(BF16), picked.astype(BF16), preferred_element_type=F32
    )
    for copy in nears:
        copy.wait_recv()
    for kind in range(2):
        for side in range(2):
            total = total + near_in[kind, side].astype(F32)
    rows_here = total

    def product(c, first):
        values = lax.dot_general(
            first, rows_here, (((0,), (0,)), ((), ())), precision=HIGH, preferred_element_type=F32
        )
        table[c, 0] = values[:, 0:128]
        table[c, 1] = values[:, 128:256]

    def swap_table(c):
        return send(table.at[c, 1 - core], sums.at[c], table_sems.at[0, c], table_sems.at[1, c], other)

    def spread_table(c):
        swaps[c].wait_recv()
        sums[c] += table[c, core]
        copies = []
        for slot, where, who in far_first:
            copies.append(
                send(chunk(c, where), pieces.at[c, slot], piece_send.at[c, slot], piece_recv.at[c, slot], who)
            )
        return copies

    def chunk(c, where):
        first = (where[0] * 8 + where[1] * 2 + where[2] % 2) * 8
        return sums.at[c, pl.ds(pl.multiple_of(first, 8), 8)]

    def reach(mate):
        return sum(min(d, 4 - d) for d in (mate[0] // 16, mate[0] // 4 % 4, mate[0] % 4))

    def drop(c, dz):
        return pltpu.make_async_remote_copy(
            src_ref=piece.at[c],
            dst_ref=landing.at[c, z % 4, core],
            send_sem=z_send.at[c, dz],
            recv_sem=z_recv.at[c, z % 4, core],
            device_id=column[dz],
            device_id_type=MESH,
        )

    def collect_chunk(c):
        result = chunk(c, (x, y, z))[...]
        for copy in spreads[c]:
            copy.wait_recv()
        for slot, _, _ in mates:
            result = result + pieces[c, slot]
        piece[c] = result
        for dz in (4, 3, 5, 2, 6, 1, 7):
            drop(c, dz).start()

        @pl.when(pair == core)
        def _():
            landing[c, z % 4, core] = piece[c]

        @pl.when(pair != core)
        def _():
            drop(c, 0).start()

    far_first = sorted(mates, key=reach, reverse=True)
    product(0, rows_here)
    table[0, 0, 128:256, :] = jnp.zeros((128, 128), F32)
    table[0, 0, 128:136, :] = own_skeleton[:, 0:128]
    table[0, 0, 136:144, :] = own_skeleton[:, 128:256]
    swaps = [swap_table(0)]
    product(1, picked)
    swaps.append(swap_table(1))
    spreads = [spread_table(0)]
    spreads.append(spread_table(1))
    collect_chunk(0)
    collect_chunk(1)

    def fan(ref, sems, first, line):
        return [
            send(ref, ref, sems.at[0, first + d - 1], sems.at[1, first + d - 1], line[d]) for d in (2, 1, 3)
        ]

    def first_leg(c):
        for plane in range(4):
            for half in range(2):

                @pl.when((core * 4 + plane != z) | (core != half))
                def _(plane=plane, half=half):
                    pltpu.make_async_remote_copy(
                        src_ref=piece.at[c],
                        dst_ref=landing.at[c, plane, half],
                        send_sem=z_send.at[c, 0],
                        recv_sem=z_recv.at[c, plane, half],
                        device_id=other,
                        device_id_type=MESH,
                    ).wait_recv()

        full_a[c, x, y] = landing[c, :, 0]
        full_b[c, y, x] = landing[c, :, 1]
        return fan(full_a.at[c, x, y], y_sems, 6 * c, along_y) + fan(full_b.at[c, y, x], x_sems, 6 * c, along_x)

    def second_leg(c, copies):
        for copy in copies:
            copy.wait_recv()
        return fan(full_a.at[c, x], x_sems, 6 * c + 3, along_x) + fan(full_b.at[c, y], y_sems, 6 * c + 3, along_y)

    legs = [first_leg(0)]
    legs.append(second_leg(0, legs[0]))
    legs.append(first_leg(1))
    for copy in legs[1]:
        copy.wait_recv()

    row = lax.broadcasted_iota(jnp.int32, (RANK, RANK), 0)
    col = lax.broadcasted_iota(jnp.int32, (RANK, RANK), 1)
    skeleton_points, sizes = [], []
    for n in range(2):
        for at_x in range(4):
            for at_y in range(4):
                span = pl.ds(at_x * 64 + at_y * 16, 16)
                planes = pl.ds(2 * n, 2)
                work[n, span, 0:128] = full_a[0, at_x, at_y, planes].reshape(16, 128)
                work[n, span, 128:256] = full_b[0, at_y, at_x, planes].reshape(16, 128)
        skeleton_points.append(
            jnp.concatenate([work[n, 128:136, 0:128], work[n, 136:144, 0:128]], axis=1)
        )
        gram = work[n]
        on_diagonal = jnp.where(row == col, gram, 0.0)
        trace = jnp.sum(jnp.sum(on_diagonal, axis=0, keepdims=True), axis=1, keepdims=True)
        work[n] = gram * (1.0 / trace) + jnp.where(row == col, 0.01, 0.0)
        sizes.append(lax.rsqrt(trace))

    row_side = features(skeleton_points[0], 4.0, True).T.astype(BF16)
    col_side = features(skeleton_points[1], 1.0, False).astype(BF16)
    kernel_skel = jnp.exp(jnp.dot(row_side, col_side, preferred_element_type=F32))

    lane8 = lax.broadcasted_iota(jnp.int32, (8, 128), 1)
    row8 = lax.broadcasted_iota(jnp.int32, (8, 128), 0)
    group8 = (lane8 // 64) * 64
    lane = lax.broadcasted_iota(jnp.int32, (64, 128), 1)
    for p in range(4):
        top = 64 * p
        aligned = (top // 128) * 128
        packed = []
        for n in range(2):
            block = work[n, top : top + 64, aligned : aligned + 128]
            packed.append(pltpu.roll(block, 64, 1) if (64 * n - top) % 128 else block)
        packed = jnp.where(lane < 64, packed[0], packed[1])
        left = [packed[8 * g : 8 * g + 8] for g in range(8)]
        inverse = [jnp.where(lane8 - group8 == row8 + 8 * g, 1.0, 0.0) for g in range(8)]
        for own in range(8):
            spread = {
                g: [
                    jnp.take_along_axis(left[g], group8 + (8 * own + t), axis=1, mode="promise_in_bounds")
                    for t in range(8)
                ]
                for g in range(own, 8)
            }

            def line(tile, t):
                return jnp.broadcast_to(tile[t : t + 1, :], (8, 128))

            solve = pivots(lambda t, u: line(spread[own][u], t))
            left_rows = solve([line(left[own], t) for t in range(8)])
            inverse_rows = solve([line(inverse[own], t) for t in range(8)])
            for g in range(own + 1, 8):
                factors = solve(spread[g])
                left[g] = left[g] - fold(factors, left_rows)
                inverse[g] = inverse[g] - fold(factors, inverse_rows)
            for t in range(8):
                inverse[own] = jnp.where(row8 == t, inverse_rows[t], inverse[own])
        packed = jnp.concatenate(inverse, axis=0)
        diagonal = jnp.concatenate([jnp.where(lane < 64, packed, 0.0), jnp.where(lane < 64, 0.0, packed)], axis=0)
        stacked = jnp.concatenate([work[n, top : top + 64, :] for n in range(2)], axis=0)
        srow = lax.broadcasted_iota(jnp.int32, (128, RANK), 0)
        scol = lax.broadcasted_iota(jnp.int32, (128, RANK), 1)
        identity = jnp.where(srow % 64 == scol % 64, 1.0, 0.0)
        stacked = jnp.where(scol // 64 == p, identity, stacked)
        solved = jnp.dot(diagonal, stacked, precision=HIGH, preferred_element_type=F32)
        done = jnp.where(scol < top + 64, solved, 0.0)
        for n in range(2):
            work[n, top : top + 64, :] = done[64 * n : 64 * n + 64]
        rest = RANK - top - 64
        if rest:
            turned = solved.T[top + 64 :, :]
            tlane = lax.broadcasted_iota(jnp.int32, (rest, 128), 1)
            tcol = lax.broadcasted_iota(jnp.int32, (rest, RANK), 1)
            for n in range(2):
                update = jnp.dot(
                    jnp.where(tlane // 64 == n, turned, 0.0), solved,
                    precision=HIGH, preferred_element_type=F32,
                )
                work[n, top + 64 :, :] = jnp.where(tcol // 64 == p, 0.0, work[n, top + 64 :, :]) - update
        if p == 0:
            legs.append(second_leg(1, legs[2]))
        if p == 2:
            for copy in legs[3]:
                copy.wait_recv()
            for n in range(2):
                for at_x in range(4):
                    for at_y in range(4):
                        span = pl.ds(at_x * 64 + at_y * 16, 16)
                        planes = pl.ds(2 * n, 2)
                        chosen[n, span, 0:128] = full_a[1, at_x, at_y, planes].reshape(16, 128)
                        chosen[n, span, 128:256] = full_b[1, at_y, at_x, planes].reshape(16, 128)
            right_part = jnp.dot(kernel_skel, chosen[1], precision=HIGH, preferred_element_type=F32)
            middle = lax.dot_general(
                chosen[0], right_part, (((0,), (0,)), ((), ())), precision=HIGH, preferred_element_type=F32
            )

    size = jnp.where(node % 2 == 0, sizes[0], sizes[1])
    factor_out[...] = work[node % 2] * size
    factor_copy = send(factor_out, factor_in, factor_sems.at[0], factor_sems.at[1], other)
    last = (((1,), (1,)), ((), ()))
    half = jnp.dot(work[0], middle, precision=HIGH, preferred_element_type=F32)
    coupling[core] = ((16384.0 / math.sqrt(RANK)) * sizes[0] * sizes[1]) * lax.dot_general(
        half, work[1], last, precision=HIGH, preferred_element_type=F32
    )
    coupling_copy = send(
        coupling.at[core], coupling.at[core], coupling_sems.at[0], coupling_sems.at[1], other
    )
    factor_copy.wait_recv()
    factor = jnp.where(node // 2 == core, factor_out[...], factor_in[...])
    basis[...] = 128.0 * lax.dot_general(
        rows_here, factor, last, precision=HIGH, preferred_element_type=F32
    )
    factor_copy.wait_send()
    coupling_copy.wait()

    for copy in list(relays.values()) + nears + list(swap.values()) + small + sum(legs, []):
        copy.wait_send()
    for c in range(2):
        swaps[c].wait_send()
        for copy in spreads[c]:
            copy.wait_send()
        for dz in range(1, 8):
            drop(c, dz).wait_send()

        @pl.when(pair != core)
        def _(c=c):
            drop(c, 0).wait_send()

    for copy in list(hops.values()) + list(outs.values()) + list(fars.values()):
        copy.wait_send()


def whole(*arguments):
    dma = pltpu.SemaphoreType.DMA

    def block(*shape, kind=F32):
        return pltpu.VMEM(shape, kind)

    i32 = jnp.int32
    return pl.pallas_call(
        whole_kernel,
        out_shape=(
            jax.ShapeDtypeStruct((ROWS, RANK), F32),
            jax.ShapeDtypeStruct((2, RANK, RANK), F32),
        ),
        in_specs=[HBM] * 6,
        out_specs=(VMEM,) * 2,
        scratch_shapes=[
            block(FEATS, ROWS, kind=BF16), block(SAMPLES, ROWS, kind=BF16), block(1, ROWS, kind=i32),
            block(1, 16, kind=i32), block(1, 32, kind=i32), block(4, RANK, kind=i32), dma((6,)),
            block(25, SPAN, 128, kind=BF16), block(2, 4, 2, 16, ROWS, kind=BF16), block(2, 4, 8, 128, kind=i32),
            block(SPAN, 128, kind=BF16), block(16, ROWS, kind=BF16), block(8, 128, kind=i32),
            block(8, 32, 128), block(8, 32, 128), block(8, 2 * ROWS, 16, kind=BF16),
            block(2 * ROWS, 2 * ROWS, kind=BF16), block(2 * ROWS, 2 * ROWS, kind=BF16), block(2, 2, 4, ROWS, RANK),
            dma((8, 2)), dma((8, 2)), dma((6, 2, 2)), dma((6, 2, 2)), dma((6, 2)), dma((6, 2)),
            dma((2, 4)), dma((2, 4)), dma((2, 4)), dma((2, 4)),
            block(2, 4, ROWS, RANK), block(2, ROWS, RANK, kind=LINK), block(2, 2, 128, RANK, kind=LINK),
            block(2, 2, ROWS, RANK, kind=LINK), block(2, 2, ROWS, RANK, kind=LINK),
            block(2, 2, RANK, 128), block(2, RANK, 128), block(2, 8, 128), block(2, 32, 8, 128),
            block(2, 4, 2, 8, 128), block(2, 4, 4, 4, 8, 128), block(2, 4, 4, 4, 8, 128),
            dma((2, 4)), dma((2, 4)), dma((2, 2, 2)), dma((2, 2, 2, 2)), dma((2, 2)), dma((2, 32)), dma((2, 32)),
            dma((2, 8)), dma((2, 4, 2)), dma((2, 12)), dma((2, 12)),
            block(2, RANK, RANK), block(2, RANK, RANK), block(RANK, RANK), block(RANK, RANK),
            dma((2,)), dma((2,)),
        ],
        compiler_params=pltpu.CompilerParams(
            collective_id=0, has_side_effects=True, vmem_limit_bytes=VMEM_LIMIT
        ),
        name="whole",
    )(*arguments)


def body(points, omega, tree_order, sibling_blocks, cousin_blocks, skeleton):
    arguments = (points, omega, tree_order.reshape(1, ROWS), sibling_blocks, cousin_blocks, skeleton)
    return whole(*(pltpu.with_memory_space_constraint(argument, pltpu.HBM) for argument in arguments))


def solution(mesh):
    return jax.shard_map(
        body,
        mesh=mesh,
        in_specs=(
            P(None, ("leaf", "sub")),
            P(None, ("leaf", "sub")),
            P(("leaf", "sub")),
            P("leaf", None),
            P("leaf", None),
            P(),
        ),
        out_specs=(P(("leaf", "sub"), None), P()),
        check_vma=False,
    )
```

```python
import math

import jax
import jax.numpy as jnp
from jax import lax
from jax.experimental import pallas as pl
from jax.experimental.pallas import tpu as pltpu
from jax.sharding import PartitionSpec as P

MESH = pl.DeviceIdType.MESH
HIGH = lax.Precision.HIGH
HIGHEST = lax.Precision.HIGHEST
F32 = jnp.float32
BF16 = jnp.bfloat16
HBM = pl.BlockSpec(memory_space=pltpu.HBM)
VMEM = pl.BlockSpec(memory_space=pltpu.VMEM)

ROWS = 256
FEATS = 8
SAMPLES = 128
RANK = 256
SPAN = 288
LINK = BF16
VMEM_LIMIT = 40 << 20


def place():
    leaf = lax.axis_index("leaf")
    core = lax.axis_index("sub")
    return leaf % 4, (leaf // 4) % 4, leaf // 16, core


def device(x, y, z, core):
    return (z * 16 + y * 4 + x, core)


def send(src, dst, send_sem, recv_sem, target):
    copy = pltpu.make_async_remote_copy(
        src_ref=src,
        dst_ref=dst,
        send_sem=send_sem,
        recv_sem=recv_sem,
        device_id=target,
        device_id_type=MESH,
    )
    copy.start()
    return copy


def features(coordinates, scale, ones_first):
    norm = -2.0 * jnp.sum(coordinates * coordinates, axis=0, keepdims=True)
    first = norm.astype(BF16).astype(F32)
    second = (norm - first).astype(BF16).astype(F32)
    third = norm - first - second
    row = lax.broadcasted_iota(jnp.int32, coordinates.shape, 0)
    start = 3 if ones_first else 0
    other = 0 if ones_first else 3
    tail = jnp.where((row >= other) & (row < other + 3), 1.0, 0.0)
    tail = jnp.where(row == start, first, tail)
    tail = jnp.where(row == start + 1, second, tail)
    tail = jnp.where(row == start + 2, third, tail)
    return jnp.concatenate([scale * coordinates, tail], axis=0)


def fold(factors, lines):
    terms = [factor * values for factor, values in zip(factors, lines, strict=True)]
    while len(terms) > 1:
        terms = [a + b for a, b in zip(terms[::2], terms[1::2], strict=True)]
    return terms[0]


def pivots(entry):
    left = {(t, u): entry(t, u) for t in range(8) for u in range(t + 1)}
    scale, lower = {}, {}
    for t in range(0, 8, 2):
        a, b, c = left[t, t], left[t + 1, t], left[t + 1, t + 1]
        scale[t] = lax.rsqrt(a)
        lower[t + 1, t] = b * scale[t]
        scale[t + 1] = a * lax.rsqrt(a * (a * c - b * b))
        for i in range(t + 2, 8):
            lower[i, t] = left[i, t] * scale[t]
            lower[i, t + 1] = (left[i, t + 1] - lower[i, t] * lower[t + 1, t]) * scale[t + 1]
        for i in range(t + 2, 8):
            for k in range(t + 2, i + 1):
                left[i, k] = left[i, k] - (lower[i, t] * lower[k, t] + lower[i, t + 1] * lower[k, t + 1])

    def solve(values):
        values = list(values)
        for t in range(0, 8, 2):
            values[t] = values[t] * scale[t]
            values[t + 1] = (values[t + 1] - values[t] * lower[t + 1, t]) * scale[t + 1]
            for i in range(t + 2, 8):
                values[i] = values[i] - (values[t] * lower[i, t] + values[t + 1] * lower[i, t + 1])
        return values

    return solve


MATE = 0
USE = [
    (MATE, 0), (6, 0), (2, 0), (5, 0), (MATE, 1), (MATE, 3), (6, 1), (6, 3),
    (3, 0), (3, 1), (MATE, 2), (6, 2), (3, 3), (3, 2), (2, 1), (2, 3),
    (5, 1), (5, 3), (2, 2), (5, 2), (4, 0), (4, 1), (4, 3), (4, 2),
]
SLOT = {block: slot for slot, block in enumerate(USE)}
KIND = {MATE: 1, 6: 1, 3: 1, 2: 0, 5: 0, 4: 0}


def make_masks(lists, near_mask, far_mask, x, y, z):
    lane = lax.broadcasted_iota(jnp.int32, (8, 128), 1)
    group = lax.broadcasted_iota(jnp.int32, (8, 128), 0) // 4
    named = jnp.full((8, 128), -1, jnp.int32)
    near = jnp.zeros((8, 128), F32)
    for slot, (dz, along) in enumerate(USE):
        plane = (z + (dz or 7 - 6 * (z % 2))) % 8
        if KIND[dz]:
            block = plane * 16 + y * 4 + (x + along) % 4
        else:
            block = plane * 16 + ((y + along) % 4) * 4 + x
        named = jnp.where((lane == slot) & (group == KIND[dz]), block, named)
        near = jnp.where(lane == slot, jnp.where(plane // 4 == z // 4, 1.0, 0.0), near)
    named = named.astype(F32)
    hit = jnp.zeros((8, 128), F32)
    for side, length in ((0, 16), (1, 32)):
        entries = jnp.concatenate(
            [lists[k, at, side : side + 1, :] for k in range(2) for at in range(4)], axis=0
        ).astype(F32)
        for e in range(length):
            hit = jnp.where(named == jnp.broadcast_to(entries[:, e : e + 1], (8, 128)), 1.0, hit)
    near_hit, far_hit = (hit * near).T, (hit * (1.0 - near)).T
    for r in range(8):
        near_mask[r] = jnp.broadcast_to(near_hit[0:32, r : r + 1], (32, 128))
        far_mask[r] = jnp.broadcast_to(far_hit[0:32, r : r + 1], (32, 128))


def whole_kernel(
    points_in, omega_in, order_in, siblings_in, cousins_in, skeleton_in,
    basis, coupling,
    points, omega, tree_order, siblings, cousins, skeleton, load_sems,
    blocks, row_points, lists, own, own_rows, own_lists, near_mask, far_mask, rows, even_tile, odd_tile, parts,
    hop_send, hop_recv, out_send, out_recv, far_send, far_recv, rows_send, rows_recv, list_send, list_recv,
    other_core, shipped, received, table, sums, piece, pieces, landing, full_a, full_b,
    core_send, core_recv, ship_sems, table_sems, piece_send, piece_recv,
    z_send, z_recv, y_sems, x_sems,
    work, chosen, factor_out, factor_in, factor_sems, coupling_sems,
):
    loads = [
        pltpu.make_async_copy(source, target, load_sems.at[k])
        for k, (source, target) in enumerate(
            [
                (omega_in, omega),
                (points_in, points),
                (order_in, tree_order),
                (siblings_in, siblings),
                (cousins_in, cousins),
                (skeleton_in, skeleton),
            ]
        )
    ]
    for copy in loads:
        copy.start()
    x, y, z, core = place()
    leaf = z * 16 + y * 4 + x
    node, pair = z // 2, z // 4
    other = device(x, y, z, 1 - core)
    right, left_side = device((x + 1) % 4, y, z, core), device((x + 3) % 4, y, z, core)
    above, below = device(x, (y + 1) % 4, z, core), device(x, (y + 3) % 4, z, core)
    upward, downward = device(x, y, (z + 1) % 8, core), device(x, y, (z + 7) % 8, core)
    mates = []
    for dz in range(2):
        for dy in range(4):
            for dx in range(4):
                if dz or dy or dx:
                    where = ((x + dx) % 4, (y + dy) % 4, node * 2 + (z + dz) % 2)
                    mates.append((dz * 16 + dy * 4 + dx, where, device(*where, core)))
    column = [device(x, y, (z + dz) % 8, pair) for dz in range(8)]
    along_x = [device((x + d) % 4, y, z, core) for d in range(4)]
    along_y = [device(x, (y + d) % 4, z, core) for d in range(4)]
    partners = [who for _, _, who in mates] + [other]
    partners += [
        device(x, y, ((node + dn) % 4) * 2 + dz, c) for dn in range(1, 4) for dz in range(2) for c in range(2)
    ]
    partners.append(device(x, y, node * 2 + (z + 1) % 2, 1 - core))
    barrier = pltpu.get_barrier_semaphore()
    for partner in partners:
        pl.semaphore_signal(barrier, inc=1, device_id=partner, device_id_type=MESH)

    loads[0].wait()
    own[0:ROWS, :] = omega[...].astype(F32).T.astype(BF16)
    loads[1].wait()
    columns = features(points[...].astype(F32), 1.0, False).astype(BF16)
    own[256:272, :] = columns[:, :128]
    own[272:288, :] = columns[:, 128:]
    halves = (pl.ds(0, SPAN // 2), pl.ds(SPAN // 2, SPAN // 2))
    pl.semaphore_wait(barrier, len(partners))

    from_below, from_above = 24 * (z % 2), 24 * ((z + 1) % 2)
    hops = {}

    def hop(ref, slot, key, half, who):
        hops[key, half] = send(
            ref.at[halves[half]], blocks.at[slot, halves[half]],
            hop_send.at[key, half], hop_recv.at[key, half], who,
        )

    for step in range(2):
        hop(own, from_above, 7, step, upward)
        hop(own, from_below, 1, 1 - step, downward)

    for copy in loads[2:]:
        copy.wait()
    local = tree_order[...] % ROWS
    lane = lax.broadcasted_iota(jnp.int32, (ROWS, ROWS), 0)
    pick = jnp.where(lane == local, 1.0, 0.0).astype(BF16)
    mine = jnp.dot(points[...], pick, preferred_element_type=F32)
    own_rows[...] = features(mine, 4.0, True).astype(BF16)
    own_lists[...] = jnp.zeros_like(own_lists)
    own_lists[0:1, 0:16] = siblings[...]
    own_lists[1:2, 0:32] = cousins[...]
    small = []
    for kind, (at, line) in enumerate(((x, along_x), (y, along_y))):
        row_points[kind, at, core] = own_rows[...]
        lists[kind, at] = own_lists[...]
        for d in range(1, 4):
            target = row_points.at[kind, at, core]
            small.append(send(own_rows, target, rows_send.at[kind, d], rows_recv.at[kind, d], line[d]))
            target = lists.at[kind, at]
            small.append(send(own_lists, target, list_send.at[kind, d], list_recv.at[kind, d], line[d]))
    parts[...] = jnp.zeros_like(parts)

    plus, minus = (above, right), (below, left_side)
    outs, fars = {}, {}

    def fan_out(k, dz, half):
        kind = KIND[dz]
        block = blocks.at[SLOT[dz, 0], halves[half]]
        for side, (at, who) in enumerate(((SLOT[dz, 3], plus[kind]), (SLOT[dz, 1], minus[kind]))):
            outs[k, side, half] = send(
                block, blocks.at[at, halves[half]], out_send.at[k, side, half], out_recv.at[k, side, half], who
            )

    def relay(k, dz):
        kind = KIND[dz]
        for side, (at, who) in enumerate(((SLOT[dz, 3], plus[kind]), (SLOT[dz, 1], minus[kind]))):
            outs[k, side, side].wait_recv()
            fars[k, side] = send(
                blocks.at[at, halves[side]], blocks.at[SLOT[dz, 2], halves[side]],
                far_send.at[k, side], far_recv.at[k, side], who,
            )

    def landed(*ks):
        for k in ks:
            for side in range(2):
                outs[k, side, 1 - side].wait_recv()

    def passed(*ks):
        for k in ks:
            for side in range(2):
                fars[k, side].wait_recv()

    for step in range(2):
        hops[7, step].wait_recv()
        hop(blocks.at[from_below], SLOT[6, 0], 6, step, upward)
        hops[1, 1 - step].wait_recv()
        hop(blocks.at[from_above], SLOT[2, 0], 2, 1 - step, downward)
    for half in range(2):
        fan_out(0, MATE, half)
    for copy in small:
        copy.wait_recv()
    swap_rows = send(row_points.at[:, :, core], row_points.at[:, :, core], rows_send.at[0, 0], rows_recv.at[0, 0], other)
    make_masks(lists, near_mask, far_mask, x, y, z)
    for step in range(2):
        hops[6, step].wait_recv()
        hop(blocks.at[SLOT[6, 0]], SLOT[5, 0], 5, step, upward)
        fan_out(1, 6, step)
        hops[2, 1 - step].wait_recv()
        hop(blocks.at[SLOT[2, 0]], SLOT[3, 0], 3, 1 - step, downward)
        fan_out(2, 2, 1 - step)
    swap_rows.wait()
    for r in range(8):
        for half in range(2):
            rows[r, half * ROWS : (half + 1) * ROWS, :] = row_points[r // 4, r % 4, half].astype(F32).T.astype(BF16)

    def kernel_tile(r, use, tile):
        columns = jnp.concatenate(
            [blocks[2 * use + k, at : at + 16, :] for k in range(2) for at in (256, 272)], axis=1
        )
        exponent = jnp.dot(rows[r], columns, preferred_element_type=F32)
        tile[...] = jnp.exp(exponent).astype(BF16)

    def add(kind, at, use, tile):
        r = kind * 4 + at
        weights = []
        for k in range(2):
            slot = 2 * use + k
            values = blocks[slot, 0:ROWS, :]
            near = near_mask[r, pl.ds(slot, 1), :].astype(BF16)
            far = far_mask[r, pl.ds(slot, 1), :].astype(BF16)
            weights.append(jnp.concatenate([values * near, values * far], axis=1))
        terms = jnp.dot(tile[...], jnp.concatenate(weights, axis=0), preferred_element_type=F32)
        parts[0, kind, at] += terms[0:ROWS]
        parts[1, kind, at] += terms[ROWS:]

    def batch(kind, count, item):
        at, use = item(0)
        kernel_tile(kind * 4 + at, use, even_tile)

        def two_steps(step, carry):
            at0, use0 = item(2 * step)
            at1, use1 = item(2 * step + 1)
            at2, use2 = item(2 * step + 2)
            kernel_tile(kind * 4 + at1, use1, odd_tile)
            add(kind, at0, use0, even_tile)
            kernel_tile(kind * 4 + at2, use2, even_tile)
            add(kind, at1, use1, odd_tile)
            return carry

        lax.fori_loop(0, (count - 1) // 2, two_steps, 0)
        if count % 2:
            add(kind, *item(count - 1), even_tile)
        else:
            at, use = item(count - 1)
            kernel_tile(kind * 4 + at, use, odd_tile)
            add(kind, *item(count - 2), even_tile)
            add(kind, at, use, odd_tile)

    batch(1, 4, lambda i: (i, 0))
    relay(0, MATE)
    hops[5, 0].wait_recv()
    hop(blocks.at[SLOT[5, 0]], SLOT[4, 0], 4, 0, upward)
    fan_out(3, 5, 0)
    hops[3, 1].wait_recv()
    hop(blocks.at[SLOT[3, 0]], SLOT[4, 0], 4, 1, downward)
    fan_out(4, 3, 1)
    hops[5, 1].wait_recv()
    fan_out(3, 5, 1)
    hops[3, 0].wait_recv()
    fan_out(4, 3, 0)
    batch(0, 4, lambda i: (i, 1))
    relay(1, 6)
    relay(2, 2)
    for half in range(2):
        hops[4, half].wait_recv()
        fan_out(5, 4, half)
    landed(0, 1)
    batch(1, 8, lambda i: (i % 4, 2 + i // 4))
    relay(3, 5)
    relay(4, 3)
    relay(5, 4)
    landed(4)
    passed(0, 1)
    batch(1, 8, lambda i: (i % 4, 4 + i // 4))
    passed(4)
    batch(1, 4, lambda i: (i, 6))

    ahead, behind, across = (x + 1) % 4, (x + 3) % 4, (x + 2) % 4
    next_y, last_y = (y + 1) % 4, (y + 3) % 4
    order = [(across, (y + 2) % 4), (ahead, next_y), (behind, last_y), (x, y)]
    swap = {}

    def give(step, kind):
        at = order[step][kind]
        swap[step, kind] = send(
            parts.at[1 - core, kind, at], other_core.at[kind, at],
            core_send.at[kind, step], core_recv.at[kind, step], other,
        )


    def partial(step, kind):
        swap[step, kind].wait_recv()
        at = order[step][kind]
        return parts[core, kind, at] + other_core[kind, at]

    ships = []

    def ship(step, kind):
        shipped[kind, step] = partial(step, kind).astype(LINK)
        who = (along_x, along_y)[kind][(2, 1, 3)[step]]
        ships.append(
            send(
                shipped.at[kind, step], received.at[kind, step],
                ship_sems.at[0, kind, step], ship_sems.at[1, kind, step], who,
            )
        )

    for step in range(4):
        give(step, 1)
    landed(2, 3, 5)
    passed(2, 3, 5)

    def last_batch(step, first=0, count=5):
        at = order[step][0]
        batch(0, count, lambda i: (at, 7 + first + i))
        if first + count == 5:
            give(step, 0)

    last_batch(0)
    for step in range(3):
        ship(step, 1)
    last_batch(1)
    ship(0, 0)
    last_batch(2)
    ship(1, 0)
    last_batch(3, 0, 2)
    ship(2, 0)
    last_batch(3, 2, 3)
    total = partial(3, 1) + partial(3, 0)
    first_row = (leaf * 2 + core) * ROWS
    row = lax.broadcasted_iota(jnp.int32, (ROWS, RANK), 0) + first_row
    picked = jnp.where(row == skeleton[pl.ds(node, 1), :], 1.0, 0.0)
    own_skeleton = jnp.dot(
        mine.astype(BF16), picked.astype(BF16), preferred_element_type=F32
    )
    for copy in ships:
        copy.wait_recv()
    for kind in range(2):
        for step in range(3):
            total = total + received[kind, step].astype(F32)
    rows_here = total

    def product(c, first):
        values = lax.dot_general(
            first, rows_here, (((0,), (0,)), ((), ())), precision=HIGH, preferred_element_type=F32
        )
        table[c, 0] = values[:, 0:128]
        table[c, 1] = values[:, 128:256]

    def swap_table(c):
        return send(table.at[c, 1 - core], sums.at[c], table_sems.at[0, c], table_sems.at[1, c], other)

    def spread_table(c):
        swaps[c].wait_recv()
        sums[c] += table[c, core]
        copies = []
        for slot, where, who in far_first:
            copies.append(
                send(chunk(c, where), pieces.at[c, slot], piece_send.at[c, slot], piece_recv.at[c, slot], who)
            )
        return copies

    def chunk(c, where):
        first = (where[0] * 8 + where[1] * 2 + where[2] % 2) * 8
        return sums.at[c, pl.ds(pl.multiple_of(first, 8), 8)]

    def reach(mate):
        return sum(min(d, 4 - d) for d in (mate[0] // 16, mate[0] // 4 % 4, mate[0] % 4))

    def drop(c, dz):
        return pltpu.make_async_remote_copy(
            src_ref=piece.at[c],
            dst_ref=landing.at[c, z % 4, core],
            send_sem=z_send.at[c, dz],
            recv_sem=z_recv.at[c, z % 4, core],
            device_id=column[dz],
            device_id_type=MESH,
        )

    def collect_chunk(c):
        result = chunk(c, (x, y, z))[...]
        for copy in spreads[c]:
            copy.wait_recv()
        for slot, _, _ in mates:
            result = result + pieces[c, slot]
        piece[c] = result
        for dz in (4, 3, 5, 2, 6, 1, 7):
            drop(c, dz).start()

        @pl.when(pair == core)
        def _():
            landing[c, z % 4, core] = piece[c]

        @pl.when(pair != core)
        def _():
            drop(c, 0).start()

    far_first = sorted(mates, key=reach, reverse=True)
    product(0, rows_here)
    table[0, 0, 128:256, :] = jnp.zeros((128, 128), F32)
    table[0, 0, 128:136, :] = own_skeleton[:, 0:128]
    table[0, 0, 136:144, :] = own_skeleton[:, 128:256]
    swaps = [swap_table(0)]
    product(1, picked)
    swaps.append(swap_table(1))
    spreads = [spread_table(0)]
    spreads.append(spread_table(1))
    collect_chunk(0)
    collect_chunk(1)

    def fan(ref, sems, first, line):
        return [
            send(ref, ref, sems.at[0, first + d - 1], sems.at[1, first + d - 1], line[d]) for d in (2, 1, 3)
        ]

    def first_leg(c):
        for plane in range(4):
            for half in range(2):

                @pl.when((core * 4 + plane != z) | (core != half))
                def _(plane=plane, half=half):
                    pltpu.make_async_remote_copy(
                        src_ref=piece.at[c],
                        dst_ref=landing.at[c, plane, half],
                        send_sem=z_send.at[c, 0],
                        recv_sem=z_recv.at[c, plane, half],
                        device_id=other,
                        device_id_type=MESH,
                    ).wait_recv()

        full_a[c, x, y] = landing[c, :, 0]
        full_b[c, y, x] = landing[c, :, 1]
        return fan(full_a.at[c, x, y], y_sems, 6 * c, along_y) + fan(full_b.at[c, y, x], x_sems, 6 * c, along_x)

    def second_leg(c, copies):
        for copy in copies:
            copy.wait_recv()
        return fan(full_a.at[c, x], x_sems, 6 * c + 3, along_x) + fan(full_b.at[c, y], y_sems, 6 * c + 3, along_y)

    legs = [first_leg(0)]
    legs.append(second_leg(0, legs[0]))
    legs.append(first_leg(1))
    legs.append(second_leg(1, legs[2]))
    for copy in legs[1]:
        copy.wait_recv()

    row = lax.broadcasted_iota(jnp.int32, (RANK, RANK), 0)
    col = lax.broadcasted_iota(jnp.int32, (RANK, RANK), 1)
    skeleton_points, sizes = [], []
    for n in range(2):
        for at_x in range(4):
            for at_y in range(4):
                span = pl.ds(at_x * 64 + at_y * 16, 16)
                planes = pl.ds(2 * n, 2)
                work[n, span, 0:128] = full_a[0, at_x, at_y, planes].reshape(16, 128)
                work[n, span, 128:256] = full_b[0, at_y, at_x, planes].reshape(16, 128)
        skeleton_points.append(
            jnp.concatenate([work[n, 128:136, 0:128], work[n, 136:144, 0:128]], axis=1)
        )
        gram = work[n]
        on_diagonal = jnp.where(row == col, gram, 0.0)
        trace = jnp.sum(jnp.sum(on_diagonal, axis=0, keepdims=True), axis=1, keepdims=True)
        work[n] = gram * (1.0 / trace) + jnp.where(row == col, 0.01, 0.0)
        sizes.append(lax.rsqrt(trace))

    row_side = features(skeleton_points[0], 4.0, True).T.astype(BF16)
    col_side = features(skeleton_points[1], 1.0, False).astype(BF16)
    kernel_skel = jnp.exp(jnp.dot(row_side, col_side, preferred_element_type=F32))

    lane8 = lax.broadcasted_iota(jnp.int32, (8, 128), 1)
    row8 = lax.broadcasted_iota(jnp.int32, (8, 128), 0)
    group8 = (lane8 // 64) * 64
    lane = lax.broadcasted_iota(jnp.int32, (64, 128), 1)
    for p in range(4):
        top = 64 * p
        aligned = (top // 128) * 128
        packed = []
        for n in range(2):
            block = work[n, top : top + 64, aligned : aligned + 128]
            packed.append(pltpu.roll(block, 64, 1) if (64 * n - top) % 128 else block)
        packed = jnp.where(lane < 64, packed[0], packed[1])
        left = [packed[8 * g : 8 * g + 8] for g in range(8)]
        inverse = [jnp.where(lane8 - group8 == row8 + 8 * g, 1.0, 0.0) for g in range(8)]
        for own in range(8):
            spread = {
                g: [
                    jnp.take_along_axis(left[g], group8 + (8 * own + t), axis=1, mode="promise_in_bounds")
                    for t in range(8)
                ]
                for g in range(own, 8)
            }

            def line(tile, t):
                return jnp.broadcast_to(tile[t : t + 1, :], (8, 128))

            solve = pivots(lambda t, u: line(spread[own][u], t))
            left_rows = solve([line(left[own], t) for t in range(8)])
            inverse_rows = solve([line(inverse[own], t) for t in range(8)])
            for g in range(own + 1, 8):
                factors = solve(spread[g])
                left[g] = left[g] - fold(factors, left_rows)
                inverse[g] = inverse[g] - fold(factors, inverse_rows)
            for t in range(8):
                inverse[own] = jnp.where(row8 == t, inverse_rows[t], inverse[own])
        packed = jnp.concatenate(inverse, axis=0)
        diagonal = jnp.concatenate([jnp.where(lane < 64, packed, 0.0), jnp.where(lane < 64, 0.0, packed)], axis=0)
        stacked = jnp.concatenate([work[n, top : top + 64, :] for n in range(2)], axis=0)
        srow = lax.broadcasted_iota(jnp.int32, (128, RANK), 0)
        scol = lax.broadcasted_iota(jnp.int32, (128, RANK), 1)
        identity = jnp.where(srow % 64 == scol % 64, 1.0, 0.0)
        stacked = jnp.where(scol // 64 == p, identity, stacked)
        solved = jnp.dot(diagonal, stacked, precision=HIGH, preferred_element_type=F32)
        done = jnp.where(scol < top + 64, solved, 0.0)
        for n in range(2):
            work[n, top : top + 64, :] = done[64 * n : 64 * n + 64]
        rest = RANK - top - 64
        if rest:
            turned = solved.T[top + 64 :, :]
            tlane = lax.broadcasted_iota(jnp.int32, (rest, 128), 1)
            tcol = lax.broadcasted_iota(jnp.int32, (rest, RANK), 1)
            for n in range(2):
                update = jnp.dot(
                    jnp.where(tlane // 64 == n, turned, 0.0), solved,
                    precision=HIGH, preferred_element_type=F32,
                )
                work[n, top + 64 :, :] = jnp.where(tcol // 64 == p, 0.0, work[n, top + 64 :, :]) - update
        if p == 1:
            for copy in legs[3]:
                copy.wait_recv()
            for n in range(2):
                for at_x in range(4):
                    for at_y in range(4):
                        span = pl.ds(at_x * 64 + at_y * 16, 16)
                        planes = pl.ds(2 * n, 2)
                        chosen[n, span, 0:128] = full_a[1, at_x, at_y, planes].reshape(16, 128)
                        chosen[n, span, 128:256] = full_b[1, at_y, at_x, planes].reshape(16, 128)
            right_part = jnp.dot(kernel_skel, chosen[1], precision=HIGH, preferred_element_type=F32)
            middle = lax.dot_general(
                chosen[0], right_part, (((0,), (0,)), ((), ())), precision=HIGH, preferred_element_type=F32
            )

    size = jnp.where(node % 2 == 0, sizes[0], sizes[1])
    factor_out[...] = work[node % 2] * size
    factor_copy = send(factor_out, factor_in, factor_sems.at[0], factor_sems.at[1], other)
    last = (((1,), (1,)), ((), ()))
    half = jnp.dot(work[0], middle, precision=HIGH, preferred_element_type=F32)
    coupling[core] = ((16384.0 / math.sqrt(RANK)) * sizes[0] * sizes[1]) * lax.dot_general(
        half, work[1], last, precision=HIGH, preferred_element_type=F32
    )
    coupling_copy = send(
        coupling.at[core], coupling.at[core], coupling_sems.at[0], coupling_sems.at[1], other
    )
    factor_copy.wait_recv()
    factor = jnp.where(node // 2 == core, factor_out[...], factor_in[...])
    basis[...] = 128.0 * lax.dot_general(
        rows_here, factor, last, precision=HIGH, preferred_element_type=F32
    )
    factor_copy.wait_send()
    coupling_copy.wait()

    for copy in ships + list(swap.values()) + small + sum(legs, []):
        copy.wait_send()
    for c in range(2):
        swaps[c].wait_send()
        for copy in spreads[c]:
            copy.wait_send()
        for dz in range(1, 8):
            drop(c, dz).wait_send()

        @pl.when(pair != core)
        def _(c=c):
            drop(c, 0).wait_send()

    for copy in list(hops.values()) + list(outs.values()) + list(fars.values()):
        copy.wait_send()


def whole(*arguments):
    dma = pltpu.SemaphoreType.DMA

    def block(*shape, kind=F32):
        return pltpu.VMEM(shape, kind)

    i32 = jnp.int32
    return pl.pallas_call(
        whole_kernel,
        out_shape=(
            jax.ShapeDtypeStruct((ROWS, RANK), F32),
            jax.ShapeDtypeStruct((2, RANK, RANK), F32),
        ),
        in_specs=[HBM] * 6,
        out_specs=(VMEM,) * 2,
        scratch_shapes=[
            block(FEATS, ROWS, kind=BF16), block(SAMPLES, ROWS, kind=BF16), block(1, ROWS, kind=i32),
            block(1, 16, kind=i32), block(1, 32, kind=i32), block(4, RANK, kind=i32), dma((6,)),
            block(25, SPAN, 128, kind=BF16), block(2, 4, 2, 16, ROWS, kind=BF16), block(2, 4, 8, 128, kind=i32),
            block(SPAN, 128, kind=BF16), block(16, ROWS, kind=BF16), block(8, 128, kind=i32),
            block(8, 32, 128), block(8, 32, 128), block(8, 2 * ROWS, 16, kind=BF16),
            block(2 * ROWS, 2 * ROWS, kind=BF16), block(2 * ROWS, 2 * ROWS, kind=BF16), block(2, 2, 4, ROWS, RANK),
            dma((8, 2)), dma((8, 2)), dma((6, 2, 2)), dma((6, 2, 2)), dma((6, 2)), dma((6, 2)),
            dma((2, 4)), dma((2, 4)), dma((2, 4)), dma((2, 4)),
            block(2, 4, ROWS, RANK), block(2, 3, ROWS, RANK, kind=LINK), block(2, 3, ROWS, RANK, kind=LINK),
            block(2, 2, RANK, 128), block(2, RANK, 128), block(2, 8, 128), block(2, 32, 8, 128),
            block(2, 4, 2, 8, 128), block(2, 4, 4, 4, 8, 128), block(2, 4, 4, 4, 8, 128),
            dma((2, 4)), dma((2, 4)), dma((2, 2, 3)), dma((2, 2)), dma((2, 32)), dma((2, 32)),
            dma((2, 8)), dma((2, 4, 2)), dma((2, 12)), dma((2, 12)),
            block(2, RANK, RANK), block(2, RANK, RANK), block(RANK, RANK), block(RANK, RANK),
            dma((2,)), dma((2,)),
        ],
        compiler_params=pltpu.CompilerParams(
            collective_id=0, has_side_effects=True, vmem_limit_bytes=VMEM_LIMIT
        ),
        name="whole",
    )(*arguments)


def body(points, omega, tree_order, sibling_blocks, cousin_blocks, skeleton):
    arguments = (points, omega, tree_order.reshape(1, ROWS), sibling_blocks, cousin_blocks, skeleton)
    return whole(*(pltpu.with_memory_space_constraint(argument, pltpu.HBM) for argument in arguments))


def solution(mesh):
    return jax.shard_map(
        body,
        mesh=mesh,
        in_specs=(
            P(None, ("leaf", "sub")),
            P(None, ("leaf", "sub")),
            P(("leaf", "sub")),
            P("leaf", None),
            P("leaf", None),
            P(),
        ),
        out_specs=(P(("leaf", "sub"), None), P()),
        check_vma=False,
    )
```

```python
import math

import jax
import jax.numpy as jnp
from jax import lax
from jax.experimental import pallas as pl
from jax.experimental.pallas import tpu as pltpu
from jax.sharding import PartitionSpec as P

MESH = pl.DeviceIdType.MESH
HIGH = lax.Precision.HIGH
HIGHEST = lax.Precision.HIGHEST
F32 = jnp.float32
BF16 = jnp.bfloat16
HBM = pl.BlockSpec(memory_space=pltpu.HBM)
VMEM = pl.BlockSpec(memory_space=pltpu.VMEM)

ROWS = 256
FEATS = 8
SAMPLES = 128
RANK = 256
SPAN = 288
LINK = BF16
VMEM_LIMIT = 40 << 20


def place():
    leaf = lax.axis_index("leaf")
    core = lax.axis_index("sub")
    return leaf % 4, (leaf // 4) % 4, leaf // 16, core


def device(x, y, z, core):
    return (z * 16 + y * 4 + x, core)


def send(src, dst, send_sem, recv_sem, target):
    copy = pltpu.make_async_remote_copy(
        src_ref=src,
        dst_ref=dst,
        send_sem=send_sem,
        recv_sem=recv_sem,
        device_id=target,
        device_id_type=MESH,
    )
    copy.start()
    return copy


def features(coordinates, scale, ones_first):
    norm = -2.0 * jnp.sum(coordinates * coordinates, axis=0, keepdims=True)
    first = norm.astype(BF16).astype(F32)
    second = (norm - first).astype(BF16).astype(F32)
    third = norm - first - second
    row = lax.broadcasted_iota(jnp.int32, coordinates.shape, 0)
    start = 3 if ones_first else 0
    other = 0 if ones_first else 3
    tail = jnp.where((row >= other) & (row < other + 3), 1.0, 0.0)
    tail = jnp.where(row == start, first, tail)
    tail = jnp.where(row == start + 1, second, tail)
    tail = jnp.where(row == start + 2, third, tail)
    return jnp.concatenate([scale * coordinates, tail], axis=0)


def fold(factors, lines):
    terms = [factor * values for factor, values in zip(factors, lines, strict=True)]
    while len(terms) > 1:
        terms = [a + b for a, b in zip(terms[::2], terms[1::2], strict=True)]
    return terms[0]


def pivots(entry):
    left = {(t, u): entry(t, u) for t in range(8) for u in range(t + 1)}
    scale, lower = {}, {}
    for t in range(0, 8, 2):
        a, b, c = left[t, t], left[t + 1, t], left[t + 1, t + 1]
        scale[t] = lax.rsqrt(a)
        lower[t + 1, t] = b * scale[t]
        scale[t + 1] = a * lax.rsqrt(a * (a * c - b * b))
        for i in range(t + 2, 8):
            lower[i, t] = left[i, t] * scale[t]
            lower[i, t + 1] = (left[i, t + 1] - lower[i, t] * lower[t + 1, t]) * scale[t + 1]
        for i in range(t + 2, 8):
            for k in range(t + 2, i + 1):
                left[i, k] = left[i, k] - (lower[i, t] * lower[k, t] + lower[i, t + 1] * lower[k, t + 1])

    def solve(values):
        values = list(values)
        for t in range(0, 8, 2):
            values[t] = values[t] * scale[t]
            values[t + 1] = (values[t + 1] - values[t] * lower[t + 1, t]) * scale[t + 1]
            for i in range(t + 2, 8):
                values[i] = values[i] - (values[t] * lower[i, t] + values[t + 1] * lower[i, t + 1])
        return values

    return solve


MATE = 0
USE = [
    (MATE, 0), (6, 0), (2, 0), (5, 0), (MATE, 1), (MATE, 3), (6, 1), (6, 3),
    (3, 0), (3, 1), (MATE, 2), (6, 2), (3, 3), (3, 2), (2, 1), (2, 3),
    (5, 1), (5, 3), (2, 2), (5, 2), (4, 0), (4, 1), (4, 3), (4, 2),
]
SLOT = {block: slot for slot, block in enumerate(USE)}
KIND = {MATE: 1, 6: 1, 3: 1, 2: 0, 5: 0, 4: 0}


def make_masks(lists, near_mask, far_mask, x, y, z):
    lane = lax.broadcasted_iota(jnp.int32, (8, 128), 1)
    group = lax.broadcasted_iota(jnp.int32, (8, 128), 0) // 4
    named = jnp.full((8, 128), -1, jnp.int32)
    near = jnp.zeros((8, 128), F32)
    for slot, (dz, along) in enumerate(USE):
        plane = (z + (dz or 7 - 6 * (z % 2))) % 8
        if KIND[dz]:
            block = plane * 16 + y * 4 + (x + along) % 4
        else:
            block = plane * 16 + ((y + along) % 4) * 4 + x
        named = jnp.where((lane == slot) & (group == KIND[dz]), block, named)
        near = jnp.where(lane == slot, jnp.where(plane // 4 == z // 4, 1.0, 0.0), near)
    named = named.astype(F32)
    hit = jnp.zeros((8, 128), F32)
    for side, length in ((0, 16), (1, 32)):
        entries = jnp.concatenate(
            [lists[k, at, side : side + 1, :] for k in range(2) for at in range(4)], axis=0
        ).astype(F32)
        for e in range(length):
            hit = jnp.where(named == jnp.broadcast_to(entries[:, e : e + 1], (8, 128)), 1.0, hit)
    near_hit, far_hit = (hit * near).T, (hit * (1.0 - near)).T
    for r in range(8):
        near_mask[r] = jnp.broadcast_to(near_hit[0:32, r : r + 1], (32, 128))
        far_mask[r] = jnp.broadcast_to(far_hit[0:32, r : r + 1], (32, 128))


def whole_kernel(
    points_in, omega_in, order_in, siblings_in, cousins_in, skeleton_in,
    basis, coupling,
    points, omega, tree_order, siblings, cousins, skeleton, load_sems,
    blocks, row_points, lists, own, own_rows, own_lists, near_mask, far_mask, rows, even_tile, odd_tile, parts,
    hop_send, hop_recv, out_send, out_recv, far_send, far_recv, rows_send, rows_recv, list_send, list_recv,
    other_core, shipped, received, table, sums, piece, pieces, landing, full_a, full_b,
    core_send, core_recv, ship_sems, table_sems, piece_send, piece_recv,
    z_send, z_recv, y_sems, x_sems,
    work, chosen, factor_out, factor_in, factor_sems, coupling_sems,
):
    loads = [
        pltpu.make_async_copy(source, target, load_sems.at[k])
        for k, (source, target) in enumerate(
            [
                (omega_in, omega),
                (points_in, points),
                (order_in, tree_order),
                (siblings_in, siblings),
                (cousins_in, cousins),
                (skeleton_in, skeleton),
            ]
        )
    ]
    for copy in loads:
        copy.start()
    x, y, z, core = place()
    leaf = z * 16 + y * 4 + x
    node, pair = z // 2, z // 4
    other = device(x, y, z, 1 - core)
    right, left_side = device((x + 1) % 4, y, z, core), device((x + 3) % 4, y, z, core)
    above, below = device(x, (y + 1) % 4, z, core), device(x, (y + 3) % 4, z, core)
    upward, downward = device(x, y, (z + 1) % 8, core), device(x, y, (z + 7) % 8, core)
    mates = []
    for dz in range(2):
        for dy in range(4):
            for dx in range(4):
                if dz or dy or dx:
                    where = ((x + dx) % 4, (y + dy) % 4, node * 2 + (z + dz) % 2)
                    mates.append((dz * 16 + dy * 4 + dx, where, device(*where, core)))
    column = [device(x, y, (z + dz) % 8, pair) for dz in range(8)]
    along_x = [device((x + d) % 4, y, z, core) for d in range(4)]
    along_y = [device(x, (y + d) % 4, z, core) for d in range(4)]
    partners = [who for _, _, who in mates] + [other]
    partners += [
        device(x, y, ((node + dn) % 4) * 2 + dz, c) for dn in range(1, 4) for dz in range(2) for c in range(2)
    ]
    partners.append(device(x, y, node * 2 + (z + 1) % 2, 1 - core))
    barrier = pltpu.get_barrier_semaphore()
    for partner in partners:
        pl.semaphore_signal(barrier, inc=1, device_id=partner, device_id_type=MESH)

    loads[0].wait()
    own[0:ROWS, :] = omega[...].astype(F32).T.astype(BF16)
    loads[1].wait()
    columns = features(points[...].astype(F32), 1.0, False).astype(BF16)
    own[256:272, :] = columns[:, :128]
    own[272:288, :] = columns[:, 128:]
    halves = (pl.ds(0, SPAN // 2), pl.ds(SPAN // 2, SPAN // 2))
    pl.semaphore_wait(barrier, len(partners))

    from_below, from_above = 24 * (z % 2), 24 * ((z + 1) % 2)
    hops = {}

    def hop(ref, slot, key, half, who):
        hops[key, half] = send(
            ref.at[halves[half]], blocks.at[slot, halves[half]],
            hop_send.at[key, half], hop_recv.at[key, half], who,
        )

    for step in range(2):
        hop(own, from_above, 7, step, upward)
        hop(own, from_below, 1, 1 - step, downward)

    for copy in loads[2:]:
        copy.wait()
    local = tree_order[...] % ROWS
    lane = lax.broadcasted_iota(jnp.int32, (ROWS, ROWS), 0)
    pick = jnp.where(lane == local, 1.0, 0.0).astype(BF16)
    mine = jnp.dot(points[...], pick, preferred_element_type=F32)
    own_rows[...] = features(mine, 4.0, True).astype(BF16)
    own_lists[...] = jnp.zeros_like(own_lists)
    own_lists[0:1, 0:16] = siblings[...]
    own_lists[1:2, 0:32] = cousins[...]
    small = []
    for kind, (at, line) in enumerate(((x, along_x), (y, along_y))):
        row_points[kind, at, core] = own_rows[...]
        lists[kind, at] = own_lists[...]
        for d in range(1, 4):
            target = row_points.at[kind, at, core]
            small.append(send(own_rows, target, rows_send.at[kind, d], rows_recv.at[kind, d], line[d]))
            target = lists.at[kind, at]
            small.append(send(own_lists, target, list_send.at[kind, d], list_recv.at[kind, d], line[d]))
    parts[...] = jnp.zeros_like(parts)

    plus, minus = (above, right), (below, left_side)
    outs, fars = {}, {}

    def fan_out(k, dz, half):
        kind = KIND[dz]
        block = blocks.at[SLOT[dz, 0], halves[half]]
        for side, (at, who) in enumerate(((SLOT[dz, 3], plus[kind]), (SLOT[dz, 1], minus[kind]))):
            outs[k, side, half] = send(
                block, blocks.at[at, halves[half]], out_send.at[k, side, half], out_recv.at[k, side, half], who
            )

    def relay(k, dz):
        kind = KIND[dz]
        for side, (at, who) in enumerate(((SLOT[dz, 3], plus[kind]), (SLOT[dz, 1], minus[kind]))):
            outs[k, side, side].wait_recv()
            fars[k, side] = send(
                blocks.at[at, halves[side]], blocks.at[SLOT[dz, 2], halves[side]],
                far_send.at[k, side], far_recv.at[k, side], who,
            )

    def landed(*ks):
        for k in ks:
            for side in range(2):
                outs[k, side, 1 - side].wait_recv()

    def passed(*ks):
        for k in ks:
            for side in range(2):
                fars[k, side].wait_recv()

    for step in range(2):
        hops[7, step].wait_recv()
        hop(blocks.at[from_below], SLOT[6, 0], 6, step, upward)
        hops[1, 1 - step].wait_recv()
        hop(blocks.at[from_above], SLOT[2, 0], 2, 1 - step, downward)
    for half in range(2):
        fan_out(0, MATE, half)
    for copy in small:
        copy.wait_recv()
    swap_rows = send(row_points.at[:, :, core], row_points.at[:, :, core], rows_send.at[0, 0], rows_recv.at[0, 0], other)
    make_masks(lists, near_mask, far_mask, x, y, z)
    for step in range(2):
        hops[6, step].wait_recv()
        hop(blocks.at[SLOT[6, 0]], SLOT[5, 0], 5, step, upward)
        fan_out(1, 6, step)
        hops[2, 1 - step].wait_recv()
        hop(blocks.at[SLOT[2, 0]], SLOT[3, 0], 3, 1 - step, downward)
        fan_out(2, 2, 1 - step)
    swap_rows.wait()
    for r in range(8):
        for half in range(2):
            rows[r, half * ROWS : (half + 1) * ROWS, :] = row_points[r // 4, r % 4, half].astype(F32).T.astype(BF16)

    def kernel_tile(r, use, tile):
        columns = jnp.concatenate(
            [blocks[2 * use + k, at : at + 16, :] for k in range(2) for at in (256, 272)], axis=1
        )
        exponent = jnp.dot(rows[r], columns, preferred_element_type=F32)
        tile[...] = jnp.exp(exponent).astype(BF16)

    def add(kind, at, use, tile):
        r = kind * 4 + at
        weights = []
        for k in range(2):
            slot = 2 * use + k
            values = blocks[slot, 0:ROWS, :]
            near = near_mask[r, pl.ds(slot, 1), :].astype(BF16)
            far = far_mask[r, pl.ds(slot, 1), :].astype(BF16)
            weights.append(jnp.concatenate([values * near, values * far], axis=1))
        terms = jnp.dot(tile[...], jnp.concatenate(weights, axis=0), preferred_element_type=F32)
        parts[0, kind, at] += terms[0:ROWS]
        parts[1, kind, at] += terms[ROWS:]

    def batch(kind, count, item, tiles=(even_tile, odd_tile), primed=False, following=None):
        now, later = tiles
        if not primed:
            at, use = item(0)
            kernel_tile(kind * 4 + at, use, now)

        def two_steps(step, carry):
            at0, use0 = item(2 * step)
            at1, use1 = item(2 * step + 1)
            at2, use2 = item(2 * step + 2)
            kernel_tile(kind * 4 + at1, use1, later)
            add(kind, at0, use0, now)
            kernel_tile(kind * 4 + at2, use2, now)
            add(kind, at1, use1, later)
            return carry

        if count > 2:
            lax.fori_loop(0, (count - 1) // 2, two_steps, 0)
        if count % 2 == 0:
            at, use = item(count - 1)
            kernel_tile(kind * 4 + at, use, later)
            add(kind, *item(count - 2), now)
            now, later = later, now
        if following is not None:
            at, use = following
            kernel_tile(kind * 4 + at, use, later)
        add(kind, *item(count - 1), now)
        return later, now

    batch(1, 4, lambda i: (i, 0))
    relay(0, MATE)
    hops[5, 0].wait_recv()
    hop(blocks.at[SLOT[5, 0]], SLOT[4, 0], 4, 0, upward)
    fan_out(3, 5, 0)
    hops[3, 1].wait_recv()
    hop(blocks.at[SLOT[3, 0]], SLOT[4, 0], 4, 1, downward)
    fan_out(4, 3, 1)
    hops[5, 1].wait_recv()
    fan_out(3, 5, 1)
    hops[3, 0].wait_recv()
    fan_out(4, 3, 0)
    batch(0, 4, lambda i: (i, 1))
    relay(1, 6)
    relay(2, 2)
    for half in range(2):
        hops[4, half].wait_recv()
        fan_out(5, 4, half)
    landed(0, 1)
    batch(1, 8, lambda i: (i % 4, 2 + i // 4))
    relay(3, 5)
    relay(4, 3)
    relay(5, 4)
    landed(4)
    passed(0, 1)
    batch(1, 8, lambda i: (i % 4, 4 + i // 4))
    passed(4)
    batch(1, 4, lambda i: (i, 6))

    ahead, behind, across = (x + 1) % 4, (x + 3) % 4, (x + 2) % 4
    next_y, last_y = (y + 1) % 4, (y + 3) % 4
    order = [(across, (y + 2) % 4), (ahead, next_y), (behind, last_y), (x, y)]
    swap = {}

    def give(step, kind):
        at = order[step][kind]
        swap[step, kind] = send(
            parts.at[1 - core, kind, at], other_core.at[kind, at],
            core_send.at[kind, step], core_recv.at[kind, step], other,
        )


    def partial(step, kind):
        swap[step, kind].wait_recv()
        at = order[step][kind]
        return parts[core, kind, at] + other_core[kind, at]

    ships = []

    def ship(step, kind):
        shipped[kind, step] = partial(step, kind).astype(LINK)
        who = (along_x, along_y)[kind][(2, 1, 3)[step]]
        ships.append(
            send(
                shipped.at[kind, step], received.at[kind, step],
                ship_sems.at[0, kind, step], ship_sems.at[1, kind, step], who,
            )
        )

    for step in range(4):
        give(step, 1)
    landed(2, 3, 5)
    passed(2, 3, 5)

    def last_batch(step, first, count, tiles, primed, following):
        at = order[step][0]
        tiles = batch(0, count, lambda i: (at, 7 + first + i), tiles, primed, following)
        if first + count == 5:
            give(step, 0)
        return tiles

    tiles = last_batch(0, 0, 5, (even_tile, odd_tile), False, (order[1][0], 7))
    for step in range(3):
        ship(step, 1)
    tiles = last_batch(1, 0, 5, tiles, True, (order[2][0], 7))
    ship(0, 0)
    tiles = last_batch(2, 0, 5, tiles, True, (order[3][0], 7))
    ship(1, 0)
    tiles = last_batch(3, 0, 2, tiles, True, (order[3][0], 9))
    ship(2, 0)
    last_batch(3, 2, 3, tiles, True, None)
    total = partial(3, 1) + partial(3, 0)
    first_row = (leaf * 2 + core) * ROWS
    row = lax.broadcasted_iota(jnp.int32, (ROWS, RANK), 0) + first_row
    picked = jnp.where(row == skeleton[pl.ds(node, 1), :], 1.0, 0.0)
    own_skeleton = jnp.dot(
        mine.astype(BF16), picked.astype(BF16), preferred_element_type=F32
    )
    for copy in ships:
        copy.wait_recv()
    for kind in range(2):
        for step in range(3):
            total = total + received[kind, step].astype(F32)
    rows_here = total

    def product(c, first):
        values = lax.dot_general(
            first, rows_here, (((0,), (0,)), ((), ())), precision=HIGH, preferred_element_type=F32
        )
        table[c, 0] = values[:, 0:128]
        table[c, 1] = values[:, 128:256]

    def swap_table(c):
        return send(table.at[c, 1 - core], sums.at[c], table_sems.at[0, c], table_sems.at[1, c], other)

    def spread_table(c):
        swaps[c].wait_recv()
        sums[c] += table[c, core]
        copies = []
        for slot, where, who in far_first:
            copies.append(
                send(chunk(c, where), pieces.at[c, slot], piece_send.at[c, slot], piece_recv.at[c, slot], who)
            )
        return copies

    def chunk(c, where):
        first = (where[0] * 8 + where[1] * 2 + where[2] % 2) * 8
        return sums.at[c, pl.ds(pl.multiple_of(first, 8), 8)]

    def reach(mate):
        return sum(min(d, 4 - d) for d in (mate[0] // 16, mate[0] // 4 % 4, mate[0] % 4))

    def drop(c, dz):
        return pltpu.make_async_remote_copy(
            src_ref=piece.at[c],
            dst_ref=landing.at[c, z % 4, core],
            send_sem=z_send.at[c, dz],
            recv_sem=z_recv.at[c, z % 4, core],
            device_id=column[dz],
            device_id_type=MESH,
        )

    def collect_chunk(c):
        result = chunk(c, (x, y, z))[...]
        for copy in spreads[c]:
            copy.wait_recv()
        for slot, _, _ in mates:
            result = result + pieces[c, slot]
        piece[c] = result
        for dz in (4, 3, 5, 2, 6, 1, 7):
            drop(c, dz).start()

        @pl.when(pair == core)
        def _():
            landing[c, z % 4, core] = piece[c]

        @pl.when(pair != core)
        def _():
            drop(c, 0).start()

    far_first = sorted(mates, key=reach, reverse=True)
    product(0, rows_here)
    table[0, 0, 128:256, :] = jnp.zeros((128, 128), F32)
    table[0, 0, 128:136, :] = own_skeleton[:, 0:128]
    table[0, 0, 136:144, :] = own_skeleton[:, 128:256]
    swaps = [swap_table(0)]
    product(1, picked)
    swaps.append(swap_table(1))
    spreads = [spread_table(0)]
    spreads.append(spread_table(1))
    collect_chunk(0)
    collect_chunk(1)

    def fan(ref, sems, first, line):
        return [
            send(ref, ref, sems.at[0, first + d - 1], sems.at[1, first + d - 1], line[d]) for d in (2, 1, 3)
        ]

    def first_leg(c):
        for plane in range(4):
            for half in range(2):

                @pl.when((core * 4 + plane != z) | (core != half))
                def _(plane=plane, half=half):
                    pltpu.make_async_remote_copy(
                        src_ref=piece.at[c],
                        dst_ref=landing.at[c, plane, half],
                        send_sem=z_send.at[c, 0],
                        recv_sem=z_recv.at[c, plane, half],
                        device_id=other,
                        device_id_type=MESH,
                    ).wait_recv()

        full_a[c, x, y] = landing[c, :, 0]
        full_b[c, y, x] = landing[c, :, 1]
        return fan(full_a.at[c, x, y], y_sems, 6 * c, along_y) + fan(full_b.at[c, y, x], x_sems, 6 * c, along_x)

    def second_leg(c, copies):
        for copy in copies:
            copy.wait_recv()
        return fan(full_a.at[c, x], x_sems, 6 * c + 3, along_x) + fan(full_b.at[c, y], y_sems, 6 * c + 3, along_y)

    legs = [first_leg(0)]
    legs.append(second_leg(0, legs[0]))
    legs.append(first_leg(1))
    legs.append(second_leg(1, legs[2]))
    for copy in legs[1]:
        copy.wait_recv()

    row = lax.broadcasted_iota(jnp.int32, (RANK, RANK), 0)
    col = lax.broadcasted_iota(jnp.int32, (RANK, RANK), 1)
    skeleton_points, sizes = [], []
    for n in range(2):
        for at_x in range(4):
            for at_y in range(4):
                span = pl.ds(at_x * 64 + at_y * 16, 16)
                planes = pl.ds(2 * n, 2)
                work[n, span, 0:128] = full_a[0, at_x, at_y, planes].reshape(16, 128)
                work[n, span, 128:256] = full_b[0, at_y, at_x, planes].reshape(16, 128)
        skeleton_points.append(
            jnp.concatenate([work[n, 128:136, 0:128], work[n, 136:144, 0:128]], axis=1)
        )
        gram = work[n]
        on_diagonal = jnp.where(row == col, gram, 0.0)
        trace = jnp.sum(jnp.sum(on_diagonal, axis=0, keepdims=True), axis=1, keepdims=True)
        work[n] = gram * (1.0 / trace) + jnp.where(row == col, 0.01, 0.0)
        sizes.append(lax.rsqrt(trace))

    row_side = features(skeleton_points[0], 4.0, True).T.astype(BF16)
    col_side = features(skeleton_points[1], 1.0, False).astype(BF16)
    kernel_skel = jnp.exp(jnp.dot(row_side, col_side, preferred_element_type=F32))

    lane8 = lax.broadcasted_iota(jnp.int32, (8, 128), 1)
    row8 = lax.broadcasted_iota(jnp.int32, (8, 128), 0)
    group8 = (lane8 // 64) * 64
    lane = lax.broadcasted_iota(jnp.int32, (64, 128), 1)
    for p in range(4):
        top = 64 * p
        aligned = (top // 128) * 128
        packed = []
        for n in range(2):
            block = work[n, top : top + 64, aligned : aligned + 128]
            packed.append(pltpu.roll(block, 64, 1) if (64 * n - top) % 128 else block)
        packed = jnp.where(lane < 64, packed[0], packed[1])
        left = [packed[8 * g : 8 * g + 8] for g in range(8)]
        inverse = [jnp.where(lane8 - group8 == row8 + 8 * g, 1.0, 0.0) for g in range(8)]
        for own in range(8):
            spread = {
                g: [
                    jnp.take_along_axis(left[g], group8 + (8 * own + t), axis=1, mode="promise_in_bounds")
                    for t in range(8)
                ]
                for g in range(own, 8)
            }

            def line(tile, t):
                return jnp.broadcast_to(tile[t : t + 1, :], (8, 128))

            solve = pivots(lambda t, u: line(spread[own][u], t))
            left_rows = solve([line(left[own], t) for t in range(8)])
            inverse_rows = solve([line(inverse[own], t) for t in range(8)])
            for g in range(own + 1, 8):
                factors = solve(spread[g])
                left[g] = left[g] - fold(factors, left_rows)
                inverse[g] = inverse[g] - fold(factors, inverse_rows)
            for t in range(8):
                inverse[own] = jnp.where(row8 == t, inverse_rows[t], inverse[own])
        packed = jnp.concatenate(inverse, axis=0)
        diagonal = jnp.concatenate([jnp.where(lane < 64, packed, 0.0), jnp.where(lane < 64, 0.0, packed)], axis=0)
        stacked = jnp.concatenate([work[n, top : top + 64, :] for n in range(2)], axis=0)
        srow = lax.broadcasted_iota(jnp.int32, (128, RANK), 0)
        scol = lax.broadcasted_iota(jnp.int32, (128, RANK), 1)
        identity = jnp.where(srow % 64 == scol % 64, 1.0, 0.0)
        stacked = jnp.where(scol // 64 == p, identity, stacked)
        solved = jnp.dot(diagonal, stacked, precision=HIGH, preferred_element_type=F32)
        done = jnp.where(scol < top + 64, solved, 0.0)
        for n in range(2):
            work[n, top : top + 64, :] = done[64 * n : 64 * n + 64]
        rest = RANK - top - 64
        if rest:
            turned = solved.T[top + 64 :, :]
            tlane = lax.broadcasted_iota(jnp.int32, (rest, 128), 1)
            tcol = lax.broadcasted_iota(jnp.int32, (rest, RANK), 1)
            for n in range(2):
                update = jnp.dot(
                    jnp.where(tlane // 64 == n, turned, 0.0), solved,
                    precision=HIGH, preferred_element_type=F32,
                )
                work[n, top + 64 :, :] = jnp.where(tcol // 64 == p, 0.0, work[n, top + 64 :, :]) - update
        if p == 1:
            for copy in legs[3]:
                copy.wait_recv()
            for n in range(2):
                for at_x in range(4):
                    for at_y in range(4):
                        span = pl.ds(at_x * 64 + at_y * 16, 16)
                        planes = pl.ds(2 * n, 2)
                        chosen[n, span, 0:128] = full_a[1, at_x, at_y, planes].reshape(16, 128)
                        chosen[n, span, 128:256] = full_b[1, at_y, at_x, planes].reshape(16, 128)
            right_part = jnp.dot(kernel_skel, chosen[1], precision=HIGH, preferred_element_type=F32)
            middle = lax.dot_general(
                chosen[0], right_part, (((0,), (0,)), ((), ())), precision=HIGH, preferred_element_type=F32
            )

    size = jnp.where(node % 2 == 0, sizes[0], sizes[1])
    factor_out[...] = work[node % 2] * size
    factor_copy = send(factor_out, factor_in, factor_sems.at[0], factor_sems.at[1], other)
    last = (((1,), (1,)), ((), ()))
    half = jnp.dot(work[0], middle, precision=HIGH, preferred_element_type=F32)
    coupling[core] = ((16384.0 / math.sqrt(RANK)) * sizes[0] * sizes[1]) * lax.dot_general(
        half, work[1], last, precision=HIGH, preferred_element_type=F32
    )
    coupling_copy = send(
        coupling.at[core], coupling.at[core], coupling_sems.at[0], coupling_sems.at[1], other
    )
    factor_copy.wait_recv()
    factor = jnp.where(node // 2 == core, factor_out[...], factor_in[...])
    basis[...] = 128.0 * lax.dot_general(
        rows_here, factor, last, precision=HIGH, preferred_element_type=F32
    )
    factor_copy.wait_send()
    coupling_copy.wait()

    for copy in ships + list(swap.values()) + small + sum(legs, []):
        copy.wait_send()
    for c in range(2):
        swaps[c].wait_send()
        for copy in spreads[c]:
            copy.wait_send()
        for dz in range(1, 8):
            drop(c, dz).wait_send()

        @pl.when(pair != core)
        def _(c=c):
            drop(c, 0).wait_send()

    for copy in list(hops.values()) + list(outs.values()) + list(fars.values()):
        copy.wait_send()


def whole(*arguments):
    dma = pltpu.SemaphoreType.DMA

    def block(*shape, kind=F32):
        return pltpu.VMEM(shape, kind)

    i32 = jnp.int32
    return pl.pallas_call(
        whole_kernel,
        out_shape=(
            jax.ShapeDtypeStruct((ROWS, RANK), F32),
            jax.ShapeDtypeStruct((2, RANK, RANK), F32),
        ),
        in_specs=[HBM] * 6,
        out_specs=(VMEM,) * 2,
        scratch_shapes=[
            block(FEATS, ROWS, kind=BF16), block(SAMPLES, ROWS, kind=BF16), block(1, ROWS, kind=i32),
            block(1, 16, kind=i32), block(1, 32, kind=i32), block(4, RANK, kind=i32), dma((6,)),
            block(25, SPAN, 128, kind=BF16), block(2, 4, 2, 16, ROWS, kind=BF16), block(2, 4, 8, 128, kind=i32),
            block(SPAN, 128, kind=BF16), block(16, ROWS, kind=BF16), block(8, 128, kind=i32),
            block(8, 32, 128), block(8, 32, 128), block(8, 2 * ROWS, 16, kind=BF16),
            block(2 * ROWS, 2 * ROWS, kind=BF16), block(2 * ROWS, 2 * ROWS, kind=BF16), block(2, 2, 4, ROWS, RANK),
            dma((8, 2)), dma((8, 2)), dma((6, 2, 2)), dma((6, 2, 2)), dma((6, 2)), dma((6, 2)),
            dma((2, 4)), dma((2, 4)), dma((2, 4)), dma((2, 4)),
            block(2, 4, ROWS, RANK), block(2, 3, ROWS, RANK, kind=LINK), block(2, 3, ROWS, RANK, kind=LINK),
            block(2, 2, RANK, 128), block(2, RANK, 128), block(2, 8, 128), block(2, 32, 8, 128),
            block(2, 4, 2, 8, 128), block(2, 4, 4, 4, 8, 128), block(2, 4, 4, 4, 8, 128),
            dma((2, 4)), dma((2, 4)), dma((2, 2, 3)), dma((2, 2)), dma((2, 32)), dma((2, 32)),
            dma((2, 8)), dma((2, 4, 2)), dma((2, 12)), dma((2, 12)),
            block(2, RANK, RANK), block(2, RANK, RANK), block(RANK, RANK), block(RANK, RANK),
            dma((2,)), dma((2,)),
        ],
        compiler_params=pltpu.CompilerParams(
            collective_id=0, has_side_effects=True, vmem_limit_bytes=VMEM_LIMIT
        ),
        name="whole",
    )(*arguments)


def body(points, omega, tree_order, sibling_blocks, cousin_blocks, skeleton):
    arguments = (points, omega, tree_order.reshape(1, ROWS), sibling_blocks, cousin_blocks, skeleton)
    return whole(*(pltpu.with_memory_space_constraint(argument, pltpu.HBM) for argument in arguments))


def solution(mesh):
    return jax.shard_map(
        body,
        mesh=mesh,
        in_specs=(
            P(None, ("leaf", "sub")),
            P(None, ("leaf", "sub")),
            P(("leaf", "sub")),
            P("leaf", None),
            P("leaf", None),
            P(),
        ),
        out_specs=(P(("leaf", "sub"), None), P()),
        check_vma=False,
    )
```
